128 devices in a mesh: phase: 2 (over core), ctx: 32 (over y, x, z_hi), fsdp: 2 (over z_lo).
Axes of the slice: x: 4, y: 4, z: 4 (z_hi: 2, z_lo: 2; z = z_hi * 2 + z_lo), core: 2. Of those that a mesh axis runs over, the one named last changes fastest.
Arguments:
- layer_in: bfloat16 [2, 4096, 960], P('fsdp', 'ctx'), may hold values from -6 to 6
- out_grad: float32 [2, 4096, 960], P('fsdp', 'ctx'), may hold values from -6 to 6
- segment_ids: int32 [2, 4096], P('fsdp'), may hold values from 0 to 3, never falling along the last dimension, each value on 1 to 2048 neighbouring positions
- block_pair: int32 [32], replicated, may hold values from 0 to 31, each once
- params: bfloat16 [2, 9830400], P('phase', ('ctx', 'fsdp')), may hold values from -2 to 2
- norm_gains: bfloat16 [2, 1920], P('phase', ('ctx', 'fsdp')), may hold values from 0.099609375 to 1.8984375
Outputs:
- phase_out: bfloat16 [2, 2, 4096, 960], P('phase', 'fsdp', 'ctx')
- phase_grad: float32 [2, 2, 4096, 960], P('phase', 'fsdp', 'ctx')
- param_grad: float32 [2, 9830400], P('phase', ('ctx', 'fsdp'))
- gain_grad: float32 [2, 1920], P('phase', ('ctx', 'fsdp'))
The draws below stay inside these ranges and needn't reach their ends.
Inputs may be any that keep to these rules, and one draw needn't show every extreme that they name: segment_ids[s] never falls along a sequence; each id covers 1 to half of 4096 positions, and one covers exactly half of 4096. `block_pair`: each value once.
All inputs are finite; a program needn't handle non-finite values.
Results may differ from the reference program's by a relative error of at most 0.03.
Values may be sent and summed in bfloat16 or wider, within the bound.
No kernel may reach another device: no remote copies, remote signals or barrier semaphores. Data moves between devices by JAX's collectives and lax.ppermute only.
A program may use at most 256 MiB of HBM per device.

```python
import math
import jax
import jax.numpy as jnp
import numpy as np
from jax import lax

H = 15
KVH = 5
HD = 64
D = 960
FF = 2560
DOCS = 4
PAIRS = 32
SEQ = 4096
MBT = 2


def draw_params(key, part):
    qkv_width = (H + 2 * KVH) * HD
    sections = [(D * qkv_width, D), (H * HD * D, D / 16.0), (D * 2 * FF, D), (FF * D, FF)]
    pieces = []
    for number, section in enumerate(sections):
        sub_key = jax.random.fold_in(key, 11 + number)
        values = jax.random.truncated_normal(sub_key, -4.0, 4.0, (2, section[0]), jnp.float32)
        pieces.append(values * (1.0 / math.sqrt(section[1])))
    return jnp.clip(jnp.concatenate(pieces, axis=1), -2.0, 2.0).astype(jnp.bfloat16)


def draw_layer_in(key, part):
    noise_key = jax.random.fold_in(key, 601)
    values = jax.random.truncated_normal(noise_key, -6.0, 6.0, (MBT, SEQ, D), jnp.float32)
    return jnp.clip(values, -6.0, 6.0).astype(jnp.bfloat16)


def shard_levels(key, dims, cuts, smallest, high):
    factor_of = 1.0
    for position, blocks in cuts:
        draws = jax.random.uniform(jax.random.fold_in(jax.random.fold_in(key, 6), position), (blocks,), jnp.float32, smallest / len(cuts), high / len(cuts))
        factor_of = factor_of * jnp.repeat(jnp.exp(draws), dims[position] // blocks).reshape((-1,) + (1,) * (len(dims) - 1 - position))
    return factor_of


def split_up(amount, total, reach, skew):
    weights = [(1 << 20) // math.isqrt(grade ** skew) + 1 for grade in range(2, amount + 1)]
    surplus, counts = total - reach - (amount - 1), [1] * (amount - 1)
    while surplus > 0:
        movable = [i for i in range(amount - 1) if counts[i] < reach]
        whole, budget = sum([weights[i] for i in movable]), surplus
        for i in movable:
            addition = min(reach - counts[i], max(1, budget * weights[i] // whole), surplus)
            counts[i] = counts[i] + addition
            surplus = surplus - addition
    return np.array([reach] + counts)


def ragged(key, amount, total, bound, slope):
    if amount == 2:
        one = jax.random.randint(key, (), max(1, total - bound), min(bound, total - 1) + 1)
        return jnp.stack([one, total - one])
    lengths = jnp.asarray(split_up(amount, total, bound, slope), jnp.int32)
    couples = (amount - 1) // 2
    source_of, taker = lengths[1:1 + 2 * couples:2], lengths[2:2 + 2 * couples:2]
    margin = jnp.minimum(source_of - 1, bound - taker)
    moved = jax.random.randint(jax.random.fold_in(key, 1), (couples,), 0, 1 << 20) % (margin + 1)
    lengths = lengths.at[1:1 + 2 * couples:2].set(source_of - moved).at[2:2 + 2 * couples:2].set(taker + moved)
    return lengths[jax.random.permutation(jax.random.fold_in(key, 2), amount)]


def noise(own_key, shape, width, limit, cuts=(), kind=jnp.bfloat16):
    factor_of = shard_levels(own_key, shape, cuts, -0.22, 0.18) if cuts else 1.0
    values = jax.random.normal(own_key, shape, jnp.float32) * width * factor_of
    return jnp.minimum(jnp.maximum(values, -limit), limit).astype(kind)


def setup_inputs(seed: int = 0) -> dict:
    arg_keys = jax.random.split(jax.random.key(seed), 7)
    layer_in = draw_layer_in(jax.random.fold_in(arg_keys[6], 71), 0)
    out_grad = noise(arg_keys[1], (MBT, SEQ, D), 1.0, 6.0, ((0, 2), (1, 32)), jnp.float32)
    segment_ids = jax.vmap(lambda own: jnp.searchsorted(jnp.cumsum(ragged(own, DOCS, SEQ, SEQ // 2, 0)), jnp.arange(SEQ), side="right"))(jax.random.split(arg_keys[2], MBT)).reshape((MBT, SEQ)).astype(jnp.int32)
    block_pair = jax.random.permutation(arg_keys[3], PAIRS).astype(jnp.int32)
    params = draw_params(jax.random.fold_in(arg_keys[6], 71), 0)
    norm_gains = jnp.clip(1.0 + 0.18 * jax.random.normal(arg_keys[5], (2, 2 * D), jnp.float32), 0.099609375, 1.8984375).astype(jnp.bfloat16)
    return dict(layer_in=layer_in, out_grad=out_grad, segment_ids=segment_ids, block_pair=block_pair, params=params, norm_gains=norm_gains)


eps = 1e-05
rope_theta = 100000.0
masked_fill = -1e+30

def rounded(values):
    return lax.optimization_barrier(values.astype(jnp.bfloat16)).astype(jnp.float32)

def norm_scale(values):
    return lax.rsqrt(lax.optimization_barrier(jnp.mean(values * values, axis=-1, keepdims=True)) + eps)

def norm_back(d_out, values, scales, gain_vec):
    scaled = d_out * gain_vec
    d_gain = lax.optimization_barrier(jnp.sum(d_out * values * scales, axis=0))
    d_values = scales * scaled - values * (scales * scales * scales) * lax.optimization_barrier(jnp.mean(scaled * values, axis=-1, keepdims=True))
    return (d_values, d_gain)

def rotate(values, offsets, head_count, inverse):
    row_count = values.shape[0]
    shaped = values.reshape(row_count, head_count, HD)
    half_dim = HD // 2
    frequency = rope_theta ** (-2.0 * jnp.arange(half_dim, dtype=jnp.float32) / HD)
    angles = offsets.astype(jnp.float32)[:, None] * frequency[None, :]
    cosine = jnp.cos(angles)[:, None, :]
    sine = jnp.sin(angles)[:, None, :]
    left = shaped[..., :half_dim]
    right = shaped[..., half_dim:]
    if inverse:
        merged = jnp.concatenate([left * cosine + right * sine, right * cosine - left * sine], axis=-1)
    else:
        merged = jnp.concatenate([left * cosine - right * sine, right * cosine + left * sine], axis=-1)
    return merged.reshape(row_count, head_count * HD)

def unpack(flat_row, gain_row):
    query_width = H * HD
    qkv_width = (H + 2 * KVH) * HD
    cut_one = D * qkv_width
    cut_two = cut_one + query_width * D
    cut_three = cut_two + D * 2 * FF
    cut_four = cut_three + FF * D
    return (flat_row[:cut_one].reshape(D, qkv_width), flat_row[cut_one:cut_two].reshape(query_width, D), flat_row[cut_two:cut_three].reshape(D, 2 * FF), flat_row[cut_three:cut_four].reshape(FF, D), gain_row[:D].astype(jnp.float32), gain_row[D:].astype(jnp.float32))

def layout(seg_row, block_pair):
    pair_count = block_pair.shape[0]
    seq_len = seg_row.shape[0]
    block_len = seq_len // (2 * pair_count)
    blocks_dealt = jnp.stack([block_pair, 2 * pair_count - 1 - block_pair], axis=1).reshape(-1).astype(jnp.int32)
    within = jnp.arange(block_len, dtype=jnp.int32)
    places = (blocks_dealt[:, None] * block_len + within[None, :]).reshape(-1)
    cell_ids = jnp.arange(seq_len, dtype=jnp.int32)
    begins = jnp.concatenate([jnp.ones((1,), dtype=jnp.bool_), seg_row[1:] != seg_row[:-1]])
    starts = lax.cummax(jnp.where(begins, cell_ids, jnp.zeros_like(cell_ids)), axis=0)
    offsets = cell_ids - starts
    dealt_seg = seg_row.reshape(2 * pair_count, block_len)[blocks_dealt].reshape(-1)
    dealt_off = offsets.reshape(2 * pair_count, block_len)[blocks_dealt].reshape(-1)
    return (places, dealt_seg, dealt_off)

def attention_forward(query, keys, vals, meta):
    places, segs, offsets = meta
    seq_len = query.shape[0]
    block_rows = min(512, seq_len)
    group_size = H // KVH
    score_scale = 1.0 / math.sqrt(HD)
    keys_all = keys.astype(jnp.float32).reshape(seq_len, KVH, HD)
    vals_all = vals.astype(jnp.float32).reshape(seq_len, KVH, HD)

    def per_block(block_index):
        first_row = block_index * block_rows
        rows_q = lax.dynamic_slice_in_dim(query, first_row, block_rows).astype(jnp.float32).reshape(block_rows, KVH, group_size, HD)
        place_q = lax.dynamic_slice_in_dim(places, first_row, block_rows)
        seg_q = lax.dynamic_slice_in_dim(segs, first_row, block_rows)
        allowed = (places[None, :] <= place_q[:, None]) & (segs[None, :] == seg_q[:, None])
        scores = jnp.einsum('rkgd,tkd->kgrt', rows_q, keys_all, precision=lax.Precision.HIGHEST) * score_scale
        masked = jnp.where(allowed, scores, masked_fill)
        peak = lax.optimization_barrier(jnp.max(masked, axis=-1))
        totals = lax.optimization_barrier(jnp.sum(jnp.exp(masked - peak[..., None]), axis=-1))
        lse = peak + jnp.log(totals)
        probs = jnp.exp(masked - lse[..., None])
        mixed = jnp.einsum('kgrt,tkd->rkgd', probs, vals_all, precision=lax.Precision.HIGHEST).reshape(block_rows, H * HD)
        return (mixed.astype(jnp.bfloat16), lse)
    mixed, lses = lax.map(per_block, jnp.arange(seq_len // block_rows, dtype=jnp.int32))
    return (mixed.reshape(seq_len, H * HD), lses)

def attention_backward(query, keys, vals, mixed, lses, d_mixed, meta):
    places, segs, offsets = meta
    seq_len = query.shape[0]
    block_rows = min(512, seq_len)
    group_size = H // KVH
    score_scale = 1.0 / math.sqrt(HD)
    keys_all = keys.astype(jnp.float32).reshape(seq_len, KVH, HD)
    vals_all = vals.astype(jnp.float32).reshape(seq_len, KVH, HD)
    delta_all = lax.optimization_barrier(jnp.sum((d_mixed * mixed.astype(jnp.float32)).reshape(seq_len, KVH, group_size, HD), axis=-1))
    d_mix_r = rounded(d_mixed)

    def per_block(state_in, block_index):
        d_keys_acc, d_vals_acc = state_in
        first_row = block_index * block_rows
        rows_q = lax.dynamic_slice_in_dim(query, first_row, block_rows).astype(jnp.float32).reshape(block_rows, KVH, group_size, HD)
        place_q = lax.dynamic_slice_in_dim(places, first_row, block_rows)
        seg_q = lax.dynamic_slice_in_dim(segs, first_row, block_rows)
        d_out = lax.dynamic_slice_in_dim(d_mix_r, first_row, block_rows).reshape(block_rows, KVH, group_size, HD)
        delta_q = jnp.transpose(lax.dynamic_slice_in_dim(delta_all, first_row, block_rows), (1, 2, 0))
        lse = lses[block_index]
        allowed = (places[None, :] <= place_q[:, None]) & (segs[None, :] == seg_q[:, None])
        scores = jnp.einsum('rkgd,tkd->kgrt', rows_q, keys_all, precision=lax.Precision.HIGHEST) * score_scale
        probs = jnp.exp(jnp.where(allowed, scores, masked_fill) - lse[..., None])
        d_vals_acc = d_vals_acc + jnp.einsum('kgrt,rkgd->tkd', rounded(probs), d_out, precision=lax.Precision.HIGHEST)
        d_probs = jnp.einsum('rkgd,tkd->kgrt', d_out, vals_all, precision=lax.Precision.HIGHEST)
        d_scores = rounded(probs * (d_probs - delta_q[..., None]) * score_scale)
        d_query = jnp.einsum('kgrt,tkd->rkgd', d_scores, keys_all, precision=lax.Precision.HIGHEST).reshape(block_rows, H * HD)
        d_keys_acc = d_keys_acc + jnp.einsum('kgrt,rkgd->tkd', d_scores, rows_q, precision=lax.Precision.HIGHEST)
        return ((d_keys_acc, d_vals_acc), d_query)
    zeros = jnp.zeros((seq_len, KVH, HD), jnp.float32)
    (d_keys, d_vals), d_query = lax.scan(per_block, (zeros, zeros), jnp.arange(seq_len // block_rows, dtype=jnp.int32))
    return (d_query.reshape(seq_len, H * HD), d_keys.reshape(seq_len, KVH * HD), d_vals.reshape(seq_len, KVH * HD))

def layer_forward(seq_in, weights, meta):
    w_qkv, w_out, w_gu, w_down, gain_one, gain_two = weights
    offsets = meta[2]
    query_width = H * HD
    key_width = KVH * HD
    resid = seq_in.astype(jnp.float32)
    scale_one = norm_scale(resid)
    normed = (resid * scale_one * gain_one).astype(jnp.bfloat16)
    proj = jnp.dot(normed, w_qkv, preferred_element_type=jnp.float32)
    query = rotate(proj[:, :query_width], offsets, H, False).astype(jnp.bfloat16)
    keys = rotate(proj[:, query_width:query_width + key_width], offsets, KVH, False).astype(jnp.bfloat16)
    vals = proj[:, query_width + key_width:].astype(jnp.bfloat16)
    mixed, lses = attention_forward(query, keys, vals, meta)
    hidden = resid + jnp.dot(mixed, w_out, preferred_element_type=jnp.float32)
    scale_two = norm_scale(hidden)
    normed_two = (hidden * scale_two * gain_two).astype(jnp.bfloat16)
    gate_up = jnp.dot(normed_two, w_gu, preferred_element_type=jnp.float32)
    gate = gate_up[:, :FF]
    up_proj = gate_up[:, FF:]
    inner = (gate * jax.nn.sigmoid(gate) * up_proj).astype(jnp.bfloat16)
    result = hidden + jnp.dot(inner, w_down, preferred_element_type=jnp.float32)
    saved = (resid, scale_one, normed, query, keys, vals, mixed, lses, hidden, scale_two, normed_two, gate, up_proj, inner)
    return (result.astype(jnp.bfloat16), saved)

def layer_backward(cotangent, saved, weights, meta):
    w_qkv, w_out, w_gu, w_down, gain_one, gain_two = weights
    resid, scale_one, normed, query, keys, vals, mixed, lses, hidden, scale_two, normed_two, gate, up_proj, inner = saved
    offsets = meta[2]
    cot_b = cotangent.astype(jnp.bfloat16)
    d_down = jnp.dot(inner.T, cot_b, preferred_element_type=jnp.float32)
    d_inner = jnp.dot(cot_b, w_down.T, preferred_element_type=jnp.float32)
    sigma = jax.nn.sigmoid(gate)
    d_gate = d_inner * up_proj * sigma * (1.0 + gate * (1.0 - sigma))
    d_up = d_inner * gate * sigma
    d_gu = jnp.concatenate([d_gate, d_up], axis=1).astype(jnp.bfloat16)
    d_wgu = jnp.dot(normed_two.T, d_gu, preferred_element_type=jnp.float32)
    d_norm_two = jnp.dot(d_gu, w_gu.T, preferred_element_type=jnp.float32)
    d_hidden, d_gain_two = norm_back(d_norm_two, hidden, scale_two, gain_two)
    d_hidden = cotangent + d_hidden
    d_hidden_b = d_hidden.astype(jnp.bfloat16)
    d_wout = jnp.dot(mixed.T, d_hidden_b, preferred_element_type=jnp.float32)
    d_mixed = jnp.dot(d_hidden_b, w_out.T, preferred_element_type=jnp.float32)
    d_query, d_keys, d_vals = attention_backward(query, keys, vals, mixed, lses, d_mixed, meta)
    d_query = rotate(d_query, offsets, H, True)
    d_keys = rotate(d_keys, offsets, KVH, True)
    d_proj = jnp.concatenate([d_query, d_keys, d_vals], axis=1).astype(jnp.bfloat16)
    d_wqkv = jnp.dot(normed.T, d_proj, preferred_element_type=jnp.float32)
    d_normed = jnp.dot(d_proj, w_qkv.T, preferred_element_type=jnp.float32)
    d_resid, d_gain_one = norm_back(d_normed, resid, scale_one, gain_one)
    return (d_hidden + d_resid, (d_wqkv, d_wout, d_wgu, d_down, d_gain_one, d_gain_two))

def reference(layer_in, out_grad, segment_ids, block_pair, params, norm_gains):
    first_layer = unpack(params[0], norm_gains[0])
    second_layer = unpack(params[1], norm_gains[1])

    def one_sequence(totals, members):
        seq_in, seq_cot, seg_row = members
        meta = layout(seg_row, block_pair)
        out_zero, saved_zero = layer_forward(seq_in, first_layer, meta)
        out_one, saved_one = layer_forward(out_zero, second_layer, meta)
        grad_one, parts_one = layer_backward(seq_cot, saved_one, second_layer, meta)
        grad_zero, parts_zero = layer_backward(grad_one, saved_zero, first_layer, meta)
        totals = jax.tree.map(jnp.add, totals, (parts_zero, parts_one))
        return (totals, (out_zero, out_one, grad_zero, grad_one))

    def zero_parts(weights):
        return tuple((jnp.zeros(member.shape, jnp.float32) for member in weights))
    start_sums = (zero_parts(first_layer), zero_parts(second_layer))
    totals, (out_zero, out_one, grad_zero, grad_one) = lax.scan(one_sequence, start_sums, (layer_in, out_grad, segment_ids))

    def flatten(parts):
        return (jnp.concatenate([member.reshape(-1) for member in parts[:4]]), jnp.concatenate([parts[4], parts[5]]))
    flat_zero, gain_zero = flatten(totals[0])
    flat_one, gain_one = flatten(totals[1])
    return (jnp.stack([out_zero, out_one]), jnp.stack([grad_zero, grad_one]), jnp.stack([flat_zero, flat_one]), jnp.stack([gain_zero, gain_one]))
```

```python
import functools

import jax
import jax.numpy as jnp
from jax import lax
from jax.experimental import pallas as pl
from jax.experimental.pallas import tpu as pltpu
from jax.sharding import PartitionSpec as P

H = 15
KVH = 5
HD = 64
D = 960
FF = 2560
GRP = H // KVH
R = 128
SHARDS = 64
SHARD = 153600
ROWS = 1280
KEYS = 4096
CHUNK = 512
PADD = 1024

eps = 1e-05
rope_theta = 100000.0
masked_fill = -1e30
f32 = jnp.float32
bf16 = jnp.bfloat16
ALL = ("phase", "ctx", "fsdp")

NT = (((1,), (1,)), ((), ()))


def mm(a, b):
    return jnp.dot(a, b, preferred_element_type=f32)


def mm_nt(a, b):
    return lax.dot_general(a, b, NT, preferred_element_type=f32)


def moved(block, shift, phases):
    dy, dx, dz = shift
    pairs = []
    for p in phases:
        for y in range(4):
            for x in range(4):
                for z in range(4):
                    to = (((y + dy) % 4) * 4 + (x + dx) % 4) * 4 + (z + dz) % 4
                    pairs.append((p * 64 + (y * 4 + x) * 4 + z, p * 64 + to))
    return lax.ppermute(block, ALL, pairs)


def unit(axis, step):
    shift = [0, 0, 0]
    shift[axis] = step
    return tuple(shift)


def ring_gather(block, axis, phases, half):
    low, high = half
    from_prev = moved(block, unit(axis, 1), phases)
    from_next = moved(block, unit(axis, -1), phases)
    far_low = moved(low(from_prev), unit(axis, 1), phases)
    far_high = moved(high(from_next), unit(axis, -1), phases)
    return from_next, far_low, far_high, from_prev


def ring_scatter(parts, axis, phases, half, joined):
    low, high = half
    add = lambda a, b: (a.astype(f32) + b.astype(f32)).astype(bf16)
    far_low = moved(low(parts[2]), unit(axis, 1), phases)
    far_high = moved(high(parts[2]), unit(axis, -1), phases)
    up = joined(add(low(parts[1]), far_low), high(parts[1]))
    down = joined(low(parts[3]), add(high(parts[3]), far_high))
    got_up = moved(up, unit(axis, 1), phases)
    got_down = moved(down, unit(axis, -1), phases)
    return parts[0].astype(f32) + got_up.astype(f32) + got_down.astype(f32)


def halves(dim, at):
    low = lambda v: lax.slice_in_dim(v, 0, at, axis=dim)
    high = lambda v: lax.slice_in_dim(v, at, v.shape[dim], axis=dim)
    return low, high


def gather_keys(kv, phases):
    half = halves(kv.ndim - 2, R // 2)

    def ring(block, axis):
        dim = block.ndim - 2
        nxt, flow, fhigh, prev = ring_gather(block, axis, phases, halves(dim, R // 2))
        return jnp.stack([block, nxt, jnp.concatenate([flow, fhigh], axis=dim), prev])

    far = moved(kv, (0, 0, 2), phases)
    first = ring(ring(kv, 0), 1)
    second = ring(ring(far, 1), 0)
    return jnp.concatenate(
        [first.reshape(16, R, 2 * KVH * HD), second.reshape(16, R, 2 * KVH * HD)]
    ).reshape(KEYS, 2 * KVH * HD)


def key_order(y, x, zh):
    order = []
    for bx in range(4):
        for by in range(4):
            order.append(((y + by) % 4) * 8 + ((x + bx) % 4) * 2 + zh)
    for by in range(4):
        for bx in range(4):
            order.append(((y + by) % 4) * 8 + ((x + bx) % 4) * 2 + (1 - zh))
    return jnp.stack(order)


def scatter_keys(d_kv, phases):
    parts = d_kv.reshape(2, 4, 4, R, 2 * KVH * HD)

    def ring(block, axis):
        dim = block.ndim - 3
        joined = lambda a, b: jnp.concatenate([a, b], axis=dim)
        return ring_scatter(
            [block[o] for o in range(4)], axis, phases, halves(dim, R // 2), joined
        )

    first = ring(ring(parts[0], 1).astype(bf16), 0)
    second = ring(ring(parts[1], 0).astype(bf16), 1)
    return first + moved(second.astype(bf16), (0, 0, 2), phases).astype(f32)


PART_ROWS = ((0, 432), (432, 864), (864, 1280))


def scatter_grads(rel):
    both = (0, 1)
    out = []
    for part, (begin, end) in enumerate(PART_ROWS):
        block = rel[:, :, :, begin:end]
        count = end - begin
        at = count // 32 * 16
        left = [0, 1, 2]
        for step in range(3):
            axis = (part + step) % 3
            where_axis = left.index(axis)
            left.remove(axis)
            pieces = [
                lax.index_in_dim(block, o, axis=where_axis, keepdims=False) for o in range(4)
            ]
            dim = pieces[0].ndim - 2
            joined = lambda a, b, dim=dim: jnp.concatenate([a, b], axis=dim)
            block = ring_scatter(pieces, axis, both, halves(dim, at), joined)
            if step < 2:
                block = block.astype(bf16)
        out.append(block)
    return jnp.concatenate(out)


def lane_of(shape):
    return lax.broadcasted_iota(jnp.int32, shape, len(shape) - 1)


def half_swapped(block):
    lane = lane_of(block.shape)
    return jnp.where(lane % HD < HD // 2, pltpu.roll(block, 96, 1), pltpu.roll(block, 32, 1))


def qkv_weight(w_ref, c):
    return w_ref[:, 96 * c : 96 * c + 96, :].reshape(D, 128)


def normed_of(u, gain):
    scale = lax.rsqrt(jnp.mean(u * u, axis=-1, keepdims=True) + eps)
    return scale, (u * scale * gain).astype(bf16)


def project_kernel(u_ref, g_ref, cos_ref, sin_ref, w_ref, qt_ref, kv_ref):
    u = u_ref[...].astype(f32)
    _, a = normed_of(u, g_ref[...])
    cos, sin = cos_ref[...], sin_ref[...]
    blocks = []
    for c in range(0, 13, 2):
        if c + 1 < 13:
            w = jnp.concatenate([qkv_weight(w_ref, c), qkv_weight(w_ref, c + 1)], axis=1)
        else:
            w = qkv_weight(w_ref, c)
        y = mm(a, w)
        for k in range(w.shape[1] // 128):
            b = y[:, 128 * k : 128 * k + 128]
            if c + k < 10:
                b = b * cos + half_swapped(b) * sin
            blocks.append(b)
    for c in range(8):
        t = (blocks[c].astype(bf16).astype(f32) * 0.125).T.astype(bf16)
        count = 128 if c < 7 else 64
        qt_ref[128 * c : 128 * c + count, :] = t[:count]
    lane = lane_of((R, 128))
    for g in range(KVH):
        k, v = blocks[(15 + g) // 2], blocks[(20 + g) // 2]
        if (15 + g) % 2:
            k = pltpu.roll(k, 64, 1)
        if (20 + g) % 2 == 0:
            v = pltpu.roll(v, 64, 1)
        kv_ref[:, 128 * g : 128 * g + 128] = jnp.where(lane < 64, k, v).astype(bf16)


def project(u, gain, cos, sin, weights):
    return pl.pallas_call(
        project_kernel,
        name="project",
        grid=(1,),
        in_specs=[
            pl.BlockSpec((R, D), lambda i: (0, 0)),
            pl.BlockSpec((1, D), lambda i: (0, 0)),
            pl.BlockSpec((R, 128), lambda i: (0, 0)),
            pl.BlockSpec((R, 128), lambda i: (0, 0)),
            pl.BlockSpec((10, ROWS, 128), lambda i: (0, 0, 0)),
        ],
        out_specs=[
            pl.BlockSpec((D, R), lambda i: (0, 0)),
            pl.BlockSpec((R, 640), lambda i: (0, 0)),
        ],
        out_shape=[
            jax.ShapeDtypeStruct((D, R), bf16),
            jax.ShapeDtypeStruct((R, 640), bf16),
        ],
        compiler_params=pltpu.CompilerParams(vmem_limit_bytes=48 << 20),
        cost_estimate=pl.CostEstimate(flops=400_000_000, bytes_accessed=4_000_000, transcendentals=0),
    )(u, gain, cos, sin, weights)


def heads_wide(ref, low):
    top = jnp.concatenate([ref[64 * h : 64 * h + 64, :] for h in range(GRP)], axis=1)
    zero = jnp.zeros_like(top)
    return jnp.concatenate([top, zero] if low else [zero, top], axis=0)


def attend_kernel(qt_ref, kv_ref, bias_ref, mixed_ref, lse_ref, s_ref):
    q = heads_wide(qt_ref, True)
    peak = jnp.full((1, GRP * R), masked_fill, f32)
    for i in range(KEYS // CHUNK):
        rows = slice(CHUNK * i, CHUNK * i + CHUNK)
        b = bias_ref[rows, :]
        s = mm(kv_ref[rows, :], q) + jnp.concatenate([b, b, b], axis=1)
        s_ref[rows, :] = s
        peak = jnp.maximum(peak, jnp.max(s, axis=0, keepdims=True))
    total = jnp.zeros((1, GRP * R), f32)
    acc = jnp.zeros((128, GRP * R), f32)
    for i in range(KEYS // CHUNK):
        rows = slice(CHUNK * i, CHUNK * i + CHUNK)
        p = jnp.exp(s_ref[rows, :] - peak)
        total = total + jnp.sum(p, axis=0, keepdims=True)
        acc = acc + mm(kv_ref[rows, :].T, p.astype(bf16))
    lse_ref[0] = peak + jnp.log(total)
    o = (acc[64:] / total).astype(bf16)
    for h in range(GRP):
        mixed_ref[64 * h : 64 * h + 64, :] = o[:, 128 * h : 128 * h + 128]


def attend(qt, kv_all, bias):
    return pl.pallas_call(
        attend_kernel,
        name="attend",
        grid=(KVH,),
        in_specs=[
            pl.BlockSpec((GRP * HD, R), lambda g: (g, 0)),
            pl.BlockSpec((KEYS, 128), lambda g: (0, g)),
            pl.BlockSpec((KEYS, R), lambda g: (0, 0)),
        ],
        out_specs=[
            pl.BlockSpec((GRP * HD, R), lambda g: (g, 0)),
            pl.BlockSpec((1, 1, GRP * R), lambda g: (g, 0, 0)),
        ],
        out_shape=[
            jax.ShapeDtypeStruct((D, R), bf16),
            jax.ShapeDtypeStruct((KVH, 1, GRP * R), f32),
        ],
        scratch_shapes=[pltpu.VMEM((KEYS, GRP * R), f32)],
        compiler_params=pltpu.CompilerParams(vmem_limit_bytes=48 << 20),
        cost_estimate=pl.CostEstimate(
            flops=4_000_000_000, bytes_accessed=8_000_000, transcendentals=7_900_000
        ),
    )(qt, kv_all, bias)


def out_weight(refs, c):
    return jnp.concatenate(
        [ref[:, 160 * c : 160 * c + 160, :].reshape(320, 128) for ref in refs], axis=0
    )


def gu_weight(refs, c):
    gl, gh, ul, uh = refs
    gate = jnp.concatenate([gl[:, c].reshape(512, 128), gh[:, c].reshape(512, 128)], axis=0)
    up = jnp.concatenate([ul[:, c].reshape(512, 128), uh[:, c].reshape(512, 128)], axis=0)
    return jnp.concatenate([gate, up], axis=1)


def down_weight(ref, c):
    return ref[:, 160 * c : 160 * c + 160, :].reshape(640, 128)


WEIGHT_SPECS = (
    [pl.BlockSpec((2, ROWS, 128), lambda j, k=k: (5 + k, 0, 0)) for k in range(3)]
    + [
        pl.BlockSpec((16, 5, 32, 128), lambda j, d=d, o=o: (1 + d, o + j, 0, 0))
        for o in (0, 4)
        for d in (0, 1)
    ]
    + [pl.BlockSpec((4, ROWS, 128), lambda j: (12 + j, 0, 0))]
)


def weight_args(gathered):
    fine = gathered.reshape(SHARDS, 40, 32, 128)
    return [gathered] * 3 + [fine] * 4 + [gathered]


def feed_kernel(
    mixed_ref, u_ref, g_ref, pad_ref, o0, o1, o2, gl, gh, ul, uh, wd,
    y_ref, h_ref, nt_ref, gate_ref, up_ref, mt_ref, n_scr, y_scr,
):
    step = pl.program_id(0)

    @pl.when(step == 0)
    def _():
        mixed = mixed_ref[...].T
        for c in range(0, 8, 2):
            w = jnp.concatenate(
                [out_weight((o0, o1, o2), c), out_weight((o0, o1, o2), c + 1)], axis=1
            )
            y = mm(mixed, w)
            end = min(128 * c + 256, D)
            h_ref[:, 128 * c : end] = u_ref[:, 128 * c : end].astype(f32) + y[:, : end - 128 * c]
        _, n = normed_of(h_ref[...], g_ref[...])
        padded = mm(n, pad_ref[...])
        n_scr[...] = padded.astype(bf16)
        nt_ref[...] = padded.T.astype(bf16)
        y_scr[...] = jnp.zeros_like(y_scr)

    n = n_scr[...]
    inner = []
    for c in range(5):
        gu = mm(n, gu_weight((gl, gh, ul, uh), c))
        gate, up = gu[:, :128], gu[:, 128:]
        cols = slice(128 * c, 128 * c + 128)
        gate_ref[:, cols] = gate
        up_ref[:, cols] = up
        m = gate * jax.nn.sigmoid(gate) * up
        mt_ref[cols, :] = m.T.astype(bf16)
        inner.append(m.astype(bf16))
    inner = jnp.concatenate(inner, axis=1)
    for c in range(0, 8, 2):
        w = jnp.concatenate([down_weight(wd, c), down_weight(wd, c + 1)], axis=1)
        y_scr[:, 128 * c : 128 * c + 256] += mm(inner, w)

    @pl.when(step == 3)
    def _():
        y_ref[...] = (h_ref[...] + y_scr[:, :D]).astype(bf16)


def feed(mixed, u, gain, pad, gathered):
    whole = lambda *shape: pl.BlockSpec(shape, lambda j: (0,) * len(shape))
    return pl.pallas_call(
        feed_kernel,
        name="feed",
        grid=(4,),
        in_specs=[whole(D, R), whole(R, D), whole(1, D), whole(D, PADD)] + WEIGHT_SPECS,
        out_specs=[
            whole(R, D),
            whole(R, D),
            whole(PADD, R),
            pl.BlockSpec((R, 640), lambda j: (0, j)),
            pl.BlockSpec((R, 640), lambda j: (0, j)),
            pl.BlockSpec((640, R), lambda j: (j, 0)),
        ],
        out_shape=[
            jax.ShapeDtypeStruct((R, D), bf16),
            jax.ShapeDtypeStruct((R, D), f32),
            jax.ShapeDtypeStruct((PADD, R), bf16),
            jax.ShapeDtypeStruct((R, FF), f32),
            jax.ShapeDtypeStruct((R, FF), f32),
            jax.ShapeDtypeStruct((FF, R), bf16),
        ],
        scratch_shapes=[pltpu.VMEM((R, PADD), bf16), pltpu.VMEM((R, PADD), f32)],
        compiler_params=pltpu.CompilerParams(vmem_limit_bytes=48 << 20),
        cost_estimate=pl.CostEstimate(
            flops=2_200_000_000, bytes_accessed=22_000_000, transcendentals=400_000
        ),
    )(mixed, u, gain, pad, *weight_args(gathered))


def norm_back(d_out, values, gain):
    scales = lax.rsqrt(jnp.mean(values * values, axis=-1, keepdims=True) + eps)
    scaled = d_out * gain
    d_gain = jnp.sum(d_out * values * scales, axis=0, keepdims=True)
    d_values = scales * scaled - values * (scales * scales * scales) * jnp.mean(
        scaled * values, axis=-1, keepdims=True
    )
    return d_values, d_gain


def feed_back_kernel(
    c_ref, gate_ref, up_ref, h_ref, g_ref, pad_ref, o0, o1, o2, gl, gh, ul, uh, wd,
    dgate_ref, dup_ref, dh_ref, dhb_ref, dg_ref, dot_ref, cb_ref, dn_scr,
):
    step = pl.program_id(0)

    @pl.when(step == 0)
    def _():
        cb_ref[...] = jnp.zeros_like(cb_ref)
        cb_ref[:, :D] = c_ref[...].astype(bf16)
        dn_scr[...] = jnp.zeros_like(dn_scr)

    d_inner = jnp.zeros((R, 640), f32)
    for c in range(0, 8, 2):
        w = jnp.concatenate([down_weight(wd, c), down_weight(wd, c + 1)], axis=1)
        d_inner = d_inner + mm_nt(cb_ref[:, 128 * c : 128 * c + 256], w)
    for c in range(5):
        cols = slice(128 * c, 128 * c + 128)
        gate, up, dm = gate_ref[:, cols], up_ref[:, cols], d_inner[:, cols]
        sigma = jax.nn.sigmoid(gate)
        d_gate = (dm * up * sigma * (1.0 + gate * (1.0 - sigma))).astype(bf16)
        d_up = (dm * gate * sigma).astype(bf16)
        dgate_ref[:, cols] = d_gate
        dup_ref[:, cols] = d_up
        both = jnp.concatenate([d_gate, d_up], axis=1)
        dn_scr[...] += mm_nt(both, gu_weight((gl, gh, ul, uh), c))

    @pl.when(step == 3)
    def _():
        padded = dn_scr[...]
        high = padded.astype(bf16)
        low = (padded - high.astype(f32)).astype(bf16)
        dn = mm_nt(high, pad_ref[...]) + mm_nt(low, pad_ref[...])
        d_h, d_gain = norm_back(dn, h_ref[...], g_ref[...])
        d_h = c_ref[...] + d_h
        dg_ref[...] = d_gain
        dh_ref[...] = d_h
        dhb_ref[...] = jnp.zeros_like(dhb_ref)
        dhb_ref[:, :D] = d_h.astype(bf16)
        d_mixed = jnp.zeros((R, D), f32)
        for c in range(0, 8, 2):
            w = jnp.concatenate(
                [out_weight((o0, o1, o2), c), out_weight((o0, o1, o2), c + 1)], axis=1
            )
            d_mixed = d_mixed + mm_nt(dhb_ref[:, 128 * c : 128 * c + 256], w)
        dot_ref[...] = d_mixed.T


def feed_back(cot, gate, up, hidden, gain, pad, gathered):
    whole = lambda *shape: pl.BlockSpec(shape, lambda j: (0,) * len(shape))
    block = pl.BlockSpec((R, 640), lambda j: (0, j))
    return pl.pallas_call(
        feed_back_kernel,
        name="feed_back",
        grid=(4,),
        in_specs=[whole(R, D), block, block, whole(R, D), whole(1, D), whole(D, PADD)]
        + WEIGHT_SPECS,
        out_specs=[
            block,
            block,
            whole(R, D),
            whole(R, PADD),
            whole(1, D),
            whole(D, R),
            whole(R, PADD),
        ],
        out_shape=[
            jax.ShapeDtypeStruct((R, FF), bf16),
            jax.ShapeDtypeStruct((R, FF), bf16),
            jax.ShapeDtypeStruct((R, D), f32),
            jax.ShapeDtypeStruct((R, PADD), bf16),
            jax.ShapeDtypeStruct((1, D), f32),
            jax.ShapeDtypeStruct((D, R), f32),
            jax.ShapeDtypeStruct((R, PADD), bf16),
        ],
        scratch_shapes=[pltpu.VMEM((R, PADD), f32)],
        compiler_params=pltpu.CompilerParams(vmem_limit_bytes=48 << 20),
        cost_estimate=pl.CostEstimate(
            flops=2_200_000_000, bytes_accessed=22_000_000, transcendentals=400_000
        ),
    )(cot, gate, up, hidden, gain, pad, *weight_args(gathered))


def attend_back_kernel(
    qt_ref, kv_ref, bias_ref, dot_ref, mixed_ref, lse_ref, dkv_ref, dqt_ref
):
    q = heads_wide(qt_ref, True)
    d_o = heads_wide(dot_ref, False)
    o = heads_wide(mixed_ref, False)
    delta = jnp.sum(d_o * o.astype(f32), axis=0, keepdims=True)
    d_o = d_o.astype(bf16)
    lse = lse_ref[0]
    both = jnp.concatenate([q, d_o], axis=1)
    acc = jnp.zeros((128, GRP * R), f32)
    for i in range(KEYS // CHUNK):
        rows = slice(CHUNK * i, CHUNK * i + CHUNK)
        b = bias_ref[rows, :]
        kv = kv_ref[rows, :]
        p = jnp.exp(mm(kv, q) + jnp.concatenate([b, b, b], axis=1) - lse)
        ds = (p * (mm(kv, d_o) - delta)).astype(bf16)
        dkv_ref[rows, :] = mm_nt(jnp.concatenate([ds, p.astype(bf16)], axis=1), both).astype(bf16)
        acc = acc + mm(kv.T, ds)
    acc = acc[:64] * 0.125
    for h in range(GRP):
        dqt_ref[64 * h : 64 * h + 64, :] = acc[:, 128 * h : 128 * h + 128]


def attend_back(qt, kv_all, bias, d_mixed, mixed, lse):
    heads = pl.BlockSpec((GRP * HD, R), lambda g: (g, 0))
    return pl.pallas_call(
        attend_back_kernel,
        name="attend_back",
        grid=(KVH,),
        in_specs=[
            heads,
            pl.BlockSpec((KEYS, 128), lambda g: (0, g)),
            pl.BlockSpec((KEYS, R), lambda g: (0, 0)),
            heads,
            heads,
            pl.BlockSpec((1, 1, GRP * R), lambda g: (g, 0, 0)),
        ],
        out_specs=[pl.BlockSpec((KEYS, 128), lambda g: (0, g)), heads],
        out_shape=[
            jax.ShapeDtypeStruct((KEYS, 640), bf16),
            jax.ShapeDtypeStruct((D, R), f32),
        ],
        compiler_params=pltpu.CompilerParams(vmem_limit_bytes=48 << 20),
        cost_estimate=pl.CostEstimate(
            flops=10_000_000_000, bytes_accessed=14_000_000, transcendentals=7_900_000
        ),
    )(qt, kv_all, bias, d_mixed, mixed, lse)


def project_back_kernel(
    dqt_ref, dkv_ref, cos_ref, sin_ref, u_ref, g_ref, dh_ref, w_ref,
    du_ref, dqkv_ref, at_ref, dg_ref,
):
    cos, sin = cos_ref[...], sin_ref[...]
    lane = lane_of((R, 128))
    dkv = [dkv_ref[:, 128 * g : 128 * g + 128] for g in range(KVH)]
    rolled = [pltpu.roll(b, 64, 1) for b in dkv]
    zero = jnp.zeros((R, 128), f32)
    blocks = [dqt_ref[128 * c : 128 * c + 128, :].T for c in range(7)]
    last = jnp.concatenate([dqt_ref[896:960, :], jnp.zeros((64, R), f32)], axis=0).T
    low = lane < 64
    blocks.append(jnp.where(low, last, rolled[0]))
    blocks.append(jnp.where(low, dkv[1], rolled[2]))
    blocks.append(jnp.where(low, dkv[3], rolled[4]))
    blocks = [b * cos - half_swapped(b) * sin for b in blocks]
    blocks.append(jnp.where(low, rolled[0], dkv[1]))
    blocks.append(jnp.where(low, rolled[2], dkv[3]))
    blocks.append(jnp.where(low, rolled[4], zero))
    da = jnp.zeros((R, D), f32)
    for c in range(0, 13, 2):
        if c + 1 < 13:
            d = jnp.concatenate([blocks[c], blocks[c + 1]], axis=1).astype(bf16)
            w = jnp.concatenate([qkv_weight(w_ref, c), qkv_weight(w_ref, c + 1)], axis=1)
        else:
            d, w = blocks[c].astype(bf16), qkv_weight(w_ref, c)
        dqkv_ref[:, 128 * c : 128 * c + d.shape[1]] = d
        da = da + mm_nt(d, w)
    u = u_ref[...].astype(f32)
    gain = g_ref[...]
    _, a = normed_of(u, gain)
    at_ref[...] = a.T
    d_u, d_gain = norm_back(da, u, gain)
    dg_ref[...] = d_gain
    du_ref[...] = dh_ref[...] + d_u


def project_back(d_query, d_kv, cos, sin, u, gain, d_hidden, weights):
    whole = lambda *shape: pl.BlockSpec(shape, lambda j: (0,) * len(shape))
    return pl.pallas_call(
        project_back_kernel,
        name="project_back",
        grid=(1,),
        in_specs=[
            whole(D, R),
            whole(R, 640),
            whole(R, 128),
            whole(R, 128),
            whole(R, D),
            whole(1, D),
            whole(R, D),
            whole(10, ROWS, 128),
        ],
        out_specs=[whole(R, D), whole(R, 13 * 128), whole(D, R), whole(1, D)],
        out_shape=[
            jax.ShapeDtypeStruct((R, D), f32),
            jax.ShapeDtypeStruct((R, 13 * 128), bf16),
            jax.ShapeDtypeStruct((D, R), bf16),
            jax.ShapeDtypeStruct((1, D), f32),
        ],
        compiler_params=pltpu.CompilerParams(vmem_limit_bytes=48 << 20),
        cost_estimate=pl.CostEstimate(flops=400_000_000, bytes_accessed=5_000_000, transcendentals=0),
    )(d_query, d_kv, cos, sin, u, gain, d_hidden, weights)


def outer_kernel(
    place_ref, at_ref, dqkv_ref, mixed_ref, dhb_ref, nt_ref, dgate_ref, dup_ref, mt_ref, cb_ref,
    gain_ref, out_ref,
):
    shard = pl.program_id(0)
    gains = gain_ref[pl.ds(shard, 1), :]

    def row_of(count, at):
        row = lax.broadcasted_iota(jnp.int32, (count, 128), 0)
        return jnp.where(row == at, gains, 0.0)

    @pl.when(shard < 10)
    def _():
        rows = at_ref[pl.ds(pl.multiple_of(96 * shard, 32), 96), :]
        res = mm(rows, dqkv_ref[...])
        for c in range(13):
            out_ref[0, 96 * c : 96 * c + 96, :] = res[:, 128 * c : 128 * c + 128].astype(bf16)
        out_ref[0, 1248:1280, :] = row_of(32, 0).astype(bf16)

    def wide(rows, cot):
        res = mm(rows, cot)
        for c in range(8):
            b = res[:, 128 * c : 128 * c + 128]
            if c == 7:
                b = b + row_of(160, 0)
            out_ref[0, 160 * c : 160 * c + 160, :] = b.astype(bf16)

    @pl.when((shard >= 10) & (shard < 16))
    def _():
        wide(mixed_ref[pl.ds(pl.multiple_of(160 * (shard - 10), 32), 160), :], dhb_ref[...])

    @pl.when((shard >= 16) & (shard < 48))
    def _():
        rows = nt_ref[pl.ds(pl.multiple_of(32 * (shard - 16), 32), 32), :]
        for part, ref in enumerate((dgate_ref, dup_ref)):
            res = mm(rows, ref[...])
            for c in range(20):
                b = res[:, 128 * c : 128 * c + 128]
                at = 32 * (20 * part + c)
                if part == 0 and c == 0:
                    b = b + row_of(32, 30)
                out_ref[0, at : at + 32, :] = b.astype(bf16)

    @pl.when(shard >= 48)
    def _():
        wide(mt_ref[pl.ds(pl.multiple_of(160 * (shard - 48), 32), 160), :], cb_ref[...])


def outer(places, at, dqkv, mixed, dhb, nt, dgate, dup, mt, cb, gains):
    whole = lambda v: pl.BlockSpec(v.shape, lambda s, place: (0,) * v.ndim)
    args = (at, dqkv, mixed, dhb, nt, dgate, dup, mt, cb, gains)
    return pl.pallas_call(
        outer_kernel,
        name="outer",
        grid_spec=pltpu.PrefetchScalarGridSpec(
            num_scalar_prefetch=1,
            grid=(SHARDS,),
            in_specs=[whole(v) for v in args],
            out_specs=pl.BlockSpec((1, ROWS, 128), lambda s, place: (place[s], 0, 0)),
        ),
        out_shape=jax.ShapeDtypeStruct((SHARDS, ROWS, 128), bf16),
        compiler_params=pltpu.CompilerParams(vmem_limit_bytes=48 << 20),
        cost_estimate=pl.CostEstimate(
            flops=2_600_000_000, bytes_accessed=24_000_000, transcendentals=0
        ),
    )(places, *args)


def shard_kind(rank):
    return jnp.where(rank < 10, 0, jnp.where((rank >= 16) & (rank < 48), 2, 1))


def shard_blocks(flat, gains, rank):
    g = jnp.zeros((1, 128), bf16).at[0, :30].set(gains)

    def narrow(_):
        w = jnp.pad(flat.reshape(96, 1600), ((0, 0), (0, 64)))
        w = w.reshape(96, 13, 128).transpose(1, 0, 2).reshape(1248, 128)
        return jnp.concatenate([w, jnp.pad(g, ((0, 31), (0, 0)))])

    def square(_):
        w = jnp.pad(flat.reshape(160, 960), ((0, 0), (0, 64)))
        w = w.reshape(160, 8, 128).transpose(1, 0, 2)
        last = jnp.concatenate([jnp.zeros((1, 64), bf16), g[:, :64]], axis=1)
        return w.at[7, 0].add(last[0]).reshape(ROWS, 128)

    def broad(_):
        w = jnp.pad(flat.reshape(30, 40, 128), ((0, 2), (0, 0), (0, 0))).transpose(1, 0, 2)
        return w.at[0, 30].set(g[0]).reshape(ROWS, 128)

    return lax.switch(shard_kind(rank), [narrow, square, broad], 0)


def blocks_shard(blocks, rank):
    def narrow(_):
        w = blocks[:1248].reshape(13, 96, 128).transpose(1, 0, 2).reshape(96, 1664)[:, :1600]
        return w.reshape(SHARD), blocks[1248, :30]

    def square(_):
        w = blocks.reshape(8, 160, 128).transpose(1, 0, 2).reshape(160, 1024)[:, :960]
        return w.reshape(SHARD), blocks[1120, 64:94]

    def broad(_):
        w = blocks.reshape(40, 32, 128).transpose(1, 0, 2)[:30]
        return w.reshape(SHARD), blocks[30, :30]

    return lax.switch(shard_kind(rank), [narrow, square, broad], 0)


def gathered_gains(gathered):
    rows = jnp.concatenate(
        [
            gathered[:10, 1248, :30],
            gathered[10:16, 1120, 64:94],
            gathered[16:48, 30, :30],
            gathered[48:, 1120, 64:94],
        ]
    ).astype(f32)
    flat = rows.reshape(1, 2 * D)
    return flat[:, :D], flat[:, D:]


def per_device(layer_in, out_grad, segment_ids, block_pair, params, norm_gains):
    phase = lax.axis_index("phase")
    ctx = lax.axis_index("ctx")
    rank = ctx * 2 + lax.axis_index("fsdp")
    y, x, z = rank // 16, (rank // 4) % 4, rank % 4
    zh = z // 2

    own = shard_blocks(params[0], norm_gains[0], rank)
    gathered = lax.all_gather(own, ("ctx", "fsdp"), axis=0)

    seg_row = segment_ids[0]
    pair = lax.dynamic_index_in_dim(block_pair, ctx, 0, keepdims=False)
    within = jnp.arange(HD, dtype=jnp.int32)
    place_q = jnp.concatenate([pair * 64 + within, (63 - pair) * 64 + within])
    seg_q = jnp.concatenate(
        [
            lax.dynamic_slice_in_dim(seg_row, pair * 64, 64),
            lax.dynamic_slice_in_dim(seg_row, (63 - pair) * 64, 64),
        ]
    )
    start_q = jnp.sum((seg_row[:, None] < seg_q[None, :]).astype(jnp.int32), axis=0)
    pairs_k = block_pair[key_order(y, x, zh)]
    place_k = (
        jnp.stack([pairs_k, 63 - pairs_k], axis=1)[:, :, None] * 64 + within[None, None, :]
    ).reshape(KEYS)
    bias = jnp.where(
        (place_k[:, None] <= place_q[None, :]) & (place_k[:, None] >= start_q[None, :]),
        0.0,
        masked_fill,
    ).astype(f32)
    frequency = rope_theta ** (-2.0 * jnp.arange(HD // 2, dtype=f32) / HD)
    angles = (place_q - start_q).astype(f32)[:, None] * frequency[None, :]
    cosine, sine = jnp.cos(angles), jnp.sin(angles)
    cos = jnp.concatenate([cosine] * 4, axis=1)
    sin = jnp.concatenate([-sine, sine, -sine, sine], axis=1)
    spread = jnp.arange(PADD, dtype=jnp.int32)
    target = jnp.where(spread % 32 < 30, (spread // 32) * 30 + spread % 32, -1)
    pad = (jnp.arange(D, dtype=jnp.int32)[:, None] == target[None, :]).astype(bf16)

    gain_one, gain_two = gathered_gains(gathered)
    first = phase == 0

    u = layer_in[0]
    kv_all = None
    for tick in range(2):
        qt, kv = project(u, gain_one, cos, sin, gathered)
        fetched = gather_keys(kv, (tick,))
        kv_all = fetched if tick == 0 else jnp.where(first, kv_all, fetched)
        mixed, lse = attend(qt, kv_all, bias)
        result, hidden, nt, gate, up, mt = feed(mixed, u, gain_two, pad, gathered)
        if tick == 0:
            u = jnp.where(first, u, lax.ppermute(result, "phase", [(0, 1)]))

    cot = out_grad[0]
    kept = None
    for tick in range(2):
        dgate, dup, dh, dhb, dg_two, d_mixed, cb = feed_back(
            cot, gate, up, hidden, gain_two, pad, gathered
        )
        d_kv_all, d_query = attend_back(qt, kv_all, bias, d_mixed, mixed, lse)
        d_kv = scatter_keys(d_kv_all, (1 - tick,))
        kept = d_kv if tick == 0 else jnp.where(first, d_kv, kept)
        d_u, dqkv, at, dg_one = project_back(
            d_query, kept, cos, sin, u, gain_one, dh, gathered
        )
        if tick == 0:
            back = lax.ppermute(d_u.astype(bf16), "phase", [(1, 0)])
            cot = jnp.where(first, back.astype(f32), cot)

    gains = jnp.concatenate([dg_one, dg_two], axis=1).reshape(SHARDS, 30)
    shards = jnp.arange(SHARDS, dtype=jnp.int32)
    square = (((shards >= 10) & (shards < 16)) | (shards >= 48))[:, None]
    gains = jnp.where(
        square, jnp.pad(gains, ((0, 0), (64, 34))), jnp.pad(gains, ((0, 0), (0, 98)))
    )
    sy, sx, sz = shards // 16, (shards // 4) % 4, shards % 4
    places = ((sy - y) % 4) * 16 + ((sx - x) % 4) * 4 + (sz - z) % 4
    grads = outer(places, at, dqkv, mixed, dhb, nt, dgate, dup, mt, cb, gains)
    total = scatter_grads(grads.reshape(4, 4, 4, ROWS, 128))
    param_part, gain_part = blocks_shard(total, rank)
    return (result[None, None], d_u[None, None], param_part[None], gain_part[None])


def solution(mesh):
    return jax.shard_map(
        per_device,
        mesh=mesh,
        in_specs=(
            P("fsdp", "ctx", None),
            P("fsdp", "ctx", None),
            P("fsdp", None),
            P(),
            P("phase", ("ctx", "fsdp")),
            P("phase", ("ctx", "fsdp")),
        ),
        out_specs=(
            P("phase", "fsdp", "ctx", None),
            P("phase", "fsdp", "ctx", None),
            P("phase", ("ctx", "fsdp")),
            P("phase", ("ctx", "fsdp")),
        ),
        check_vma=False,
    )
```

```python
import functools

import jax
import jax.numpy as jnp
from jax import lax
from jax.experimental import pallas as pl
from jax.experimental.pallas import tpu as pltpu
from jax.sharding import PartitionSpec as P

H = 15
KVH = 5
HD = 64
D = 960
FF = 2560
GRP = H // KVH
R = 128
SHARDS = 64
SHARD = 153600
ROWS = 1280
KEYS = 4096
CHUNK = 512
PADD = 1024
SIDE = 3
QSIDE = SIDE * GRP * HD
QPAD = 2 * QSIDE

eps = 1e-05
rope_theta = 100000.0
masked_fill = -1e30
f32 = jnp.float32
bf16 = jnp.bfloat16
ALL = ("phase", "ctx", "fsdp")

NT = (((1,), (1,)), ((), ()))


def mm(a, b):
    return jnp.dot(a, b, preferred_element_type=f32)


def mm_nt(a, b):
    return lax.dot_general(a, b, NT, preferred_element_type=f32)


STEPS = ((1, 3), (3, 1))


def swapped(block, way):
    pairs = []
    for p in range(2):
        dy, dx, dz = way(p)
        for y in range(4):
            for x in range(4):
                for z in range(4):
                    to = ((y ^ dy) * 4 + (x ^ dx)) * 4 + (z ^ dz)
                    pairs.append((p * 64 + (y * 4 + x) * 4 + z, p * 64 + to))
    return lax.ppermute(block, ALL, pairs)


def over(block, source):
    return lax.ppermute(block, "phase", [(source, 1 - source)])


def along(axes, number):
    def way(p):
        shift = [0, 0, 0]
        shift[axes[p]] = STEPS[p][number]
        return tuple(shift)

    return way


def far_z(p):
    return (0, 0, 2)


def gather_keys(kv):
    tail = kv.shape
    far = swapped(kv, far_z)
    near = kv
    orders = (((0, 1), (1, 0)), ((1, 0), (0, 1)))
    blocks = [near[None], far[None]]
    for leg in range(2):
        for number in range(2):
            for k in range(2):
                got = swapped(blocks[k], along(orders[k][leg], number))
                blocks[k] = jnp.concatenate([blocks[k], got], axis=0)
    return jnp.concatenate(blocks, axis=0).reshape(KEYS, tail[1])


def scatter_keys(d_kv):
    parts = d_kv.reshape(2, 16, R, d_kv.shape[1])
    orders = (((0, 1), (1, 0)), ((1, 0), (0, 1)))
    blocks = [parts[0], parts[1]]
    for leg in (1, 0):
        for number in (1, 0):
            for k in (1, 0):
                half = blocks[k].shape[0] // 2
                got = swapped(blocks[k][half:], along(orders[k][leg], number))
                total = blocks[k][:half].astype(f32) + got.astype(f32)
                last = k == 0 and half == 1
                blocks[k] = total if last else total.astype(bf16)
    return blocks[0][0] + swapped(blocks[1][0], far_z).astype(f32)


def slot_offsets(phase):
    return jnp.where(phase == 0, jnp.array([0, 1, 3, 2]), jnp.array([0, 3, 1, 2]))


def slot_of(offset, phase):
    at = jnp.where(phase == 0, jnp.array([0, 1, 3, 2]), jnp.array([0, 2, 3, 1]))
    return at[offset]


def key_order(y, x, zh, phase):
    off = slot_offsets(phase)
    outer = jnp.repeat(off, 4)
    inner = jnp.tile(off, 4)
    out = []
    for k in range(2):
        first_y = phase == k
        oy = jnp.where(first_y, inner, outer)
        ox = jnp.where(first_y, outer, inner)
        out.append((y ^ oy) * 8 + (x ^ ox) * 2 + (zh ^ k))
    return jnp.concatenate(out)


PART_ROWS = ((0, 432), (432, 864), (864, 1280))


def scatter_grads(rel):
    blocks = [rel[:, :, :, begin:end] for begin, end in PART_ROWS]
    left = [[0, 1, 2], [0, 1, 2], [0, 1, 2]]
    for leg in range(3):
        for number in (1, 0):
            for part in range(3):
                axis = (part + leg) % 3
                dim = left[part].index(axis)
                block = blocks[part]
                half = block.shape[dim] // 2
                keep = lax.slice_in_dim(block, 0, half, axis=dim)
                send = lax.slice_in_dim(block, half, 2 * half, axis=dim)
                got = swapped(send, along((axis, axis), number))
                total = keep.astype(f32) + got.astype(f32)
                if number == 0:
                    total = lax.squeeze(total, (dim,))
                    left[part].remove(axis)
                if leg < 2 or number:
                    total = total.astype(bf16)
                blocks[part] = total
    return jnp.concatenate(blocks)


def lane_of(shape):
    return lax.broadcasted_iota(jnp.int32, shape, len(shape) - 1)


def half_swapped(block):
    lane = lane_of(block.shape)
    return jnp.where(lane % HD < HD // 2, pltpu.roll(block, 96, 1), pltpu.roll(block, 32, 1))


def qkv_weight(w_ref, c):
    return w_ref[:, 96 * c : 96 * c + 96, :].reshape(D, 128)


def normed_of(u, gain):
    scale = lax.rsqrt(jnp.mean(u * u, axis=-1, keepdims=True) + eps)
    return scale, (u * scale * gain).astype(bf16)


def project_kernel(u_ref, g_ref, cos_ref, sin_ref, w_ref, qt_ref, kv_ref):
    u = u_ref[...].astype(f32)
    _, a = normed_of(u, g_ref[...])
    cos, sin = cos_ref[...], sin_ref[...]
    blocks = []
    for c in range(0, 13, 2):
        if c + 1 < 13:
            w = jnp.concatenate([qkv_weight(w_ref, c), qkv_weight(w_ref, c + 1)], axis=1)
        else:
            w = qkv_weight(w_ref, c)
        y = mm(a, w)
        for k in range(w.shape[1] // 128):
            b = y[:, 128 * k : 128 * k + 128]
            if c + k < 10:
                b = b * cos + half_swapped(b) * sin
            blocks.append(b)
    for c in range(8):
        t = (blocks[c].astype(bf16).astype(f32) * 0.125).T.astype(bf16)
        count = 128 if c < 7 else 64
        qt_ref[128 * c : 128 * c + count, :] = t[:count]
    qt_ref[D:, :] = jnp.zeros((QPAD - D, R), bf16)
    kv_ref[:, 640:] = jnp.zeros((R, 128), bf16)
    lane = lane_of((R, 128))
    for g in range(KVH):
        k, v = blocks[(15 + g) // 2], blocks[(20 + g) // 2]
        if (15 + g) % 2:
            k = pltpu.roll(k, 64, 1)
        if (20 + g) % 2 == 0:
            v = pltpu.roll(v, 64, 1)
        kv_ref[:, 128 * g : 128 * g + 128] = jnp.where(lane < 64, k, v).astype(bf16)


def project(u, gain, cos, sin, weights):
    return pl.pallas_call(
        project_kernel,
        name="project",
        grid=(1,),
        in_specs=[
            pl.BlockSpec((R, D), lambda i: (0, 0)),
            pl.BlockSpec((1, D), lambda i: (0, 0)),
            pl.BlockSpec((R, 128), lambda i: (0, 0)),
            pl.BlockSpec((R, 128), lambda i: (0, 0)),
            pl.BlockSpec((10, ROWS, 128), lambda i: (0, 0, 0)),
        ],
        out_specs=[
            pl.BlockSpec((QPAD, R), lambda i: (0, 0)),
            pl.BlockSpec((R, 768), lambda i: (0, 0)),
        ],
        out_shape=[
            jax.ShapeDtypeStruct((QPAD, R), bf16),
            jax.ShapeDtypeStruct((R, 768), bf16),
        ],
        compiler_params=pltpu.CompilerParams(vmem_limit_bytes=48 << 20),
        cost_estimate=pl.CostEstimate(flops=400_000_000, bytes_accessed=4_000_000, transcendentals=0),
    )(u, gain, cos, sin, weights)


def heads_wide(ref, low):
    top = jnp.concatenate([ref[64 * h : 64 * h + 64, :] for h in range(GRP)], axis=1)
    zero = jnp.zeros_like(top)
    return jnp.concatenate([top, zero] if low else [zero, top], axis=0)


def attend_kernel(qt_ref, kv_ref, bias_ref, mixed_ref, lse_ref, s_ref):
    q = heads_wide(qt_ref, True)
    peak = jnp.full((1, GRP * R), masked_fill, f32)
    for i in range(KEYS // CHUNK):
        rows = slice(CHUNK * i, CHUNK * i + CHUNK)
        b = bias_ref[rows, :]
        s = mm(kv_ref[rows, :], q) + jnp.concatenate([b, b, b], axis=1)
        s_ref[rows, :] = s
        peak = jnp.maximum(peak, jnp.max(s, axis=0, keepdims=True))
    total = jnp.zeros((1, GRP * R), f32)
    acc = jnp.zeros((128, GRP * R), f32)
    for i in range(KEYS // CHUNK):
        rows = slice(CHUNK * i, CHUNK * i + CHUNK)
        p = jnp.exp(s_ref[rows, :] - peak)
        total = total + jnp.sum(p, axis=0, keepdims=True)
        acc = acc + mm(kv_ref[rows, :].T, p.astype(bf16))
    lse_ref[0] = peak + jnp.log(total)
    o = (acc[64:] / total).astype(bf16)
    for h in range(GRP):
        mixed_ref[64 * h : 64 * h + 64, :] = o[:, 128 * h : 128 * h + 128]


def attend(qt, kv_all, bias):
    return pl.pallas_call(
        attend_kernel,
        name="attend",
        grid=(SIDE,),
        in_specs=[
            pl.BlockSpec((GRP * HD, R), lambda g: (g, 0)),
            pl.BlockSpec((KEYS, 128), lambda g: (0, g)),
            pl.BlockSpec((KEYS, R), lambda g: (0, 0)),
        ],
        out_specs=[
            pl.BlockSpec((GRP * HD, R), lambda g: (g, 0)),
            pl.BlockSpec((1, 1, GRP * R), lambda g: (g, 0, 0)),
        ],
        out_shape=[
            jax.ShapeDtypeStruct((QSIDE, R), bf16),
            jax.ShapeDtypeStruct((SIDE, 1, GRP * R), f32),
        ],
        scratch_shapes=[pltpu.VMEM((KEYS, GRP * R), f32)],
        compiler_params=pltpu.CompilerParams(vmem_limit_bytes=48 << 20),
        cost_estimate=pl.CostEstimate(
            flops=4_000_000_000, bytes_accessed=8_000_000, transcendentals=7_900_000
        ),
    )(qt, kv_all, bias)


def out_weight(refs, c):
    return jnp.concatenate(
        [ref[:, 160 * c : 160 * c + 160, :].reshape(320, 128) for ref in refs], axis=0
    )


def gu_weight(refs, c):
    gl, gh, ul, uh = refs
    gate = jnp.concatenate([gl[:, c].reshape(512, 128), gh[:, c].reshape(512, 128)], axis=0)
    up = jnp.concatenate([ul[:, c].reshape(512, 128), uh[:, c].reshape(512, 128)], axis=0)
    return jnp.concatenate([gate, up], axis=1)


def down_weight(ref, c):
    return ref[:, 160 * c : 160 * c + 160, :].reshape(640, 128)


WEIGHT_SPECS = (
    [pl.BlockSpec((2, ROWS, 128), lambda j, k=k: (5 + k, 0, 0)) for k in range(3)]
    + [
        pl.BlockSpec((16, 5, 32, 128), lambda j, d=d, o=o: (1 + d, o + j, 0, 0))
        for o in (0, 4)
        for d in (0, 1)
    ]
    + [pl.BlockSpec((4, ROWS, 128), lambda j: (12 + j, 0, 0))]
)


def weight_args(gathered):
    fine = gathered.reshape(SHARDS, 40, 32, 128)
    return [gathered] * 3 + [fine] * 4 + [gathered]


def feed_kernel(
    mixed_ref, u_ref, g_ref, pad_ref, o0, o1, o2, gl, gh, ul, uh, wd,
    y_ref, h_ref, nt_ref, gate_ref, up_ref, mt_ref, n_scr, y_scr,
):
    step = pl.program_id(0)

    @pl.when(step == 0)
    def _():
        mixed = mixed_ref[...].T
        for c in range(0, 8, 2):
            w = jnp.concatenate(
                [out_weight((o0, o1, o2), c), out_weight((o0, o1, o2), c + 1)], axis=1
            )
            y = mm(mixed, w)
            end = min(128 * c + 256, D)
            h_ref[:, 128 * c : end] = u_ref[:, 128 * c : end].astype(f32) + y[:, : end - 128 * c]
        _, n = normed_of(h_ref[...], g_ref[...])
        padded = mm(n, pad_ref[...])
        n_scr[...] = padded.astype(bf16)
        nt_ref[...] = padded.T.astype(bf16)
        y_scr[...] = jnp.zeros_like(y_scr)

    n = n_scr[...]
    inner = []
    for c in range(5):
        gu = mm(n, gu_weight((gl, gh, ul, uh), c))
        gate, up = gu[:, :128], gu[:, 128:]
        cols = slice(128 * c, 128 * c + 128)
        gate_ref[:, cols] = gate
        up_ref[:, cols] = up
        m = gate * jax.nn.sigmoid(gate) * up
        mt_ref[cols, :] = m.T.astype(bf16)
        inner.append(m.astype(bf16))
    inner = jnp.concatenate(inner, axis=1)
    for c in range(0, 8, 2):
        w = jnp.concatenate([down_weight(wd, c), down_weight(wd, c + 1)], axis=1)
        y_scr[:, 128 * c : 128 * c + 256] += mm(inner, w)

    @pl.when(step == 3)
    def _():
        y_ref[...] = (h_ref[...] + y_scr[:, :D]).astype(bf16)


def feed(mixed, u, gain, pad, gathered):
    whole = lambda *shape: pl.BlockSpec(shape, lambda j: (0,) * len(shape))
    return pl.pallas_call(
        feed_kernel,
        name="feed",
        grid=(4,),
        in_specs=[whole(D, R), whole(R, D), whole(1, D), whole(D, PADD)] + WEIGHT_SPECS,
        out_specs=[
            whole(R, D),
            whole(R, D),
            whole(PADD, R),
            pl.BlockSpec((R, 640), lambda j: (0, j)),
            pl.BlockSpec((R, 640), lambda j: (0, j)),
            pl.BlockSpec((640, R), lambda j: (j, 0)),
        ],
        out_shape=[
            jax.ShapeDtypeStruct((R, D), bf16),
            jax.ShapeDtypeStruct((R, D), f32),
            jax.ShapeDtypeStruct((PADD, R), bf16),
            jax.ShapeDtypeStruct((R, FF), f32),
            jax.ShapeDtypeStruct((R, FF), f32),
            jax.ShapeDtypeStruct((FF, R), bf16),
        ],
        scratch_shapes=[pltpu.VMEM((R, PADD), bf16), pltpu.VMEM((R, PADD), f32)],
        compiler_params=pltpu.CompilerParams(vmem_limit_bytes=48 << 20),
        cost_estimate=pl.CostEstimate(
            flops=2_200_000_000, bytes_accessed=22_000_000, transcendentals=400_000
        ),
    )(mixed, u, gain, pad, *weight_args(gathered))


def norm_back(d_out, values, gain):
    scales = lax.rsqrt(jnp.mean(values * values, axis=-1, keepdims=True) + eps)
    scaled = d_out * gain
    d_gain = jnp.sum(d_out * values * scales, axis=0, keepdims=True)
    d_values = scales * scaled - values * (scales * scales * scales) * jnp.mean(
        scaled * values, axis=-1, keepdims=True
    )
    return d_values, d_gain


def feed_back_kernel(
    c_ref, gate_ref, up_ref, h_ref, g_ref, pad_ref, o0, o1, o2, gl, gh, ul, uh, wd,
    dgate_ref, dup_ref, dh_ref, dhb_ref, dg_ref, dot_ref, cb_ref, dn_scr,
):
    step = pl.program_id(0)

    @pl.when(step == 0)
    def _():
        cb_ref[...] = jnp.zeros_like(cb_ref)
        cb_ref[:, :D] = c_ref[...].astype(bf16)
        dn_scr[...] = jnp.zeros_like(dn_scr)

    d_inner = jnp.zeros((R, 640), f32)
    for c in range(0, 8, 2):
        w = jnp.concatenate([down_weight(wd, c), down_weight(wd, c + 1)], axis=1)
        d_inner = d_inner + mm_nt(cb_ref[:, 128 * c : 128 * c + 256], w)
    for c in range(5):
        cols = slice(128 * c, 128 * c + 128)
        gate, up, dm = gate_ref[:, cols], up_ref[:, cols], d_inner[:, cols]
        sigma = jax.nn.sigmoid(gate)
        d_gate = (dm * up * sigma * (1.0 + gate * (1.0 - sigma))).astype(bf16)
        d_up = (dm * gate * sigma).astype(bf16)
        dgate_ref[:, cols] = d_gate
        dup_ref[:, cols] = d_up
        both = jnp.concatenate([d_gate, d_up], axis=1)
        dn_scr[...] += mm_nt(both, gu_weight((gl, gh, ul, uh), c))

    @pl.when(step == 3)
    def _():
        padded = dn_scr[...]
        high = padded.astype(bf16)
        low = (padded - high.astype(f32)).astype(bf16)
        dn = mm_nt(high, pad_ref[...]) + mm_nt(low, pad_ref[...])
        d_h, d_gain = norm_back(dn, h_ref[...], g_ref[...])
        d_h = c_ref[...] + d_h
        dg_ref[...] = d_gain
        dh_ref[...] = d_h
        dhb_ref[...] = jnp.zeros_like(dhb_ref)
        dhb_ref[:, :D] = d_h.astype(bf16)
        d_mixed = jnp.zeros((R, D), f32)
        for c in range(0, 8, 2):
            w = jnp.concatenate(
                [out_weight((o0, o1, o2), c), out_weight((o0, o1, o2), c + 1)], axis=1
            )
            d_mixed = d_mixed + mm_nt(dhb_ref[:, 128 * c : 128 * c + 256], w)
        dot_ref[:D, :] = d_mixed.T
        dot_ref[D:, :] = jnp.zeros((QPAD - D, R), f32)


def feed_back(cot, gate, up, hidden, gain, pad, gathered):
    whole = lambda *shape: pl.BlockSpec(shape, lambda j: (0,) * len(shape))
    block = pl.BlockSpec((R, 640), lambda j: (0, j))
    return pl.pallas_call(
        feed_back_kernel,
        name="feed_back",
        grid=(4,),
        in_specs=[whole(R, D), block, block, whole(R, D), whole(1, D), whole(D, PADD)]
        + WEIGHT_SPECS,
        out_specs=[
            block,
            block,
            whole(R, D),
            whole(R, PADD),
            whole(1, D),
            whole(QPAD, R),
            whole(R, PADD),
        ],
        out_shape=[
            jax.ShapeDtypeStruct((R, FF), bf16),
            jax.ShapeDtypeStruct((R, FF), bf16),
            jax.ShapeDtypeStruct((R, D), f32),
            jax.ShapeDtypeStruct((R, PADD), bf16),
            jax.ShapeDtypeStruct((1, D), f32),
            jax.ShapeDtypeStruct((QPAD, R), f32),
            jax.ShapeDtypeStruct((R, PADD), bf16),
        ],
        scratch_shapes=[pltpu.VMEM((R, PADD), f32)],
        compiler_params=pltpu.CompilerParams(vmem_limit_bytes=48 << 20),
        cost_estimate=pl.CostEstimate(
            flops=2_200_000_000, bytes_accessed=22_000_000, transcendentals=400_000
        ),
    )(cot, gate, up, hidden, gain, pad, *weight_args(gathered))


def attend_back_kernel(
    qt_ref, kv_ref, bias_ref, dot_ref, mixed_ref, lse_ref, dkv_ref, dqt_ref
):
    q = heads_wide(qt_ref, True)
    d_o = heads_wide(dot_ref, False)
    o = heads_wide(mixed_ref, False)
    delta = jnp.sum(d_o * o.astype(f32), axis=0, keepdims=True)
    d_o = d_o.astype(bf16)
    lse = lse_ref[0]
    both = jnp.concatenate([q, d_o], axis=1)
    acc = jnp.zeros((128, GRP * R), f32)
    for i in range(KEYS // CHUNK):
        rows = slice(CHUNK * i, CHUNK * i + CHUNK)
        b = bias_ref[rows, :]
        kv = kv_ref[rows, :]
        p = jnp.exp(mm(kv, q) + jnp.concatenate([b, b, b], axis=1) - lse)
        ds = (p * (mm(kv, d_o) - delta)).astype(bf16)
        dkv_ref[rows, :] = mm_nt(jnp.concatenate([ds, p.astype(bf16)], axis=1), both).astype(bf16)
        acc = acc + mm(kv.T, ds)
    acc = acc[:64] * 0.125
    for h in range(GRP):
        dqt_ref[64 * h : 64 * h + 64, :] = acc[:, 128 * h : 128 * h + 128]


def attend_back(qt, kv_all, bias, d_mixed, mixed, lse):
    heads = pl.BlockSpec((GRP * HD, R), lambda g: (g, 0))
    return pl.pallas_call(
        attend_back_kernel,
        name="attend_back",
        grid=(SIDE,),
        in_specs=[
            heads,
            pl.BlockSpec((KEYS, 128), lambda g: (0, g)),
            pl.BlockSpec((KEYS, R), lambda g: (0, 0)),
            heads,
            heads,
            pl.BlockSpec((1, 1, GRP * R), lambda g: (g, 0, 0)),
        ],
        out_specs=[pl.BlockSpec((KEYS, 128), lambda g: (0, g)), heads],
        out_shape=[
            jax.ShapeDtypeStruct((KEYS, SIDE * 128), bf16),
            jax.ShapeDtypeStruct((QSIDE, R), f32),
        ],
        compiler_params=pltpu.CompilerParams(vmem_limit_bytes=48 << 20),
        cost_estimate=pl.CostEstimate(
            flops=10_000_000_000, bytes_accessed=14_000_000, transcendentals=7_900_000
        ),
    )(qt, kv_all, bias, d_mixed, mixed, lse)


def project_back_kernel(
    dqt_ref, dkv_ref, cos_ref, sin_ref, u_ref, g_ref, dh_ref, w_ref,
    du_ref, dqkv_ref, at_ref, dg_ref,
):
    cos, sin = cos_ref[...], sin_ref[...]
    lane = lane_of((R, 128))
    dkv = [dkv_ref[:, 128 * g : 128 * g + 128] for g in range(KVH)]
    rolled = [pltpu.roll(b, 64, 1) for b in dkv]
    zero = jnp.zeros((R, 128), f32)
    blocks = [dqt_ref[128 * c : 128 * c + 128, :].T for c in range(7)]
    last = jnp.concatenate([dqt_ref[896:960, :], jnp.zeros((64, R), f32)], axis=0).T
    low = lane < 64
    blocks.append(jnp.where(low, last, rolled[0]))
    blocks.append(jnp.where(low, dkv[1], rolled[2]))
    blocks.append(jnp.where(low, dkv[3], rolled[4]))
    blocks = [b * cos - half_swapped(b) * sin for b in blocks]
    blocks.append(jnp.where(low, rolled[0], dkv[1]))
    blocks.append(jnp.where(low, rolled[2], dkv[3]))
    blocks.append(jnp.where(low, rolled[4], zero))
    da = jnp.zeros((R, D), f32)
    for c in range(0, 13, 2):
        if c + 1 < 13:
            d = jnp.concatenate([blocks[c], blocks[c + 1]], axis=1).astype(bf16)
            w = jnp.concatenate([qkv_weight(w_ref, c), qkv_weight(w_ref, c + 1)], axis=1)
        else:
            d, w = blocks[c].astype(bf16), qkv_weight(w_ref, c)
        dqkv_ref[:, 128 * c : 128 * c + d.shape[1]] = d
        da = da + mm_nt(d, w)
    u = u_ref[...].astype(f32)
    gain = g_ref[...]
    _, a = normed_of(u, gain)
    at_ref[...] = a.T
    d_u, d_gain = norm_back(da, u, gain)
    dg_ref[...] = d_gain
    du_ref[...] = dh_ref[...] + d_u


def project_back(d_query, d_kv, cos, sin, u, gain, d_hidden, weights):
    whole = lambda *shape: pl.BlockSpec(shape, lambda j: (0,) * len(shape))
    return pl.pallas_call(
        project_back_kernel,
        name="project_back",
        grid=(1,),
        in_specs=[
            whole(D, R),
            whole(R, 640),
            whole(R, 128),
            whole(R, 128),
            whole(R, D),
            whole(1, D),
            whole(R, D),
            whole(10, ROWS, 128),
        ],
        out_specs=[whole(R, D), whole(R, 13 * 128), whole(D, R), whole(1, D)],
        out_shape=[
            jax.ShapeDtypeStruct((R, D), f32),
            jax.ShapeDtypeStruct((R, 13 * 128), bf16),
            jax.ShapeDtypeStruct((D, R), bf16),
            jax.ShapeDtypeStruct((1, D), f32),
        ],
        compiler_params=pltpu.CompilerParams(vmem_limit_bytes=48 << 20),
        cost_estimate=pl.CostEstimate(flops=400_000_000, bytes_accessed=5_000_000, transcendentals=0),
    )(d_query, d_kv, cos, sin, u, gain, d_hidden, weights)


def outer_kernel(
    place_ref, slot_ref, at_ref, dqkv_ref, mixed_ref, dhb_ref, nt_ref, dgate_ref, dup_ref, mt_ref,
    cb_ref, gain_ref, out_ref,
):
    step = pl.program_id(0)

    def row_of(k, count, at):
        row = lax.broadcasted_iota(jnp.int32, (count, 128), 0)
        return jnp.where(row == at, gain_ref[pl.ds(4 * step + k, 1), :], 0.0)

    def narrow(start, ks):
        count = len(ks)
        rows = at_ref[pl.ds(pl.multiple_of(start, 32), 96 * count), :]
        for c in range(0, 13, 2):
            width = min(256, 1664 - 128 * c)
            res = mm(rows, dqkv_ref[:, 128 * c : 128 * c + width])
            for i, k in enumerate(ks):
                for h in range(width // 128):
                    out_ref[0, slot_ref[k], 96 * (c + h) : 96 * (c + h) + 96, :] = res[
                        96 * i : 96 * i + 96, 128 * h : 128 * h + 128
                    ].astype(bf16)
        for k in ks:
            out_ref[0, slot_ref[k], 1248:1280, :] = row_of(k, 32, 0).astype(bf16)

    def wide(ref, start, cot_ref, ks):
        rows = ref[pl.ds(pl.multiple_of(start, 32), 160 * len(ks)), :]
        for c in range(0, 8, 2):
            res = mm(rows, cot_ref[:, 128 * c : 128 * c + 256])
            for i, k in enumerate(ks):
                for h in range(2):
                    b = res[160 * i : 160 * i + 160, 128 * h : 128 * h + 128]
                    if c + h == 7:
                        b = b + row_of(k, 160, 0)
                    at = 160 * (c + h)
                    out_ref[0, slot_ref[k], at : at + 160, :] = b.astype(bf16)

    @pl.when(step < 2)
    def _():
        narrow(384 * step, (0, 1, 2, 3))

    @pl.when(step == 2)
    def _():
        narrow(768, (0, 1))
        wide(mixed_ref, 0, dhb_ref, (2, 3))

    @pl.when(step == 3)
    def _():
        wide(mixed_ref, 320, dhb_ref, (0, 1, 2, 3))

    @pl.when((step >= 4) & (step < 12))
    def _():
        rows = nt_ref[pl.ds(pl.multiple_of(128 * (step - 4), 128), 128), :]
        for part, ref in enumerate((dgate_ref, dup_ref)):
            for c in range(0, 20, 2):
                res = mm(rows, ref[:, 128 * c : 128 * c + 256])
                for k in range(4):
                    for h in range(2):
                        b = res[32 * k : 32 * k + 32, 128 * h : 128 * h + 128]
                        at = 32 * (20 * part + c + h)
                        if at == 0:
                            b = b + row_of(k, 32, 30)
                        out_ref[0, slot_ref[k], at : at + 32, :] = b.astype(bf16)

    @pl.when(step >= 12)
    def _():
        wide(mt_ref, 640 * (step - 12), cb_ref, (0, 1, 2, 3))


def outer(places, slots, at, dqkv, mixed, dhb, nt, dgate, dup, mt, cb, gains):
    whole = lambda v: pl.BlockSpec(v.shape, lambda s, place, slot: (0,) * v.ndim)
    args = (at, dqkv, mixed, dhb, nt, dgate, dup, mt, cb, gains)
    return pl.pallas_call(
        outer_kernel,
        name="outer",
        grid_spec=pltpu.PrefetchScalarGridSpec(
            num_scalar_prefetch=2,
            grid=(16,),
            in_specs=[whole(v) for v in args],
            out_specs=pl.BlockSpec((1, 4, ROWS, 128), lambda s, place, slot: (place[s], 0, 0, 0)),
        ),
        out_shape=jax.ShapeDtypeStruct((16, 4, ROWS, 128), bf16),
        compiler_params=pltpu.CompilerParams(vmem_limit_bytes=48 << 20),
        cost_estimate=pl.CostEstimate(
            flops=2_600_000_000, bytes_accessed=24_000_000, transcendentals=0
        ),
    )(places, slots, *args)


def shard_kind(rank):
    return jnp.where(rank < 10, 0, jnp.where((rank >= 16) & (rank < 48), 2, 1))


def shard_blocks(flat, gains, rank):
    g = jnp.zeros((1, 128), bf16).at[0, :30].set(gains)

    def narrow(_):
        w = jnp.pad(flat.reshape(96, 1600), ((0, 0), (0, 64)))
        w = w.reshape(96, 13, 128).transpose(1, 0, 2).reshape(1248, 128)
        return jnp.concatenate([w, jnp.pad(g, ((0, 31), (0, 0)))])

    def square(_):
        w = jnp.pad(flat.reshape(160, 960), ((0, 0), (0, 64)))
        w = w.reshape(160, 8, 128).transpose(1, 0, 2)
        last = jnp.concatenate([jnp.zeros((1, 64), bf16), g[:, :64]], axis=1)
        return w.at[7, 0].add(last[0]).reshape(ROWS, 128)

    def broad(_):
        w = jnp.pad(flat.reshape(30, 40, 128), ((0, 2), (0, 0), (0, 0))).transpose(1, 0, 2)
        return w.at[0, 30].set(g[0]).reshape(ROWS, 128)

    return lax.switch(shard_kind(rank), [narrow, square, broad], 0)


def blocks_shard(blocks, rank):
    def narrow(_):
        w = blocks[:1248].reshape(13, 96, 128).transpose(1, 0, 2).reshape(96, 1664)[:, :1600]
        return w.reshape(SHARD), blocks[1248, :30]

    def square(_):
        w = blocks.reshape(8, 160, 128).transpose(1, 0, 2).reshape(160, 1024)[:, :960]
        return w.reshape(SHARD), blocks[1120, 64:94]

    def broad(_):
        w = blocks.reshape(40, 32, 128).transpose(1, 0, 2)[:30]
        return w.reshape(SHARD), blocks[30, :30]

    return lax.switch(shard_kind(rank), [narrow, square, broad], 0)


def gathered_gains(gathered):
    rows = jnp.concatenate(
        [
            gathered[:10, 1248, :30],
            gathered[10:16, 1120, 64:94],
            gathered[16:48, 30, :30],
            gathered[48:, 1120, 64:94],
        ]
    ).astype(f32)
    flat = rows.reshape(1, 2 * D)
    return flat[:, :D], flat[:, D:]


def per_device(layer_in, out_grad, segment_ids, block_pair, params, norm_gains):
    phase = lax.axis_index("phase")
    ctx = lax.axis_index("ctx")
    rank = ctx * 2 + lax.axis_index("fsdp")
    y, x, z = rank // 16, (rank // 4) % 4, rank % 4
    zh = z // 2

    own = shard_blocks(params[0], norm_gains[0], rank)
    gathered = lax.all_gather(own, ("ctx", "fsdp"), axis=0)

    seg_row = segment_ids[0]
    pair = lax.dynamic_index_in_dim(block_pair, ctx, 0, keepdims=False)
    within = jnp.arange(HD, dtype=jnp.int32)
    place_q = jnp.concatenate([pair * 64 + within, (63 - pair) * 64 + within])
    seg_q = jnp.concatenate(
        [
            lax.dynamic_slice_in_dim(seg_row, pair * 64, 64),
            lax.dynamic_slice_in_dim(seg_row, (63 - pair) * 64, 64),
        ]
    )
    start_q = jnp.sum((seg_row[:, None] < seg_q[None, :]).astype(jnp.int32), axis=0)
    pairs_k = block_pair[key_order(y, x, zh, phase)]
    place_k = (
        jnp.stack([pairs_k, 63 - pairs_k], axis=1)[:, :, None] * 64 + within[None, None, :]
    ).reshape(KEYS)
    bias = jnp.where(
        (place_k[:, None] <= place_q[None, :]) & (place_k[:, None] >= start_q[None, :]),
        0.0,
        masked_fill,
    ).astype(f32)
    frequency = rope_theta ** (-2.0 * jnp.arange(HD // 2, dtype=f32) / HD)
    angles = (place_q - start_q).astype(f32)[:, None] * frequency[None, :]
    cosine, sine = jnp.cos(angles), jnp.sin(angles)
    cos = jnp.concatenate([cosine] * 4, axis=1)
    sin = jnp.concatenate([-sine, sine, -sine, sine], axis=1)
    spread = jnp.arange(PADD, dtype=jnp.int32)
    target = jnp.where(spread % 32 < 30, (spread // 32) * 30 + spread % 32, -1)
    pad = (jnp.arange(D, dtype=jnp.int32)[:, None] == target[None, :]).astype(bf16)

    gain_one, gain_two = gathered_gains(gathered)
    first = phase == 0

    u = layer_in[0]
    mixed = None
    kept = []
    for tick in range(2):
        active = phase == tick
        qt, kv = project(u, gain_one, cos, sin, gathered)
        kv_side = jnp.where(active, kv[:, :384], over(kv[:, 384:], tick))
        qt_side = jnp.where(active, qt[:QSIDE], over(qt[QSIDE:], tick))
        kv_all = gather_keys(kv_side)
        mixed_side, lse = attend(qt_side, kv_all, bias)
        kept.append((qt_side, kv_all, mixed_side, lse))
        far = over(mixed_side[: D - QSIDE], 1 - tick)
        whole = jnp.concatenate([mixed_side, far])
        mixed = whole if tick == 0 else jnp.where(active, whole, mixed)
        result, hidden, nt, gate, up, mt = feed(mixed, u, gain_two, pad, gathered)
        if tick == 0:
            u = jnp.where(first, u, over(result, 0))

    cot = out_grad[0]
    d_query = d_kv = None
    for tick in range(2):
        layer = 1 - tick
        active = phase == layer
        qt_side, kv_all, mixed_side, lse = kept[layer]
        dgate, dup, dh, dhb, dg_two, d_mixed, cb = feed_back(
            cot, gate, up, hidden, gain_two, pad, gathered
        )
        d_side = jnp.where(active, d_mixed[:QSIDE], over(d_mixed[QSIDE:], layer))
        d_kv_all, dq_side = attend_back(qt_side, kv_all, bias, d_side, mixed_side, lse)
        dq_new = jnp.concatenate([dq_side, over(dq_side[: D - QSIDE], tick)])
        dkv_side = scatter_keys(d_kv_all)
        dkv_new = jnp.concatenate([dkv_side, over(dkv_side[:, :256], tick)], axis=1)
        d_query = dq_new if tick == 0 else jnp.where(active, dq_new, d_query)
        d_kv = dkv_new if tick == 0 else jnp.where(active, dkv_new, d_kv)
        d_u, dqkv, at, dg_one = project_back(
            d_query, d_kv, cos, sin, u, gain_one, dh, gathered
        )
        if tick == 0:
            cot = jnp.where(first, over(d_u.astype(bf16), 1).astype(f32), cot)

    gains = jnp.concatenate([dg_one, dg_two], axis=1).reshape(SHARDS, 30)
    shards = jnp.arange(SHARDS, dtype=jnp.int32)
    square = (((shards >= 10) & (shards < 16)) | (shards >= 48))[:, None]
    gains = jnp.where(
        square, jnp.pad(gains, ((0, 0), (64, 34))), jnp.pad(gains, ((0, 0), (0, 98)))
    )
    four = jnp.arange(4, dtype=jnp.int32)
    slots_y, slots_x, slots_z = (slot_of(four ^ at_axis, phase) for at_axis in (y, x, z))
    places = (slots_y[:, None] * 4 + slots_x[None, :]).reshape(16)
    grads = outer(places, slots_z, at, dqkv, mixed, dhb, nt, dgate, dup, mt, cb, gains)
    total = scatter_grads(grads.reshape(4, 4, 4, ROWS, 128))
    param_part, gain_part = blocks_shard(total, rank)
    return (result[None, None], d_u[None, None], param_part[None], gain_part[None])


def solution(mesh):
    return jax.shard_map(
        per_device,
        mesh=mesh,
        in_specs=(
            P("fsdp", "ctx", None),
            P("fsdp", "ctx", None),
            P("fsdp", None),
            P(),
            P("phase", ("ctx", "fsdp")),
            P("phase", ("ctx", "fsdp")),
        ),
        out_specs=(
            P("phase", "fsdp", "ctx", None),
            P("phase", "fsdp", "ctx", None),
            P("phase", ("ctx", "fsdp")),
            P("phase", ("ctx", "fsdp")),
        ),
        check_vma=False,
    )
```

```python
import functools

import jax
import jax.numpy as jnp
from jax import lax
from jax.experimental import pallas as pl
from jax.experimental.pallas import tpu as pltpu
from jax.sharding import PartitionSpec as P

H = 15
KVH = 5
HD = 64
D = 960
FF = 2560
GRP = H // KVH
R = 128
SHARDS = 64
SHARD = 153600
ROWS = 1280
KEYS = 4096
CHUNK = 512
PADD = 1024
SIDE = 3
QSIDE = SIDE * GRP * HD
QPAD = 2 * QSIDE

eps = 1e-05
rope_theta = 100000.0
masked_fill = -1e30
f32 = jnp.float32
bf16 = jnp.bfloat16
ALL = ("phase", "ctx", "fsdp")

NT = (((1,), (1,)), ((), ()))


def mm(a, b):
    return jnp.dot(a, b, preferred_element_type=f32)


def mm_nt(a, b):
    return lax.dot_general(a, b, NT, preferred_element_type=f32)


STEPS = ((1, 3), (3, 1))


def swapped(block, way):
    pairs = []
    for p in range(2):
        dy, dx, dz = way(p)
        for y in range(4):
            for x in range(4):
                for z in range(4):
                    to = ((y ^ dy) * 4 + (x ^ dx)) * 4 + (z ^ dz)
                    pairs.append((p * 64 + (y * 4 + x) * 4 + z, p * 64 + to))
    return lax.ppermute(block, ALL, pairs)


def over(block, source):
    return lax.ppermute(block, "phase", [(source, 1 - source)])


def along(axes, number):
    def way(p):
        shift = [0, 0, 0]
        shift[axes[p]] = STEPS[p][number]
        return tuple(shift)

    return way


def far_z(p):
    return (0, 0, 2)


def gather_keys(kv):
    tail = kv.shape
    far = swapped(kv, far_z)
    near = kv
    orders = (((0, 1), (1, 0)), ((1, 0), (0, 1)))
    blocks = [near[None], far[None]]
    for leg in range(2):
        for number in range(2):
            if leg and number:
                blocks = list(lax.optimization_barrier(tuple(blocks)))
            for k in range(2):
                got = swapped(blocks[k], along(orders[k][leg], number))
                blocks[k] = jnp.concatenate([blocks[k], got], axis=0)
    return jnp.concatenate(blocks, axis=0).reshape(KEYS, tail[1])


def scatter_keys(d_kv):
    parts = d_kv.reshape(2, 16, R, d_kv.shape[1])
    orders = (((0, 1), (1, 0)), ((1, 0), (0, 1)))
    blocks = [parts[0], parts[1]]
    for leg in (1, 0):
        for number in (1, 0):
            for k in (1, 0):
                half = blocks[k].shape[0] // 2
                got = swapped(blocks[k][half:], along(orders[k][leg], number))
                total = blocks[k][:half].astype(f32) + got.astype(f32)
                last = k == 0 and half == 1
                blocks[k] = total if last else total.astype(bf16)
    return blocks[0][0] + swapped(blocks[1][0], far_z).astype(f32)


def slot_offsets(phase):
    return jnp.where(phase == 0, jnp.array([0, 1, 3, 2]), jnp.array([0, 3, 1, 2]))


def slot_of(offset, phase):
    at = jnp.where(phase == 0, jnp.array([0, 1, 3, 2]), jnp.array([0, 2, 3, 1]))
    return at[offset]


def key_order(y, x, zh, phase):
    off = slot_offsets(phase)
    outer = jnp.repeat(off, 4)
    inner = jnp.tile(off, 4)
    out = []
    for k in range(2):
        first_y = phase == k
        oy = jnp.where(first_y, inner, outer)
        ox = jnp.where(first_y, outer, inner)
        out.append((y ^ oy) * 8 + (x ^ ox) * 2 + (zh ^ k))
    return jnp.concatenate(out)


PART_ROWS = ((0, 432), (432, 864), (864, 1280))


PART_AXES = ((0, 1, 2), (1, 2, 0), (2, 0, 1))


def scatter_grads(keep, send):
    keep, send = list(keep), list(send)
    for leg in range(3):
        for number in (1, 0):
            for part, axes in enumerate(PART_AXES):
                axis = axes[leg]
                got = swapped(send[part], along((axis, axis), number))
                mine = keep[part]

                def total(at, mine=mine, got=got):
                    return mine[at].astype(f32) + got[at].astype(f32)

                if number:
                    keep[part] = total(0).astype(bf16)
                    send[part] = total(1).astype(bf16)
                elif leg < 2:
                    keep[part] = total(slice(0, 2)).astype(bf16)
                    send[part] = total(slice(2, 4)).astype(bf16)
                else:
                    keep[part] = total(slice(None))
    return jnp.concatenate(keep)


def lane_of(shape):
    return lax.broadcasted_iota(jnp.int32, shape, len(shape) - 1)


def half_swapped(block):
    lane = lane_of(block.shape)
    return jnp.where(lane % HD < HD // 2, pltpu.roll(block, 96, 1), pltpu.roll(block, 32, 1))


def qkv_weight(w_ref, c):
    return w_ref[:, 96 * c : 96 * c + 96, :].reshape(D, 128)


def normed_of(u, gain):
    scale = lax.rsqrt(jnp.mean(u * u, axis=-1, keepdims=True) + eps)
    return scale, (u * scale * gain).astype(bf16)


def project_kernel(u_ref, g_ref, cos_ref, sin_ref, w_ref, qt_ref, kv_ref):
    u = u_ref[...].astype(f32)
    _, a = normed_of(u, g_ref[...])
    cos, sin = cos_ref[...], sin_ref[...]
    blocks = []
    for c in range(0, 13, 2):
        if c + 1 < 13:
            w = jnp.concatenate([qkv_weight(w_ref, c), qkv_weight(w_ref, c + 1)], axis=1)
        else:
            w = qkv_weight(w_ref, c)
        y = mm(a, w)
        for k in range(w.shape[1] // 128):
            b = y[:, 128 * k : 128 * k + 128]
            if c + k < 10:
                b = b * cos + half_swapped(b) * sin
            blocks.append(b)
    for c in range(8):
        t = (blocks[c].astype(bf16).astype(f32) * 0.125).T.astype(bf16)
        count = 128 if c < 7 else 64
        qt_ref[128 * c : 128 * c + count, :] = t[:count]
    qt_ref[D:, :] = jnp.zeros((QPAD - D, R), bf16)
    kv_ref[:, 640:] = jnp.zeros((R, 128), bf16)
    lane = lane_of((R, 128))
    for g in range(KVH):
        k, v = blocks[(15 + g) // 2], blocks[(20 + g) // 2]
        if (15 + g) % 2:
            k = pltpu.roll(k, 64, 1)
        if (20 + g) % 2 == 0:
            v = pltpu.roll(v, 64, 1)
        kv_ref[:, 128 * g : 128 * g + 128] = jnp.where(lane < 64, k, v).astype(bf16)


def project(u, gain, cos, sin, weights):
    return pl.pallas_call(
        project_kernel,
        name="project",
        grid=(1,),
        in_specs=[
            pl.BlockSpec((R, D), lambda i: (0, 0)),
            pl.BlockSpec((1, D), lambda i: (0, 0)),
            pl.BlockSpec((R, 128), lambda i: (0, 0)),
            pl.BlockSpec((R, 128), lambda i: (0, 0)),
            pl.BlockSpec((10, ROWS, 128), lambda i: (0, 0, 0)),
        ],
        out_specs=[
            pl.BlockSpec((QPAD, R), lambda i: (0, 0)),
            pl.BlockSpec((R, 768), lambda i: (0, 0)),
        ],
        out_shape=[
            jax.ShapeDtypeStruct((QPAD, R), bf16),
            jax.ShapeDtypeStruct((R, 768), bf16),
        ],
        compiler_params=pltpu.CompilerParams(vmem_limit_bytes=48 << 20),
        cost_estimate=pl.CostEstimate(flops=400_000_000, bytes_accessed=4_000_000, transcendentals=0),
    )(u, gain, cos, sin, weights)


def heads_wide(ref, low):
    top = jnp.concatenate([ref[64 * h : 64 * h + 64, :] for h in range(GRP)], axis=1)
    zero = jnp.zeros_like(top)
    return jnp.concatenate([top, zero] if low else [zero, top], axis=0)


def attend_kernel(qt_ref, kv_ref, bias_ref, mixed_ref, lse_ref, s_ref):
    q = heads_wide(qt_ref, True)
    peak = jnp.full((1, GRP * R), masked_fill, f32)
    for i in range(KEYS // CHUNK):
        rows = slice(CHUNK * i, CHUNK * i + CHUNK)
        b = bias_ref[rows, :]
        s = mm(kv_ref[rows, :], q) + jnp.concatenate([b, b, b], axis=1)
        s_ref[rows, :] = s
        peak = jnp.maximum(peak, jnp.max(s, axis=0, keepdims=True))
    total = jnp.zeros((1, GRP * R), f32)
    acc = jnp.zeros((128, GRP * R), f32)
    for i in range(KEYS // CHUNK):
        rows = slice(CHUNK * i, CHUNK * i + CHUNK)
        p = jnp.exp(s_ref[rows, :] - peak)
        total = total + jnp.sum(p, axis=0, keepdims=True)
        acc = acc + mm(kv_ref[rows, :].T, p.astype(bf16))
    lse_ref[0] = peak + jnp.log(total)
    o = (acc[64:] / total).astype(bf16)
    for h in range(GRP):
        mixed_ref[64 * h : 64 * h + 64, :] = o[:, 128 * h : 128 * h + 128]


def attend(qt, kv_all, bias):
    return pl.pallas_call(
        attend_kernel,
        name="attend",
        grid=(SIDE,),
        in_specs=[
            pl.BlockSpec((GRP * HD, R), lambda g: (g, 0)),
            pl.BlockSpec((KEYS, 128), lambda g: (0, g)),
            pl.BlockSpec((KEYS, R), lambda g: (0, 0)),
        ],
        out_specs=[
            pl.BlockSpec((GRP * HD, R), lambda g: (g, 0)),
            pl.BlockSpec((1, 1, GRP * R), lambda g: (g, 0, 0)),
        ],
        out_shape=[
            jax.ShapeDtypeStruct((QSIDE, R), bf16),
            jax.ShapeDtypeStruct((SIDE, 1, GRP * R), f32),
        ],
        scratch_shapes=[pltpu.VMEM((KEYS, GRP * R), f32)],
        compiler_params=pltpu.CompilerParams(vmem_limit_bytes=48 << 20),
        cost_estimate=pl.CostEstimate(
            flops=4_000_000_000, bytes_accessed=8_000_000, transcendentals=7_900_000
        ),
    )(qt, kv_all, bias)


def out_weight(refs, c):
    return jnp.concatenate(
        [ref[:, 160 * c : 160 * c + 160, :].reshape(320, 128) for ref in refs], axis=0
    )


def gu_weight(refs, c):
    gl, gh, ul, uh = refs
    gate = jnp.concatenate([gl[:, c].reshape(512, 128), gh[:, c].reshape(512, 128)], axis=0)
    up = jnp.concatenate([ul[:, c].reshape(512, 128), uh[:, c].reshape(512, 128)], axis=0)
    return jnp.concatenate([gate, up], axis=1)


def down_weight(ref, c):
    return ref[:, 160 * c : 160 * c + 160, :].reshape(640, 128)


WEIGHT_SPECS = (
    [pl.BlockSpec((2, ROWS, 128), lambda j, k=k: (5 + k, 0, 0)) for k in range(3)]
    + [
        pl.BlockSpec((16, 5, 32, 128), lambda j, d=d, o=o: (1 + d, o + j, 0, 0))
        for o in (0, 4)
        for d in (0, 1)
    ]
    + [pl.BlockSpec((4, ROWS, 128), lambda j: (12 + j, 0, 0))]
)


def weight_args(gathered):
    fine = gathered.reshape(SHARDS, 40, 32, 128)
    return [gathered] * 3 + [fine] * 4 + [gathered]


def feed_kernel(
    mixed_ref, u_ref, g_ref, pad_ref, o0, o1, o2, gl, gh, ul, uh, wd,
    y_ref, h_ref, nt_ref, gate_ref, up_ref, mt_ref, n_scr, y_scr,
):
    step = pl.program_id(0)

    @pl.when(step == 0)
    def _():
        mixed = mixed_ref[...].T
        for c in range(0, 8, 2):
            w = jnp.concatenate(
                [out_weight((o0, o1, o2), c), out_weight((o0, o1, o2), c + 1)], axis=1
            )
            y = mm(mixed, w)
            end = min(128 * c + 256, D)
            h_ref[:, 128 * c : end] = u_ref[:, 128 * c : end].astype(f32) + y[:, : end - 128 * c]
        _, n = normed_of(h_ref[...], g_ref[...])
        padded = mm(n, pad_ref[...])
        n_scr[...] = padded.astype(bf16)
        nt_ref[...] = padded.T.astype(bf16)
        y_scr[...] = jnp.zeros_like(y_scr)

    n = n_scr[...]
    inner = []
    for c in range(5):
        gu = mm(n, gu_weight((gl, gh, ul, uh), c))
        gate, up = gu[:, :128], gu[:, 128:]
        cols = slice(128 * c, 128 * c + 128)
        gate_ref[:, cols] = gate
        up_ref[:, cols] = up
        m = gate * jax.nn.sigmoid(gate) * up
        mt_ref[cols, :] = m.T.astype(bf16)
        inner.append(m.astype(bf16))
    inner = jnp.concatenate(inner, axis=1)
    for c in range(0, 8, 2):
        w = jnp.concatenate([down_weight(wd, c), down_weight(wd, c + 1)], axis=1)
        y_scr[:, 128 * c : 128 * c + 256] += mm(inner, w)

    @pl.when(step == 3)
    def _():
        y_ref[...] = (h_ref[...] + y_scr[:, :D]).astype(bf16)


def feed(mixed, u, gain, pad, gathered):
    whole = lambda *shape: pl.BlockSpec(shape, lambda j: (0,) * len(shape))
    return pl.pallas_call(
        feed_kernel,
        name="feed",
        grid=(4,),
        in_specs=[whole(D, R), whole(R, D), whole(1, D), whole(D, PADD)] + WEIGHT_SPECS,
        out_specs=[
            whole(R, D),
            whole(R, D),
            whole(PADD, R),
            pl.BlockSpec((R, 640), lambda j: (0, j)),
            pl.BlockSpec((R, 640), lambda j: (0, j)),
            pl.BlockSpec((640, R), lambda j: (j, 0)),
        ],
        out_shape=[
            jax.ShapeDtypeStruct((R, D), bf16),
            jax.ShapeDtypeStruct((R, D), f32),
            jax.ShapeDtypeStruct((PADD, R), bf16),
            jax.ShapeDtypeStruct((R, FF), f32),
            jax.ShapeDtypeStruct((R, FF), f32),
            jax.ShapeDtypeStruct((FF, R), bf16),
        ],
        scratch_shapes=[pltpu.VMEM((R, PADD), bf16), pltpu.VMEM((R, PADD), f32)],
        compiler_params=pltpu.CompilerParams(vmem_limit_bytes=48 << 20),
        cost_estimate=pl.CostEstimate(
            flops=2_200_000_000, bytes_accessed=22_000_000, transcendentals=400_000
        ),
    )(mixed, u, gain, pad, *weight_args(gathered))


def norm_back(d_out, values, gain):
    scales = lax.rsqrt(jnp.mean(values * values, axis=-1, keepdims=True) + eps)
    scaled = d_out * gain
    d_gain = jnp.sum(d_out * values * scales, axis=0, keepdims=True)
    d_values = scales * scaled - values * (scales * scales * scales) * jnp.mean(
        scaled * values, axis=-1, keepdims=True
    )
    return d_values, d_gain


def feed_back_kernel(
    c_ref, gate_ref, up_ref, h_ref, g_ref, pad_ref, o0, o1, o2, gl, gh, ul, uh, wd,
    dgate_ref, dup_ref, dh_ref, dhb_ref, dg_ref, dot_ref, cb_ref, dn_scr,
):
    step = pl.program_id(0)

    @pl.when(step == 0)
    def _():
        cb_ref[...] = jnp.zeros_like(cb_ref)
        cb_ref[:, :D] = c_ref[...].astype(bf16)
        dn_scr[...] = jnp.zeros_like(dn_scr)

    d_inner = jnp.zeros((R, 640), f32)
    for c in range(0, 8, 2):
        w = jnp.concatenate([down_weight(wd, c), down_weight(wd, c + 1)], axis=1)
        d_inner = d_inner + mm_nt(cb_ref[:, 128 * c : 128 * c + 256], w)
    for c in range(5):
        cols = slice(128 * c, 128 * c + 128)
        gate, up, dm = gate_ref[:, cols], up_ref[:, cols], d_inner[:, cols]
        sigma = jax.nn.sigmoid(gate)
        d_gate = (dm * up * sigma * (1.0 + gate * (1.0 - sigma))).astype(bf16)
        d_up = (dm * gate * sigma).astype(bf16)
        dgate_ref[:, cols] = d_gate
        dup_ref[:, cols] = d_up
        both = jnp.concatenate([d_gate, d_up], axis=1)
        dn_scr[...] += mm_nt(both, gu_weight((gl, gh, ul, uh), c))

    @pl.when(step == 3)
    def _():
        padded = dn_scr[...]
        high = padded.astype(bf16)
        low = (padded - high.astype(f32)).astype(bf16)
        dn = mm_nt(high, pad_ref[...]) + mm_nt(low, pad_ref[...])
        d_h, d_gain = norm_back(dn, h_ref[...], g_ref[...])
        d_h = c_ref[...] + d_h
        dg_ref[...] = d_gain
        dh_ref[...] = d_h
        dhb_ref[...] = jnp.zeros_like(dhb_ref)
        dhb_ref[:, :D] = d_h.astype(bf16)
        d_mixed = jnp.zeros((R, D), f32)
        for c in range(0, 8, 2):
            w = jnp.concatenate(
                [out_weight((o0, o1, o2), c), out_weight((o0, o1, o2), c + 1)], axis=1
            )
            d_mixed = d_mixed + mm_nt(dhb_ref[:, 128 * c : 128 * c + 256], w)
        dot_ref[:D, :] = d_mixed.T
        dot_ref[D:, :] = jnp.zeros((QPAD - D, R), f32)


def feed_back(cot, gate, up, hidden, gain, pad, gathered):
    whole = lambda *shape: pl.BlockSpec(shape, lambda j: (0,) * len(shape))
    block = pl.BlockSpec((R, 640), lambda j: (0, j))
    return pl.pallas_call(
        feed_back_kernel,
        name="feed_back",
        grid=(4,),
        in_specs=[whole(R, D), block, block, whole(R, D), whole(1, D), whole(D, PADD)]
        + WEIGHT_SPECS,
        out_specs=[
            block,
            block,
            whole(R, D),
            whole(R, PADD),
            whole(1, D),
            whole(QPAD, R),
            whole(R, PADD),
        ],
        out_shape=[
            jax.ShapeDtypeStruct((R, FF), bf16),
            jax.ShapeDtypeStruct((R, FF), bf16),
            jax.ShapeDtypeStruct((R, D), f32),
            jax.ShapeDtypeStruct((R, PADD), bf16),
            jax.ShapeDtypeStruct((1, D), f32),
            jax.ShapeDtypeStruct((QPAD, R), f32),
            jax.ShapeDtypeStruct((R, PADD), bf16),
        ],
        scratch_shapes=[pltpu.VMEM((R, PADD), f32)],
        compiler_params=pltpu.CompilerParams(vmem_limit_bytes=48 << 20),
        cost_estimate=pl.CostEstimate(
            flops=2_200_000_000, bytes_accessed=22_000_000, transcendentals=400_000
        ),
    )(cot, gate, up, hidden, gain, pad, *weight_args(gathered))


def attend_back_kernel(
    qt_ref, kv_ref, bias_ref, dot_ref, mixed_ref, lse_ref, dkv_ref, dqt_ref
):
    q = heads_wide(qt_ref, True)
    d_o = heads_wide(dot_ref, False)
    o = heads_wide(mixed_ref, False)
    delta = jnp.sum(d_o * o.astype(f32), axis=0, keepdims=True)
    d_o = d_o.astype(bf16)
    lse = lse_ref[0]
    both = jnp.concatenate([q, d_o], axis=1)
    acc = jnp.zeros((128, GRP * R), f32)
    for i in range(KEYS // CHUNK):
        rows = slice(CHUNK * i, CHUNK * i + CHUNK)
        b = bias_ref[rows, :]
        kv = kv_ref[rows, :]
        p = jnp.exp(mm(kv, q) + jnp.concatenate([b, b, b], axis=1) - lse)
        ds = (p * (mm(kv, d_o) - delta)).astype(bf16)
        dkv_ref[rows, :] = mm_nt(jnp.concatenate([ds, p.astype(bf16)], axis=1), both).astype(bf16)
        acc = acc + mm(kv.T, ds)
    acc = acc[:64] * 0.125
    for h in range(GRP):
        dqt_ref[64 * h : 64 * h + 64, :] = acc[:, 128 * h : 128 * h + 128]


def attend_back(qt, kv_all, bias, d_mixed, mixed, lse):
    heads = pl.BlockSpec((GRP * HD, R), lambda g: (g, 0))
    return pl.pallas_call(
        attend_back_kernel,
        name="attend_back",
        grid=(SIDE,),
        in_specs=[
            heads,
            pl.BlockSpec((KEYS, 128), lambda g: (0, g)),
            pl.BlockSpec((KEYS, R), lambda g: (0, 0)),
            heads,
            heads,
            pl.BlockSpec((1, 1, GRP * R), lambda g: (g, 0, 0)),
        ],
        out_specs=[pl.BlockSpec((KEYS, 128), lambda g: (0, g)), heads],
        out_shape=[
            jax.ShapeDtypeStruct((KEYS, SIDE * 128), bf16),
            jax.ShapeDtypeStruct((QSIDE, R), f32),
        ],
        compiler_params=pltpu.CompilerParams(vmem_limit_bytes=48 << 20),
        cost_estimate=pl.CostEstimate(
            flops=10_000_000_000, bytes_accessed=14_000_000, transcendentals=7_900_000
        ),
    )(qt, kv_all, bias, d_mixed, mixed, lse)


def project_back_kernel(
    dqt_ref, dkv_ref, cos_ref, sin_ref, u_ref, g_ref, dh_ref, w_ref,
    du_ref, dqkv_ref, at_ref, dg_ref,
):
    cos, sin = cos_ref[...], sin_ref[...]
    lane = lane_of((R, 128))
    dkv = [dkv_ref[:, 128 * g : 128 * g + 128] for g in range(KVH)]
    rolled = [pltpu.roll(b, 64, 1) for b in dkv]
    zero = jnp.zeros((R, 128), f32)
    blocks = [dqt_ref[128 * c : 128 * c + 128, :].T for c in range(7)]
    last = jnp.concatenate([dqt_ref[896:960, :], jnp.zeros((64, R), f32)], axis=0).T
    low = lane < 64
    blocks.append(jnp.where(low, last, rolled[0]))
    blocks.append(jnp.where(low, dkv[1], rolled[2]))
    blocks.append(jnp.where(low, dkv[3], rolled[4]))
    blocks = [b * cos - half_swapped(b) * sin for b in blocks]
    blocks.append(jnp.where(low, rolled[0], dkv[1]))
    blocks.append(jnp.where(low, rolled[2], dkv[3]))
    blocks.append(jnp.where(low, rolled[4], zero))
    da = jnp.zeros((R, D), f32)
    for c in range(0, 13, 2):
        if c + 1 < 13:
            d = jnp.concatenate([blocks[c], blocks[c + 1]], axis=1).astype(bf16)
            w = jnp.concatenate([qkv_weight(w_ref, c), qkv_weight(w_ref, c + 1)], axis=1)
        else:
            d, w = blocks[c].astype(bf16), qkv_weight(w_ref, c)
        dqkv_ref[:, 128 * c : 128 * c + d.shape[1]] = d
        da = da + mm_nt(d, w)
    u = u_ref[...].astype(f32)
    gain = g_ref[...]
    _, a = normed_of(u, gain)
    at_ref[...] = a.T
    d_u, d_gain = norm_back(da, u, gain)
    dg_ref[...] = d_gain
    du_ref[...] = dh_ref[...] + d_u


def project_back(d_query, d_kv, cos, sin, u, gain, d_hidden, weights):
    whole = lambda *shape: pl.BlockSpec(shape, lambda j: (0,) * len(shape))
    return pl.pallas_call(
        project_back_kernel,
        name="project_back",
        grid=(1,),
        in_specs=[
            whole(D, R),
            whole(R, 640),
            whole(R, 128),
            whole(R, 128),
            whole(R, D),
            whole(1, D),
            whole(R, D),
            whole(10, ROWS, 128),
        ],
        out_specs=[whole(R, D), whole(R, 13 * 128), whole(D, R), whole(1, D)],
        out_shape=[
            jax.ShapeDtypeStruct((R, D), f32),
            jax.ShapeDtypeStruct((R, 13 * 128), bf16),
            jax.ShapeDtypeStruct((D, R), bf16),
            jax.ShapeDtypeStruct((1, D), f32),
        ],
        compiler_params=pltpu.CompilerParams(vmem_limit_bytes=48 << 20),
        cost_estimate=pl.CostEstimate(flops=400_000_000, bytes_accessed=5_000_000, transcendentals=0),
    )(d_query, d_kv, cos, sin, u, gain, d_hidden, weights)


def outer_kernel(
    slot_ref, at_ref, dqkv_ref, mixed_ref, dhb_ref, nt_ref, dgate_ref, dup_ref, mt_ref, cb_ref,
    gain_ref, k0, k1, k2, s0, s1, s2, stage, sems,
):
    step = pl.program_id(0)
    buf = step % 2
    slot_y, slot_x = slot_ref[step // 4], slot_ref[4 + step % 4]
    zslot = [slot_ref[8 + k] for k in range(4)]
    out_ref = stage.at[buf]
    (a0, b0), (a1, b1), (a2, b2) = PART_ROWS

    def copy(i, buf, half=0):
        src = stage.at[buf]
        if i == 0:
            src, dst = src.at[:, a0:b0], (k0, s0)[half].at[slot_y % 2, slot_x]
        elif i == 1:
            src, dst = src.at[:, a1:b1], (k1, s1)[half].at[slot_x % 2, :, slot_y]
        elif i == 2:
            src, dst = src.at[0:2, a2:b2], k2.at[:, slot_y, slot_x]
        else:
            src, dst = src.at[2:4, a2:b2], s2.at[:, slot_y, slot_x]
        return pltpu.make_async_copy(src, dst, sems.at[buf, i])

    @pl.when(step >= 2)
    def _():
        for i in range(4):
            copy(i, buf).wait()

    def row_of(k, count, at):
        row = lax.broadcasted_iota(jnp.int32, (count, 128), 0)
        return jnp.where(row == at, gain_ref[pl.ds(4 * step + k, 1), :], 0.0)

    def narrow(start, ks):
        count = len(ks)
        rows = at_ref[pl.ds(pl.multiple_of(start, 32), 96 * count), :]
        for c in range(0, 13, 2):
            width = min(256, 1664 - 128 * c)
            res = mm(rows, dqkv_ref[:, 128 * c : 128 * c + width])
            for i, k in enumerate(ks):
                for h in range(width // 128):
                    out_ref[zslot[k], 96 * (c + h) : 96 * (c + h) + 96, :] = res[
                        96 * i : 96 * i + 96, 128 * h : 128 * h + 128
                    ].astype(bf16)
        for k in ks:
            out_ref[zslot[k], 1248:1280, :] = row_of(k, 32, 0).astype(bf16)

    def wide(ref, start, cot_ref, ks):
        rows = ref[pl.ds(pl.multiple_of(start, 32), 160 * len(ks)), :]
        for c in range(0, 8, 2):
            res = mm(rows, cot_ref[:, 128 * c : 128 * c + 256])
            for i, k in enumerate(ks):
                for h in range(2):
                    b = res[160 * i : 160 * i + 160, 128 * h : 128 * h + 128]
                    if c + h == 7:
                        b = b + row_of(k, 160, 0)
                    at = 160 * (c + h)
                    out_ref[zslot[k], at : at + 160, :] = b.astype(bf16)

    @pl.when(step < 2)
    def _():
        narrow(384 * step, (0, 1, 2, 3))

    @pl.when(step == 2)
    def _():
        narrow(768, (0, 1))
        wide(mixed_ref, 0, dhb_ref, (2, 3))

    @pl.when(step == 3)
    def _():
        wide(mixed_ref, 320, dhb_ref, (0, 1, 2, 3))

    @pl.when((step >= 4) & (step < 12))
    def _():
        rows = nt_ref[pl.ds(pl.multiple_of(128 * (step - 4), 128), 128), :]
        for part, ref in enumerate((dgate_ref, dup_ref)):
            for c in range(0, 20, 2):
                res = mm(rows, ref[:, 128 * c : 128 * c + 256])
                for k in range(4):
                    for h in range(2):
                        b = res[32 * k : 32 * k + 32, 128 * h : 128 * h + 128]
                        at = 32 * (20 * part + c + h)
                        if at == 0:
                            b = b + row_of(k, 32, 30)
                        out_ref[zslot[k], at : at + 32, :] = b.astype(bf16)

    @pl.when(step >= 12)
    def _():
        wide(mt_ref, 640 * (step - 12), cb_ref, (0, 1, 2, 3))

    for half in range(2):

        @pl.when(slot_y // 2 == half)
        def _(half=half):
            copy(0, buf, half).start()

        @pl.when(slot_x // 2 == half)
        def _(half=half):
            copy(1, buf, half).start()

    copy(2, buf).start()
    copy(3, buf).start()

    @pl.when(step == 15)
    def _():
        for last in (0, 1):
            for i in range(4):
                copy(i, last).wait()


def outer(slots, at, dqkv, mixed, dhb, nt, dgate, dup, mt, cb, gains):
    whole = lambda v: pl.BlockSpec(v.shape, lambda s, slot: (0,) * v.ndim)
    args = (at, dqkv, mixed, dhb, nt, dgate, dup, mt, cb, gains)
    shapes = [
        jax.ShapeDtypeStruct((2, 4, 4, end - begin, 128), bf16) for begin, end in PART_ROWS
    ]
    out = pl.pallas_call(
        outer_kernel,
        name="outer",
        grid_spec=pltpu.PrefetchScalarGridSpec(
            num_scalar_prefetch=1,
            grid=(16,),
            in_specs=[whole(v) for v in args],
            out_specs=[pl.BlockSpec(memory_space=pl.ANY)] * 6,
            scratch_shapes=[
                pltpu.VMEM((2, 4, ROWS, 128), bf16),
                pltpu.SemaphoreType.DMA((2, 4)),
            ],
        ),
        out_shape=shapes * 2,
        compiler_params=pltpu.CompilerParams(vmem_limit_bytes=48 << 20),
        cost_estimate=pl.CostEstimate(
            flops=2_600_000_000, bytes_accessed=24_000_000, transcendentals=0
        ),
    )(slots, *args)
    return out[:3], out[3:]


def shard_kind(rank):
    return jnp.where(rank < 10, 0, jnp.where((rank >= 16) & (rank < 48), 2, 1))


def shard_blocks(flat, gains, rank):
    g = jnp.zeros((1, 128), bf16).at[0, :30].set(gains)

    def narrow(_):
        w = jnp.pad(flat.reshape(96, 1600), ((0, 0), (0, 64)))
        w = w.reshape(96, 13, 128).transpose(1, 0, 2).reshape(1248, 128)
        return jnp.concatenate([w, jnp.pad(g, ((0, 31), (0, 0)))])

    def square(_):
        w = jnp.pad(flat.reshape(160, 960), ((0, 0), (0, 64)))
        w = w.reshape(160, 8, 128).transpose(1, 0, 2)
        last = jnp.concatenate([jnp.zeros((1, 64), bf16), g[:, :64]], axis=1)
        return w.at[7, 0].add(last[0]).reshape(ROWS, 128)

    def broad(_):
        w = jnp.pad(flat.reshape(30, 40, 128), ((0, 2), (0, 0), (0, 0))).transpose(1, 0, 2)
        return w.at[0, 30].set(g[0]).reshape(ROWS, 128)

    return lax.switch(shard_kind(rank), [narrow, square, broad], 0)


def blocks_shard(blocks, rank):
    def narrow(_):
        w = blocks[:1248].reshape(13, 96, 128).transpose(1, 0, 2).reshape(96, 1664)[:, :1600]
        return w.reshape(SHARD), blocks[1248, :30]

    def square(_):
        w = blocks.reshape(8, 160, 128).transpose(1, 0, 2).reshape(160, 1024)[:, :960]
        return w.reshape(SHARD), blocks[1120, 64:94]

    def broad(_):
        w = blocks.reshape(40, 32, 128).transpose(1, 0, 2)[:30]
        return w.reshape(SHARD), blocks[30, :30]

    return lax.switch(shard_kind(rank), [narrow, square, broad], 0)


def gathered_gains(gathered):
    rows = jnp.concatenate(
        [
            gathered[:10, 1248, :30],
            gathered[10:16, 1120, 64:94],
            gathered[16:48, 30, :30],
            gathered[48:, 1120, 64:94],
        ]
    ).astype(f32)
    flat = rows.reshape(1, 2 * D)
    return flat[:, :D], flat[:, D:]


def per_device(layer_in, out_grad, segment_ids, block_pair, params, norm_gains):
    phase = lax.axis_index("phase")
    ctx = lax.axis_index("ctx")
    rank = ctx * 2 + lax.axis_index("fsdp")
    y, x, z = rank // 16, (rank // 4) % 4, rank % 4
    zh = z // 2

    own = shard_blocks(params[0], norm_gains[0], rank)
    gathered = lax.all_gather(own, ("ctx", "fsdp"), axis=0)

    seg_row = segment_ids[0]
    pair = lax.dynamic_index_in_dim(block_pair, ctx, 0, keepdims=False)
    within = jnp.arange(HD, dtype=jnp.int32)
    place_q = jnp.concatenate([pair * 64 + within, (63 - pair) * 64 + within])
    seg_q = jnp.concatenate(
        [
            lax.dynamic_slice_in_dim(seg_row, pair * 64, 64),
            lax.dynamic_slice_in_dim(seg_row, (63 - pair) * 64, 64),
        ]
    )
    start_q = jnp.sum((seg_row[:, None] < seg_q[None, :]).astype(jnp.int32), axis=0)
    pairs_k = block_pair[key_order(y, x, zh, phase)]
    place_k = (
        jnp.stack([pairs_k, 63 - pairs_k], axis=1)[:, :, None] * 64 + within[None, None, :]
    ).reshape(KEYS)
    bias = jnp.where(
        (place_k[:, None] <= place_q[None, :]) & (place_k[:, None] >= start_q[None, :]),
        0.0,
        masked_fill,
    ).astype(f32)
    frequency = rope_theta ** (-2.0 * jnp.arange(HD // 2, dtype=f32) / HD)
    angles = (place_q - start_q).astype(f32)[:, None] * frequency[None, :]
    cosine, sine = jnp.cos(angles), jnp.sin(angles)
    cos = jnp.concatenate([cosine] * 4, axis=1)
    sin = jnp.concatenate([-sine, sine, -sine, sine], axis=1)
    spread = jnp.arange(PADD, dtype=jnp.int32)
    target = jnp.where(spread % 32 < 30, (spread // 32) * 30 + spread % 32, -1)
    pad = (jnp.arange(D, dtype=jnp.int32)[:, None] == target[None, :]).astype(bf16)

    gain_one, gain_two = gathered_gains(gathered)
    first = phase == 0

    u = layer_in[0]
    mixed = None
    kept = []
    for tick in range(2):
        active = phase == tick
        qt, kv = project(u, gain_one, cos, sin, gathered)
        kv_side = jnp.where(active, kv[:, :384], over(kv[:, 384:], tick))
        qt_side = jnp.where(active, qt[:QSIDE], over(qt[QSIDE:], tick))
        kv_all = gather_keys(kv_side)
        mixed_side, lse = attend(qt_side, kv_all, bias)
        kept.append((qt_side, kv_all, mixed_side, lse))
        far = over(mixed_side[: D - QSIDE], 1 - tick)
        whole = jnp.concatenate([mixed_side, far])
        mixed = whole if tick == 0 else jnp.where(active, whole, mixed)
        result, hidden, nt, gate, up, mt = feed(mixed, u, gain_two, pad, gathered)
        if tick == 0:
            u = jnp.where(first, u, over(result, 0))

    cot = out_grad[0]
    d_query = d_kv = None
    for tick in range(2):
        layer = 1 - tick
        active = phase == layer
        qt_side, kv_all, mixed_side, lse = kept[layer]
        dgate, dup, dh, dhb, dg_two, d_mixed, cb = feed_back(
            cot, gate, up, hidden, gain_two, pad, gathered
        )
        d_side = jnp.where(active, d_mixed[:QSIDE], over(d_mixed[QSIDE:], layer))
        d_kv_all, dq_side = attend_back(qt_side, kv_all, bias, d_side, mixed_side, lse)
        dq_new = jnp.concatenate([dq_side, over(dq_side[: D - QSIDE], tick)])
        dkv_side = scatter_keys(d_kv_all)
        dkv_new = jnp.concatenate([dkv_side, over(dkv_side[:, :256], tick)], axis=1)
        d_query = dq_new if tick == 0 else jnp.where(active, dq_new, d_query)
        d_kv = dkv_new if tick == 0 else jnp.where(active, dkv_new, d_kv)
        d_u, dqkv, at, dg_one = project_back(
            d_query, d_kv, cos, sin, u, gain_one, dh, gathered
        )
        if tick == 0:
            cot = jnp.where(first, over(d_u.astype(bf16), 1).astype(f32), cot)

    gains = jnp.concatenate([dg_one, dg_two], axis=1).reshape(SHARDS, 30)
    shards = jnp.arange(SHARDS, dtype=jnp.int32)
    square = (((shards >= 10) & (shards < 16)) | (shards >= 48))[:, None]
    gains = jnp.where(
        square, jnp.pad(gains, ((0, 0), (64, 34))), jnp.pad(gains, ((0, 0), (0, 98)))
    )
    four = jnp.arange(4, dtype=jnp.int32)
    slots = jnp.concatenate([slot_of(four ^ at_axis, phase) for at_axis in (y, x, z)])
    keep, send = outer(slots, at, dqkv, mixed, dhb, nt, dgate, dup, mt, cb, gains)
    total = scatter_grads(keep, send)
    param_part, gain_part = blocks_shard(total, rank)
    return (result[None, None], d_u[None, None], param_part[None], gain_part[None])


def solution(mesh):
    return jax.shard_map(
        per_device,
        mesh=mesh,
        in_specs=(
            P("fsdp", "ctx", None),
            P("fsdp", "ctx", None),
            P("fsdp", None),
            P(),
            P("phase", ("ctx", "fsdp")),
            P("phase", ("ctx", "fsdp")),
        ),
        out_specs=(
            P("phase", "fsdp", "ctx", None),
            P("phase", "fsdp", "ctx", None),
            P("phase", ("ctx", "fsdp")),
            P("phase", ("ctx", "fsdp")),
        ),
        check_vma=False,
    )
```

```python
import functools

import jax
import jax.numpy as jnp
from jax import lax
from jax.experimental import pallas as pl
from jax.experimental.pallas import tpu as pltpu
from jax.sharding import PartitionSpec as P

H = 15
KVH = 5
HD = 64
D = 960
FF = 2560
GRP = H // KVH
R = 128
SHARDS = 64
SHARD = 153600
ROWS = 1280
KEYS = 4096
CHUNK = 512
PADD = 1024
SIDE = 3
QSIDE = SIDE * GRP * HD
QPAD = 2 * QSIDE

eps = 1e-05
rope_theta = 100000.0
masked_fill = -1e30
f32 = jnp.float32
bf16 = jnp.bfloat16
ALL = ("phase", "ctx", "fsdp")

NT = (((1,), (1,)), ((), ()))


def mm(a, b):
    return jnp.dot(a, b, preferred_element_type=f32)


def mm_nt(a, b):
    return lax.dot_general(a, b, NT, preferred_element_type=f32)


STEPS = ((1, 3), (3, 1))


def swapped(block, way):
    pairs = []
    for p in range(2):
        dy, dx, dz = way(p)
        for y in range(4):
            for x in range(4):
                for z in range(4):
                    to = ((y ^ dy) * 4 + (x ^ dx)) * 4 + (z ^ dz)
                    pairs.append((p * 64 + (y * 4 + x) * 4 + z, p * 64 + to))
    return lax.ppermute(block, ALL, pairs)


def over(block, source):
    return lax.ppermute(block, "phase", [(source, 1 - source)])


def along(axes, number):
    def way(p):
        shift = [0, 0, 0]
        shift[axes[p]] = STEPS[p][number]
        return tuple(shift)

    return way


def far_z(p):
    return (0, 0, 2)


def gather_keys(kv):
    tail = kv.shape
    far = swapped(kv, far_z)
    near = kv
    orders = (((0, 1), (1, 0)), ((1, 0), (0, 1)))
    blocks = [near[None], far[None]]
    for leg in range(2):
        for number in range(2):
            if leg and number:
                blocks = list(lax.optimization_barrier(tuple(blocks)))
            for k in range(2):
                got = swapped(blocks[k], along(orders[k][leg], number))
                blocks[k] = jnp.concatenate([blocks[k], got], axis=0)
    return jnp.concatenate(blocks, axis=0).reshape(KEYS, tail[1])


def scatter_keys(d_kv, beside=None):
    parts = d_kv.reshape(2, 16, R, d_kv.shape[1])
    orders = (((0, 1), (1, 0)), ((1, 0), (0, 1)))
    blocks = [parts[0], parts[1]]
    for leg in (1, 0):
        for number in (1, 0):
            for k in (1, 0):
                half = blocks[k].shape[0] // 2
                got = swapped(blocks[k][half:], along(orders[k][leg], number))
                total = blocks[k][:half].astype(f32) + got.astype(f32)
                last = k == 0 and half == 1
                blocks[k] = total if last else total.astype(bf16)
            if beside is not None and number == 0:
                beside = planes_step(beside, 0, leg)
                blocks, beside = lax.optimization_barrier((blocks, beside))
    total = blocks[0][0] + swapped(blocks[1][0], far_z).astype(f32)
    return total if beside is None else (total, beside)


def slot_offsets(phase):
    return jnp.where(phase == 0, jnp.array([0, 1, 3, 2]), jnp.array([0, 3, 1, 2]))


def slot_of(offset, phase):
    at = jnp.where(phase == 0, jnp.array([0, 1, 3, 2]), jnp.array([0, 2, 3, 1]))
    return at[offset]


def key_order(y, x, zh, phase):
    off = slot_offsets(phase)
    outer = jnp.repeat(off, 4)
    inner = jnp.tile(off, 4)
    out = []
    for k in range(2):
        first_y = phase == k
        oy = jnp.where(first_y, inner, outer)
        ox = jnp.where(first_y, outer, inner)
        out.append((y ^ oy) * 8 + (x ^ ox) * 2 + (zh ^ k))
    return jnp.concatenate(out)


HALF = ROWS // 2
PLUS = ROWS + 16
PART_AXES = ((1, 2), (2, 1))


def summed(mine, got, at):
    return (mine[at].astype(f32) + got[at].astype(f32)).astype(bf16)


def planes_step(state, leg, number):
    keep, send = list(state[0]), list(state[1])
    for part, axes in enumerate(PART_AXES):
        axis = axes[leg]
        got = swapped(send[part], along((axis, axis), number))
        mine = keep[part]
        if number:
            keep[part] = summed(mine, got, 0)
            send[part] = summed(mine, got, 1)
        elif leg == 0:
            keep[part] = summed(mine, got, slice(0, 2))
            send[part] = summed(mine, got, slice(2, 4))
        else:
            keep[part] = summed(mine, got, slice(None))
    return keep, send


def scatter_planes(state, legs=(0, 1)):
    for leg in legs:
        for number in (1, 0):
            state = planes_step(state, leg, number)
    return state[0]


def scatter_last(planes, y, phase):
    slots = planes[y ^ slot_offsets(phase)]
    got = swapped(slots[2:], along((0, 0), 1))
    send = summed(slots[1], got[1], slice(None))
    keep = slots[0].astype(f32) + got[0].astype(f32)
    return keep + swapped(send, along((0, 0), 0)).astype(f32)


def lane_of(shape):
    return lax.broadcasted_iota(jnp.int32, shape, len(shape) - 1)


def half_swapped(block):
    lane = lane_of(block.shape)
    return jnp.where(lane % HD < HD // 2, pltpu.roll(block, 96, 1), pltpu.roll(block, 32, 1))


def qkv_weight(w_ref, c):
    return w_ref[:, 96 * c : 96 * c + 96, :].reshape(D, 128)


def normed_of(u, gain):
    scale = lax.rsqrt(jnp.mean(u * u, axis=-1, keepdims=True) + eps)
    return scale, (u * scale * gain).astype(bf16)


def project_kernel(u_ref, g_ref, cos_ref, sin_ref, w_ref, qt_ref, kv_ref):
    u = u_ref[...].astype(f32)
    _, a = normed_of(u, g_ref[...])
    cos, sin = cos_ref[...], sin_ref[...]
    blocks = []
    for c in range(0, 13, 2):
        if c + 1 < 13:
            w = jnp.concatenate([qkv_weight(w_ref, c), qkv_weight(w_ref, c + 1)], axis=1)
        else:
            w = qkv_weight(w_ref, c)
        y = mm(a, w)
        for k in range(w.shape[1] // 128):
            b = y[:, 128 * k : 128 * k + 128]
            if c + k < 10:
                b = b * cos + half_swapped(b) * sin
            blocks.append(b)
    for c in range(8):
        t = (blocks[c].astype(bf16).astype(f32) * 0.125).T.astype(bf16)
        count = 128 if c < 7 else 64
        qt_ref[128 * c : 128 * c + count, :] = t[:count]
    qt_ref[D:, :] = jnp.zeros((QPAD - D, R), bf16)
    kv_ref[:, 640:] = jnp.zeros((R, 128), bf16)
    lane = lane_of((R, 128))
    for g in range(KVH):
        k, v = blocks[(15 + g) // 2], blocks[(20 + g) // 2]
        if (15 + g) % 2:
            k = pltpu.roll(k, 64, 1)
        if (20 + g) % 2 == 0:
            v = pltpu.roll(v, 64, 1)
        kv_ref[:, 128 * g : 128 * g + 128] = jnp.where(lane < 64, k, v).astype(bf16)


def project(u, gain, cos, sin, weights):
    return pl.pallas_call(
        project_kernel,
        name="project",
        grid=(1,),
        in_specs=[
            pl.BlockSpec((R, D), lambda i: (0, 0)),
            pl.BlockSpec((1, D), lambda i: (0, 0)),
            pl.BlockSpec((R, 128), lambda i: (0, 0)),
            pl.BlockSpec((R, 128), lambda i: (0, 0)),
            pl.BlockSpec((10, ROWS, 128), lambda i: (0, 0, 0)),
        ],
        out_specs=[
            pl.BlockSpec((QPAD, R), lambda i: (0, 0)),
            pl.BlockSpec((R, 768), lambda i: (0, 0)),
        ],
        out_shape=[
            jax.ShapeDtypeStruct((QPAD, R), bf16),
            jax.ShapeDtypeStruct((R, 768), bf16),
        ],
        compiler_params=pltpu.CompilerParams(vmem_limit_bytes=48 << 20),
        cost_estimate=pl.CostEstimate(flops=400_000_000, bytes_accessed=4_000_000, transcendentals=0),
    )(u, gain, cos, sin, weights)


def heads_wide(ref, low):
    top = jnp.concatenate([ref[64 * h : 64 * h + 64, :] for h in range(GRP)], axis=1)
    zero = jnp.zeros_like(top)
    return jnp.concatenate([top, zero] if low else [zero, top], axis=0)


def attend_kernel(qt_ref, kv_ref, bias_ref, mixed_ref, lse_ref, s_ref):
    q = heads_wide(qt_ref, True)
    peak = jnp.full((1, GRP * R), masked_fill, f32)
    for i in range(KEYS // CHUNK):
        rows = slice(CHUNK * i, CHUNK * i + CHUNK)
        b = bias_ref[rows, :]
        s = mm(kv_ref[rows, :], q) + jnp.concatenate([b, b, b], axis=1)
        s_ref[rows, :] = s
        peak = jnp.maximum(peak, jnp.max(s, axis=0, keepdims=True))
    total = jnp.zeros((1, GRP * R), f32)
    acc = jnp.zeros((128, GRP * R), f32)
    for i in range(KEYS // CHUNK):
        rows = slice(CHUNK * i, CHUNK * i + CHUNK)
        p = jnp.exp(s_ref[rows, :] - peak)
        total = total + jnp.sum(p, axis=0, keepdims=True)
        acc = acc + mm(kv_ref[rows, :].T, p.astype(bf16))
    lse_ref[0] = peak + jnp.log(total)
    o = (acc[64:] / total).astype(bf16)
    for h in range(GRP):
        mixed_ref[64 * h : 64 * h + 64, :] = o[:, 128 * h : 128 * h + 128]


def attend(qt, kv_all, bias):
    return pl.pallas_call(
        attend_kernel,
        name="attend",
        grid=(SIDE,),
        in_specs=[
            pl.BlockSpec((GRP * HD, R), lambda g: (g, 0)),
            pl.BlockSpec((KEYS, 128), lambda g: (0, g)),
            pl.BlockSpec((KEYS, R), lambda g: (0, 0)),
        ],
        out_specs=[
            pl.BlockSpec((GRP * HD, R), lambda g: (g, 0)),
            pl.BlockSpec((1, 1, GRP * R), lambda g: (g, 0, 0)),
        ],
        out_shape=[
            jax.ShapeDtypeStruct((QSIDE, R), bf16),
            jax.ShapeDtypeStruct((SIDE, 1, GRP * R), f32),
        ],
        scratch_shapes=[pltpu.VMEM((KEYS, GRP * R), f32)],
        compiler_params=pltpu.CompilerParams(vmem_limit_bytes=48 << 20),
        cost_estimate=pl.CostEstimate(
            flops=4_000_000_000, bytes_accessed=8_000_000, transcendentals=7_900_000
        ),
    )(qt, kv_all, bias)


def out_weight(refs, c):
    return jnp.concatenate(
        [ref[:, 160 * c : 160 * c + 160, :].reshape(320, 128) for ref in refs], axis=0
    )


def gu_weight(refs, c):
    gl, gh, ul, uh = refs
    gate = jnp.concatenate([gl[:, c].reshape(512, 128), gh[:, c].reshape(512, 128)], axis=0)
    up = jnp.concatenate([ul[:, c].reshape(512, 128), uh[:, c].reshape(512, 128)], axis=0)
    return jnp.concatenate([gate, up], axis=1)


def down_weight(ref, c):
    return ref[:, 160 * c : 160 * c + 160, :].reshape(640, 128)


WEIGHT_SPECS = (
    [pl.BlockSpec((2, ROWS, 128), lambda j, k=k: (5 + k, 0, 0)) for k in range(3)]
    + [
        pl.BlockSpec((16, 5, 32, 128), lambda j, d=d, o=o: (1 + d, o + j, 0, 0))
        for o in (0, 4)
        for d in (0, 1)
    ]
    + [pl.BlockSpec((4, ROWS, 128), lambda j: (12 + j, 0, 0))]
)


def weight_args(gathered):
    fine = gathered.reshape(SHARDS, 40, 32, 128)
    return [gathered] * 3 + [fine] * 4 + [gathered]


def feed_kernel(
    mixed_ref, u_ref, g_ref, pad_ref, o0, o1, o2, gl, gh, ul, uh, wd,
    y_ref, h_ref, nt_ref, gate_ref, up_ref, mt_ref, n_scr, y_scr,
):
    step = pl.program_id(0)

    @pl.when(step == 0)
    def _():
        mixed = mixed_ref[...].T
        for c in range(0, 8, 2):
            w = jnp.concatenate(
                [out_weight((o0, o1, o2), c), out_weight((o0, o1, o2), c + 1)], axis=1
            )
            y = mm(mixed, w)
            end = min(128 * c + 256, D)
            h_ref[:, 128 * c : end] = u_ref[:, 128 * c : end].astype(f32) + y[:, : end - 128 * c]
        _, n = normed_of(h_ref[...], g_ref[...])
        padded = mm(n, pad_ref[...])
        n_scr[...] = padded.astype(bf16)
        nt_ref[...] = padded.T.astype(bf16)
        y_scr[...] = jnp.zeros_like(y_scr)

    n = n_scr[...]
    inner = []
    for c in range(5):
        gu = mm(n, gu_weight((gl, gh, ul, uh), c))
        gate, up = gu[:, :128], gu[:, 128:]
        cols = slice(128 * c, 128 * c + 128)
        gate_ref[:, cols] = gate
        up_ref[:, cols] = up
        m = gate * jax.nn.sigmoid(gate) * up
        mt_ref[cols, :] = m.T.astype(bf16)
        inner.append(m.astype(bf16))
    inner = jnp.concatenate(inner, axis=1)
    for c in range(0, 8, 2):
        w = jnp.concatenate([down_weight(wd, c), down_weight(wd, c + 1)], axis=1)
        y_scr[:, 128 * c : 128 * c + 256] += mm(inner, w)

    @pl.when(step == 3)
    def _():
        y_ref[...] = (h_ref[...] + y_scr[:, :D]).astype(bf16)


def feed(mixed, u, gain, pad, gathered):
    whole = lambda *shape: pl.BlockSpec(shape, lambda j: (0,) * len(shape))
    return pl.pallas_call(
        feed_kernel,
        name="feed",
        grid=(4,),
        in_specs=[whole(D, R), whole(R, D), whole(1, D), whole(D, PADD)] + WEIGHT_SPECS,
        out_specs=[
            whole(R, D),
            whole(R, D),
            whole(PADD, R),
            pl.BlockSpec((R, 640), lambda j: (0, j)),
            pl.BlockSpec((R, 640), lambda j: (0, j)),
            pl.BlockSpec((640, R), lambda j: (j, 0)),
        ],
        out_shape=[
            jax.ShapeDtypeStruct((R, D), bf16),
            jax.ShapeDtypeStruct((R, D), f32),
            jax.ShapeDtypeStruct((PADD, R), bf16),
            jax.ShapeDtypeStruct((R, FF), f32),
            jax.ShapeDtypeStruct((R, FF), f32),
            jax.ShapeDtypeStruct((FF, R), bf16),
        ],
        scratch_shapes=[pltpu.VMEM((R, PADD), bf16), pltpu.VMEM((R, PADD), f32)],
        compiler_params=pltpu.CompilerParams(vmem_limit_bytes=48 << 20),
        cost_estimate=pl.CostEstimate(
            flops=2_200_000_000, bytes_accessed=22_000_000, transcendentals=400_000
        ),
    )(mixed, u, gain, pad, *weight_args(gathered))


def norm_back(d_out, values, gain):
    scales = lax.rsqrt(jnp.mean(values * values, axis=-1, keepdims=True) + eps)
    scaled = d_out * gain
    d_gain = jnp.sum(d_out * values * scales, axis=0, keepdims=True)
    d_values = scales * scaled - values * (scales * scales * scales) * jnp.mean(
        scaled * values, axis=-1, keepdims=True
    )
    return d_values, d_gain


def feed_back_kernel(
    c_ref, gate_ref, up_ref, h_ref, g_ref, pad_ref, o0, o1, o2, gl, gh, ul, uh, wd,
    dgate_ref, dup_ref, dh_ref, dhb_ref, dg_ref, dot_ref, cb_ref, dn_scr,
):
    step = pl.program_id(0)

    @pl.when(step == 0)
    def _():
        cb_ref[...] = jnp.zeros_like(cb_ref)
        cb_ref[:, :D] = c_ref[...].astype(bf16)
        dn_scr[...] = jnp.zeros_like(dn_scr)

    d_inner = jnp.zeros((R, 640), f32)
    for c in range(0, 8, 2):
        w = jnp.concatenate([down_weight(wd, c), down_weight(wd, c + 1)], axis=1)
        d_inner = d_inner + mm_nt(cb_ref[:, 128 * c : 128 * c + 256], w)
    for c in range(5):
        cols = slice(128 * c, 128 * c + 128)
        gate, up, dm = gate_ref[:, cols], up_ref[:, cols], d_inner[:, cols]
        sigma = jax.nn.sigmoid(gate)
        d_gate = (dm * up * sigma * (1.0 + gate * (1.0 - sigma))).astype(bf16)
        d_up = (dm * gate * sigma).astype(bf16)
        dgate_ref[:, cols] = d_gate
        dup_ref[:, cols] = d_up
        both = jnp.concatenate([d_gate, d_up], axis=1)
        dn_scr[...] += mm_nt(both, gu_weight((gl, gh, ul, uh), c))

    @pl.when(step == 3)
    def _():
        padded = dn_scr[...]
        high = padded.astype(bf16)
        low = (padded - high.astype(f32)).astype(bf16)
        dn = mm_nt(high, pad_ref[...]) + mm_nt(low, pad_ref[...])
        d_h, d_gain = norm_back(dn, h_ref[...], g_ref[...])
        d_h = c_ref[...] + d_h
        dg_ref[...] = d_gain
        dh_ref[...] = d_h
        dhb_ref[...] = jnp.zeros_like(dhb_ref)
        dhb_ref[:, :D] = d_h.astype(bf16)
        d_mixed = jnp.zeros((R, D), f32)
        for c in range(0, 8, 2):
            w = jnp.concatenate(
                [out_weight((o0, o1, o2), c), out_weight((o0, o1, o2), c + 1)], axis=1
            )
            d_mixed = d_mixed + mm_nt(dhb_ref[:, 128 * c : 128 * c + 256], w)
        dot_ref[:D, :] = d_mixed.T
        dot_ref[D:, :] = jnp.zeros((QPAD - D, R), f32)


def feed_back(cot, gate, up, hidden, gain, pad, gathered):
    whole = lambda *shape: pl.BlockSpec(shape, lambda j: (0,) * len(shape))
    block = pl.BlockSpec((R, 640), lambda j: (0, j))
    return pl.pallas_call(
        feed_back_kernel,
        name="feed_back",
        grid=(4,),
        in_specs=[whole(R, D), block, block, whole(R, D), whole(1, D), whole(D, PADD)]
        + WEIGHT_SPECS,
        out_specs=[
            block,
            block,
            whole(R, D),
            whole(R, PADD),
            whole(1, D),
            whole(QPAD, R),
            whole(R, PADD),
        ],
        out_shape=[
            jax.ShapeDtypeStruct((R, FF), bf16),
            jax.ShapeDtypeStruct((R, FF), bf16),
            jax.ShapeDtypeStruct((R, D), f32),
            jax.ShapeDtypeStruct((R, PADD), bf16),
            jax.ShapeDtypeStruct((1, D), f32),
            jax.ShapeDtypeStruct((QPAD, R), f32),
            jax.ShapeDtypeStruct((R, PADD), bf16),
        ],
        scratch_shapes=[pltpu.VMEM((R, PADD), f32)],
        compiler_params=pltpu.CompilerParams(vmem_limit_bytes=48 << 20),
        cost_estimate=pl.CostEstimate(
            flops=2_200_000_000, bytes_accessed=22_000_000, transcendentals=400_000
        ),
    )(cot, gate, up, hidden, gain, pad, *weight_args(gathered))


def attend_back_kernel(
    qt_ref, kv_ref, bias_ref, dot_ref, mixed_ref, lse_ref, dkv_ref, dqt_ref
):
    q = heads_wide(qt_ref, True)
    d_o = heads_wide(dot_ref, False)
    o = heads_wide(mixed_ref, False)
    delta = jnp.sum(d_o * o.astype(f32), axis=0, keepdims=True)
    d_o = d_o.astype(bf16)
    lse = lse_ref[0]
    both = jnp.concatenate([q, d_o], axis=1)
    acc = jnp.zeros((128, GRP * R), f32)
    for i in range(KEYS // CHUNK):
        rows = slice(CHUNK * i, CHUNK * i + CHUNK)
        b = bias_ref[rows, :]
        kv = kv_ref[rows, :]
        p = jnp.exp(mm(kv, q) + jnp.concatenate([b, b, b], axis=1) - lse)
        ds = (p * (mm(kv, d_o) - delta)).astype(bf16)
        dkv_ref[rows, :] = mm_nt(jnp.concatenate([ds, p.astype(bf16)], axis=1), both).astype(bf16)
        acc = acc + mm(kv.T, ds)
    acc = acc[:64] * 0.125
    for h in range(GRP):
        dqt_ref[64 * h : 64 * h + 64, :] = acc[:, 128 * h : 128 * h + 128]


def attend_back(qt, kv_all, bias, d_mixed, mixed, lse):
    heads = pl.BlockSpec((GRP * HD, R), lambda g: (g, 0))
    return pl.pallas_call(
        attend_back_kernel,
        name="attend_back",
        grid=(SIDE,),
        in_specs=[
            heads,
            pl.BlockSpec((KEYS, 128), lambda g: (0, g)),
            pl.BlockSpec((KEYS, R), lambda g: (0, 0)),
            heads,
            heads,
            pl.BlockSpec((1, 1, GRP * R), lambda g: (g, 0, 0)),
        ],
        out_specs=[pl.BlockSpec((KEYS, 128), lambda g: (0, g)), heads],
        out_shape=[
            jax.ShapeDtypeStruct((KEYS, SIDE * 128), bf16),
            jax.ShapeDtypeStruct((QSIDE, R), f32),
        ],
        compiler_params=pltpu.CompilerParams(vmem_limit_bytes=48 << 20),
        cost_estimate=pl.CostEstimate(
            flops=10_000_000_000, bytes_accessed=14_000_000, transcendentals=7_900_000
        ),
    )(qt, kv_all, bias, d_mixed, mixed, lse)


def project_back_kernel(
    dqt_ref, dkv_ref, cos_ref, sin_ref, u_ref, g_ref, dh_ref, w_ref,
    du_ref, dqkv_ref, at_ref, dg_ref,
):
    cos, sin = cos_ref[...], sin_ref[...]
    lane = lane_of((R, 128))
    dkv = [dkv_ref[:, 128 * g : 128 * g + 128] for g in range(KVH)]
    rolled = [pltpu.roll(b, 64, 1) for b in dkv]
    zero = jnp.zeros((R, 128), f32)
    blocks = [dqt_ref[128 * c : 128 * c + 128, :].T for c in range(7)]
    last = jnp.concatenate([dqt_ref[896:960, :], jnp.zeros((64, R), f32)], axis=0).T
    low = lane < 64
    blocks.append(jnp.where(low, last, rolled[0]))
    blocks.append(jnp.where(low, dkv[1], rolled[2]))
    blocks.append(jnp.where(low, dkv[3], rolled[4]))
    blocks = [b * cos - half_swapped(b) * sin for b in blocks]
    blocks.append(jnp.where(low, rolled[0], dkv[1]))
    blocks.append(jnp.where(low, rolled[2], dkv[3]))
    blocks.append(jnp.where(low, rolled[4], zero))
    da = jnp.zeros((R, D), f32)
    for c in range(0, 13, 2):
        if c + 1 < 13:
            d = jnp.concatenate([blocks[c], blocks[c + 1]], axis=1).astype(bf16)
            w = jnp.concatenate([qkv_weight(w_ref, c), qkv_weight(w_ref, c + 1)], axis=1)
        else:
            d, w = blocks[c].astype(bf16), qkv_weight(w_ref, c)
        dqkv_ref[:, 128 * c : 128 * c + d.shape[1]] = d
        da = da + mm_nt(d, w)
    u = u_ref[...].astype(f32)
    gain = g_ref[...]
    _, a = normed_of(u, gain)
    at_ref[...] = a.T
    d_u, d_gain = norm_back(da, u, gain)
    dg_ref[...] = d_gain
    du_ref[...] = dh_ref[...] + d_u


def project_back(d_query, d_kv, cos, sin, u, gain, d_hidden, weights):
    whole = lambda *shape: pl.BlockSpec(shape, lambda j: (0,) * len(shape))
    return pl.pallas_call(
        project_back_kernel,
        name="project_back",
        grid=(1,),
        in_specs=[
            whole(D, R),
            whole(R, 640),
            whole(R, 128),
            whole(R, 128),
            whole(R, D),
            whole(1, D),
            whole(R, D),
            whole(10, ROWS, 128),
        ],
        out_specs=[whole(R, D), whole(R, 13 * 128), whole(D, R), whole(1, D)],
        out_shape=[
            jax.ShapeDtypeStruct((R, D), f32),
            jax.ShapeDtypeStruct((R, 13 * 128), bf16),
            jax.ShapeDtypeStruct((D, R), bf16),
            jax.ShapeDtypeStruct((1, D), f32),
        ],
        compiler_params=pltpu.CompilerParams(vmem_limit_bytes=48 << 20),
        cost_estimate=pl.CostEstimate(flops=400_000_000, bytes_accessed=5_000_000, transcendentals=0),
    )(d_query, d_kv, cos, sin, u, gain, d_hidden, weights)


def stage_out(step, slot_ref, planes, outs, stage, sems, fill):
    buf = step % 2
    plane = step // 4
    slot_x = slot_ref[step % 4]
    zslot = [slot_ref[4 + k] for k in range(4)]
    ka, kb, sa, sb = outs
    rows = stage.shape[2]

    def copy(i, buf, half=0):
        src = stage.at[buf]
        if i == 0:
            src, dst = src.at[:, 0:HALF], (ka, sa)[half].at[slot_x % 2, :, plane]
        elif i == 1:
            src, dst = src.at[0:2, HALF:rows], kb.at[:, slot_x, plane]
        else:
            src, dst = src.at[2:4, HALF:rows], sb.at[:, slot_x, plane]
        return pltpu.make_async_copy(src, dst, sems.at[buf, i])

    @pl.when(step >= 2)
    def _():
        for i in range(3):
            copy(i, buf).wait()

    fill(stage.at[buf], zslot)

    for half in range(2):

        @pl.when(slot_x // 2 == half)
        def _(half=half):
            copy(0, buf, half).start()

    copy(1, buf).start()
    copy(2, buf).start()

    @pl.when(step == 4 * planes - 1)
    def _():
        for last in (0, 1):
            for i in range(3):
                copy(i, last).wait()


def outer_square(out_ref, zslot, ref, start, cot_ref, ks):
    rows = ref[pl.ds(pl.multiple_of(start, 32), 160 * len(ks)), :]
    for c in range(0, 8, 2):
        res = mm(rows, cot_ref[:, 128 * c : 128 * c + 256])
        for i, k in enumerate(ks):
            for h in range(2):
                b = res[160 * i : 160 * i + 160, 128 * h : 128 * h + 128]
                at = 160 * (c + h)
                out_ref[zslot[k], at : at + 160, :] = b.astype(bf16)


def outer_feed_kernel(
    slot_ref, nt_ref, dgate_ref, dup_ref, mt_ref, cb_ref, ka, kb, sa, sb, stage, sems
):
    step = pl.program_id(0)

    def fill(out_ref, zslot):
        @pl.when(step < 8)
        def _():
            rows = nt_ref[pl.ds(pl.multiple_of(128 * step, 128), 128), :]
            for part, ref in enumerate((dgate_ref, dup_ref)):
                for c in range(0, 20, 2):
                    res = mm(rows, ref[:, 128 * c : 128 * c + 256])
                    for k in range(4):
                        for h in range(2):
                            b = res[32 * k : 32 * k + 32, 128 * h : 128 * h + 128]
                            at = 32 * (20 * part + c + h)
                            out_ref[zslot[k], at : at + 32, :] = b.astype(bf16)

        @pl.when(step >= 8)
        def _():
            outer_square(out_ref, zslot, mt_ref, 640 * (step - 8), cb_ref, (0, 1, 2, 3))

    stage_out(step, slot_ref, 3, (ka, kb, sa, sb), stage, sems, fill)


def outer_attend_kernel(
    slot_ref, at_ref, dqkv_ref, mixed_ref, dhb_ref, gain_ref, ka, kb, sa, sb, stage, sems
):
    step = pl.program_id(0)

    def fill(out_ref, zslot):
        def narrow(start, ks):
            count = len(ks)
            rows = at_ref[pl.ds(pl.multiple_of(start, 32), 96 * count), :]
            for c in range(0, 13, 2):
                width = min(256, 1664 - 128 * c)
                res = mm(rows, dqkv_ref[:, 128 * c : 128 * c + width])
                for i, k in enumerate(ks):
                    for h in range(width // 128):
                        at = 96 * (c + h)
                        out_ref[zslot[k], at : at + 96, :] = res[
                            96 * i : 96 * i + 96, 128 * h : 128 * h + 128
                        ].astype(bf16)
            for k in ks:
                out_ref[zslot[k], 1248:ROWS, :] = jnp.zeros((32, 128), bf16)

        for k in range(4):
            out_ref[zslot[k], ROWS:PLUS, :] = gain_ref[4 * step + k].astype(bf16)

        @pl.when(step < 2)
        def _():
            narrow(384 * step, (0, 1, 2, 3))

        @pl.when(step == 2)
        def _():
            narrow(768, (0, 1))
            outer_square(out_ref, zslot, mixed_ref, 0, dhb_ref, (2, 3))

        @pl.when(step == 3)
        def _():
            outer_square(out_ref, zslot, mixed_ref, 320, dhb_ref, (0, 1, 2, 3))

    stage_out(step, slot_ref, 1, (ka, kb, sa, sb), stage, sems, fill)


def outer(kernel, name, slots, planes, rows, args):
    whole = lambda v: pl.BlockSpec(v.shape, lambda s, slot: (0,) * v.ndim)
    shapes = [
        jax.ShapeDtypeStruct((2, 4, planes, count, 128), bf16) for count in (HALF, rows - HALF)
    ]
    out = pl.pallas_call(
        kernel,
        name=name,
        grid_spec=pltpu.PrefetchScalarGridSpec(
            num_scalar_prefetch=1,
            grid=(4 * planes,),
            in_specs=[whole(v) for v in args],
            out_specs=[pl.BlockSpec(memory_space=pl.ANY)] * 4,
            scratch_shapes=[
                pltpu.VMEM((2, 4, rows, 128), bf16),
                pltpu.SemaphoreType.DMA((2, 3)),
            ],
        ),
        out_shape=shapes * 2,
        compiler_params=pltpu.CompilerParams(vmem_limit_bytes=48 << 20),
        cost_estimate=pl.CostEstimate(
            flops=650_000_000 * planes, bytes_accessed=6_000_000 * planes, transcendentals=0
        ),
    )(slots, *args)
    return list(out[:2]), list(out[2:])


def shard_kind(rank):
    return jnp.where(rank < 10, 0, jnp.where((rank >= 16) & (rank < 48), 2, 1))


def shard_blocks(flat, gains, rank):
    g = jnp.zeros((1, 128), bf16).at[0, :30].set(gains)

    def narrow(_):
        w = jnp.pad(flat.reshape(96, 1600), ((0, 0), (0, 64)))
        w = w.reshape(96, 13, 128).transpose(1, 0, 2).reshape(1248, 128)
        return jnp.concatenate([w, jnp.pad(g, ((0, 31), (0, 0)))])

    def square(_):
        w = jnp.pad(flat.reshape(160, 960), ((0, 0), (0, 64)))
        w = w.reshape(160, 8, 128).transpose(1, 0, 2)
        last = jnp.concatenate([jnp.zeros((1, 64), bf16), g[:, :64]], axis=1)
        return w.at[7, 0].add(last[0]).reshape(ROWS, 128)

    def broad(_):
        w = jnp.pad(flat.reshape(30, 40, 128), ((0, 2), (0, 0), (0, 0))).transpose(1, 0, 2)
        return w.at[0, 30].set(g[0]).reshape(ROWS, 128)

    return lax.switch(shard_kind(rank), [narrow, square, broad], 0)


def blocks_shard(blocks, rank):
    def narrow(_):
        w = blocks[:1248].reshape(13, 96, 128).transpose(1, 0, 2).reshape(96, 1664)[:, :1600]
        return w.reshape(SHARD)

    def square(_):
        w = blocks.reshape(8, 160, 128).transpose(1, 0, 2).reshape(160, 1024)[:, :960]
        return w.reshape(SHARD)

    def broad(_):
        return blocks.reshape(40, 32, 128).transpose(1, 0, 2)[:30].reshape(SHARD)

    return lax.switch(shard_kind(rank), [narrow, square, broad], 0)


def gathered_gains(gathered):
    rows = jnp.concatenate(
        [
            gathered[:10, 1248, :30],
            gathered[10:16, 1120, 64:94],
            gathered[16:48, 30, :30],
            gathered[48:, 1120, 64:94],
        ]
    ).astype(f32)
    flat = rows.reshape(1, 2 * D)
    return flat[:, :D], flat[:, D:]


def per_device(layer_in, out_grad, segment_ids, block_pair, params, norm_gains):
    phase = lax.axis_index("phase")
    ctx = lax.axis_index("ctx")
    rank = ctx * 2 + lax.axis_index("fsdp")
    y, x, z = rank // 16, (rank // 4) % 4, rank % 4
    zh = z // 2

    own = shard_blocks(params[0], norm_gains[0], rank)
    gathered = lax.all_gather(own, ("ctx", "fsdp"), axis=0)

    seg_row = segment_ids[0]
    pair = lax.dynamic_index_in_dim(block_pair, ctx, 0, keepdims=False)
    within = jnp.arange(HD, dtype=jnp.int32)
    place_q = jnp.concatenate([pair * 64 + within, (63 - pair) * 64 + within])
    seg_q = jnp.concatenate(
        [
            lax.dynamic_slice_in_dim(seg_row, pair * 64, 64),
            lax.dynamic_slice_in_dim(seg_row, (63 - pair) * 64, 64),
        ]
    )
    start_q = jnp.sum((seg_row[:, None] < seg_q[None, :]).astype(jnp.int32), axis=0)
    pairs_k = block_pair[key_order(y, x, zh, phase)]
    place_k = (
        jnp.stack([pairs_k, 63 - pairs_k], axis=1)[:, :, None] * 64 + within[None, None, :]
    ).reshape(KEYS)
    bias = jnp.where(
        (place_k[:, None] <= place_q[None, :]) & (place_k[:, None] >= start_q[None, :]),
        0.0,
        masked_fill,
    ).astype(f32)
    frequency = rope_theta ** (-2.0 * jnp.arange(HD // 2, dtype=f32) / HD)
    angles = (place_q - start_q).astype(f32)[:, None] * frequency[None, :]
    cosine, sine = jnp.cos(angles), jnp.sin(angles)
    cos = jnp.concatenate([cosine] * 4, axis=1)
    sin = jnp.concatenate([-sine, sine, -sine, sine], axis=1)
    spread = jnp.arange(PADD, dtype=jnp.int32)
    target = jnp.where(spread % 32 < 30, (spread // 32) * 30 + spread % 32, -1)
    pad = (jnp.arange(D, dtype=jnp.int32)[:, None] == target[None, :]).astype(bf16)

    gain_one, gain_two = gathered_gains(gathered)
    first = phase == 0

    u = layer_in[0]
    mixed = None
    kept = []
    for tick in range(2):
        active = phase == tick
        qt, kv = project(u, gain_one, cos, sin, gathered)
        kv_side = jnp.where(active, kv[:, :384], over(kv[:, 384:], tick))
        qt_side = jnp.where(active, qt[:QSIDE], over(qt[QSIDE:], tick))
        kv_all = gather_keys(kv_side)
        mixed_side, lse = attend(qt_side, kv_all, bias)
        kept.append((qt_side, kv_all, mixed_side, lse))
        far = over(mixed_side[: D - QSIDE], 1 - tick)
        whole = jnp.concatenate([mixed_side, far])
        mixed = whole if tick == 0 else jnp.where(active, whole, mixed)
        result, hidden, nt, gate, up, mt = feed(mixed, u, gain_two, pad, gathered)
        if tick == 0:
            u = jnp.where(first, u, over(result, 0))

    four = jnp.arange(4, dtype=jnp.int32)
    slots = jnp.concatenate([slot_of(four ^ at_axis, phase) for at_axis in (x, z)])

    cot = out_grad[0]
    d_query = d_kv = None
    for tick in range(2):
        layer = 1 - tick
        active = phase == layer
        qt_side, kv_all, mixed_side, lse = kept[layer]
        dgate, dup, dh, dhb, dg_two, d_mixed, cb = feed_back(
            cot, gate, up, hidden, gain_two, pad, gathered
        )
        if tick:
            feeds = outer(
                outer_feed_kernel, "outer_feed", slots, 3, ROWS, (nt, dgate, dup, mt, cb)
            )
        d_side = jnp.where(active, d_mixed[:QSIDE], over(d_mixed[QSIDE:], layer))
        if tick:
            d_side, feeds = lax.optimization_barrier((d_side, feeds))
        d_kv_all, dq_side = attend_back(qt_side, kv_all, bias, d_side, mixed_side, lse)
        dq_new = jnp.concatenate([dq_side, over(dq_side[: D - QSIDE], tick)])
        if tick:
            dkv_side, feeds = scatter_keys(d_kv_all, feeds)
        else:
            dkv_side = scatter_keys(d_kv_all)
        dkv_new = jnp.concatenate([dkv_side, over(dkv_side[:, :256], tick)], axis=1)
        d_query = dq_new if tick == 0 else jnp.where(active, dq_new, d_query)
        d_kv = dkv_new if tick == 0 else jnp.where(active, dkv_new, d_kv)
        d_u, dqkv, at, dg_one = project_back(
            d_query, d_kv, cos, sin, u, gain_one, dh, gathered
        )
        if tick == 0:
            cot = jnp.where(first, over(d_u.astype(bf16), 1).astype(f32), cot)

    gains = jnp.concatenate([dg_one, dg_two], axis=1).reshape(4, 16, 30).transpose(1, 0, 2)
    gains = jnp.pad(gains, ((0, 0), (0, 12), (0, 98)))
    last = outer(
        outer_attend_kernel, "outer_attend", slots, 1, PLUS, (at, dqkv, mixed, dhb, gains)
    )
    last = scatter_planes(last)
    plane = jnp.concatenate([last[0][0], last[1][0]])
    feeds = jnp.concatenate(scatter_planes(feeds, (1,)), axis=1)
    tail = jnp.pad(plane[ROWS : ROWS + 4, None], ((0, 0), (0, 15), (0, 0)))
    planes = jnp.concatenate([plane[None, :ROWS], feeds])
    total = scatter_last(jnp.concatenate([planes, tail], axis=1), y, phase)
    param_part = blocks_shard(total[:ROWS], rank)
    gain_part = total[ROWS, :30]
    return (result[None, None], d_u[None, None], param_part[None], gain_part[None])


def solution(mesh):
    return jax.shard_map(
        per_device,
        mesh=mesh,
        in_specs=(
            P("fsdp", "ctx", None),
            P("fsdp", "ctx", None),
            P("fsdp", None),
            P(),
            P("phase", ("ctx", "fsdp")),
            P("phase", ("ctx", "fsdp")),
        ),
        out_specs=(
            P("phase", "fsdp", "ctx", None),
            P("phase", "fsdp", "ctx", None),
            P("phase", ("ctx", "fsdp")),
            P("phase", ("ctx", "fsdp")),
        ),
        check_vma=False,
    )
```

```python
import functools

import jax
import jax.numpy as jnp
from jax import lax
from jax.experimental import pallas as pl
from jax.experimental.pallas import tpu as pltpu
from jax.sharding import PartitionSpec as P

H = 15
KVH = 5
HD = 64
D = 960
FF = 2560
GRP = H // KVH
R = 128
SHARDS = 64
SHARD = 153600
ROWS = 1280
KEYS = 4096
CHUNK = 512
PADD = 1024
SIDE = 3
QSIDE = SIDE * GRP * HD
QPAD = 2 * QSIDE

eps = 1e-05
rope_theta = 100000.0
masked_fill = -1e30
f32 = jnp.float32
bf16 = jnp.bfloat16
ALL = ("phase", "ctx", "fsdp")

NT = (((1,), (1,)), ((), ()))


def mm(a, b):
    return jnp.dot(a, b, preferred_element_type=f32)


def mm_nt(a, b):
    return lax.dot_general(a, b, NT, preferred_element_type=f32)


STEPS = ((1, 3), (3, 1))


def swapped(block, way):
    pairs = []
    for p in range(2):
        dy, dx, dz = way(p)
        for y in range(4):
            for x in range(4):
                for z in range(4):
                    to = ((y ^ dy) * 4 + (x ^ dx)) * 4 + (z ^ dz)
                    pairs.append((p * 64 + (y * 4 + x) * 4 + z, p * 64 + to))
    return lax.ppermute(block, ALL, pairs)


def over(block, source):
    return lax.ppermute(block, "phase", [(source, 1 - source)])


def along(axes, number):
    def way(p):
        shift = [0, 0, 0]
        shift[axes[p]] = STEPS[p][number]
        return tuple(shift)

    return way


def far_z(p):
    return (0, 0, 2)


def gather_keys(kv):
    tail = kv.shape
    far = swapped(kv, far_z)
    near = kv
    orders = (((0, 1), (1, 0)), ((1, 0), (0, 1)))
    blocks = [near[None], far[None]]
    for leg in range(2):
        for number in range(2):
            if leg and number:
                blocks = list(lax.optimization_barrier(tuple(blocks)))
            for k in range(2):
                got = swapped(blocks[k], along(orders[k][leg], number))
                blocks[k] = jnp.concatenate([blocks[k], got], axis=0)
    return jnp.concatenate(blocks, axis=0).reshape(KEYS, tail[1])


def scatter_keys(d_kv):
    parts = d_kv.reshape(2, 16, R, d_kv.shape[1])
    orders = (((0, 1), (1, 0)), ((1, 0), (0, 1)))
    blocks = [parts[0], parts[1]]
    for leg in (1, 0):
        for number in (1, 0):
            for k in (1, 0):
                half = blocks[k].shape[0] // 2
                got = swapped(blocks[k][half:], along(orders[k][leg], number))
                total = blocks[k][:half].astype(f32) + got.astype(f32)
                last = k == 0 and half == 1
                blocks[k] = total if last else total.astype(bf16)
    return blocks[0][0] + swapped(blocks[1][0], far_z).astype(f32)


def slot_offsets(phase):
    return jnp.where(phase == 0, jnp.array([0, 1, 3, 2]), jnp.array([0, 3, 1, 2]))


def slot_of(offset, phase):
    at = jnp.where(phase == 0, jnp.array([0, 1, 3, 2]), jnp.array([0, 2, 3, 1]))
    return at[offset]


def key_order(y, x, zh, phase):
    off = slot_offsets(phase)
    outer = jnp.repeat(off, 4)
    inner = jnp.tile(off, 4)
    out = []
    for k in range(2):
        first_y = phase == k
        oy = jnp.where(first_y, inner, outer)
        ox = jnp.where(first_y, outer, inner)
        out.append((y ^ oy) * 8 + (x ^ ox) * 2 + (zh ^ k))
    return jnp.concatenate(out)


HALF = ROWS // 2


def gather_front(own, gains, y, phase):
    row = jnp.pad(gains[None], ((0, 15), (0, 98)))
    block = jnp.concatenate([own, row])[None]
    for number in range(2):
        block = jnp.concatenate([block, swapped(block, along((0, 0), number))])
    at = slot_of(jnp.arange(4, dtype=jnp.int32) ^ y, phase)
    front = lax.dynamic_index_in_dim(block, at[0], 0, keepdims=False)
    rows = jnp.pad(block[:, ROWS][at], ((0, 12), (0, 0)))
    blocks = [front[None, :HALF], jnp.concatenate([front[HALF:ROWS], rows])[None]]
    axes = ((1, 2), (2, 1))
    for leg in range(2):
        for number in range(2):
            for part in range(2):
                axis = axes[part][leg]
                got = swapped(blocks[part], along((axis, axis), number))
                blocks[part] = jnp.concatenate([blocks[part], got])
    return blocks


PART_ROWS = ((0, 432), (432, 864), (864, 1280))


PART_AXES = ((0, 1, 2), (1, 2, 0), (2, 0, 1))


def scatter_grads(keep, send):
    keep, send = list(keep), list(send)
    for leg in range(3):
        for number in (1, 0):
            for part, axes in enumerate(PART_AXES):
                axis = axes[leg]
                got = swapped(send[part], along((axis, axis), number))
                mine = keep[part]

                def total(at, mine=mine, got=got):
                    return mine[at].astype(f32) + got[at].astype(f32)

                if number:
                    keep[part] = total(0).astype(bf16)
                    send[part] = total(1).astype(bf16)
                elif leg < 2:
                    keep[part] = total(slice(0, 2)).astype(bf16)
                    send[part] = total(slice(2, 4)).astype(bf16)
                else:
                    keep[part] = total(slice(None))
    return jnp.concatenate(keep)


def lane_of(shape):
    return lax.broadcasted_iota(jnp.int32, shape, len(shape) - 1)


def half_swapped(block):
    lane = lane_of(block.shape)
    return jnp.where(lane % HD < HD // 2, pltpu.roll(block, 96, 1), pltpu.roll(block, 32, 1))


def qkv_weight(w_ref, c):
    return w_ref[:, 96 * c : 96 * c + 96, :].reshape(D, 128)


def normed_of(u, gain):
    scale = lax.rsqrt(jnp.mean(u * u, axis=-1, keepdims=True) + eps)
    return scale, (u * scale * gain).astype(bf16)


def front_weight(idx_ref, wa_ref, wb_ref, c):
    pieces = []
    for d in range(10):
        low, high = 96 * c, 96 * c + 96
        if low < HALF:
            pieces.append(wa_ref[idx_ref[d], low : min(high, HALF), :])
        if high > HALF:
            pieces.append(wb_ref[idx_ref[16 + d], max(low, HALF) - HALF : high - HALF, :])
    return jnp.concatenate(pieces, axis=0)


def project_kernel(idx_ref, u_ref, g_ref, cos_ref, sin_ref, wa_ref, wb_ref, qt_ref, kv_ref):
    u = u_ref[...].astype(f32)
    _, a = normed_of(u, g_ref[...])
    cos, sin = cos_ref[...], sin_ref[...]
    blocks = []
    for c in range(0, 13, 2):
        w = front_weight(idx_ref, wa_ref, wb_ref, c)
        if c + 1 < 13:
            w = jnp.concatenate([w, front_weight(idx_ref, wa_ref, wb_ref, c + 1)], axis=1)
        y = mm(a, w)
        for k in range(w.shape[1] // 128):
            b = y[:, 128 * k : 128 * k + 128]
            if c + k < 10:
                b = b * cos + half_swapped(b) * sin
            blocks.append(b)
    for c in range(8):
        t = (blocks[c].astype(bf16).astype(f32) * 0.125).T.astype(bf16)
        count = 128 if c < 7 else 64
        qt_ref[128 * c : 128 * c + count, :] = t[:count]
    qt_ref[D:, :] = jnp.zeros((QPAD - D, R), bf16)
    kv_ref[:, 640:] = jnp.zeros((R, 128), bf16)
    lane = lane_of((R, 128))
    for g in range(KVH):
        k, v = blocks[(15 + g) // 2], blocks[(20 + g) // 2]
        if (15 + g) % 2:
            k = pltpu.roll(k, 64, 1)
        if (20 + g) % 2 == 0:
            v = pltpu.roll(v, 64, 1)
        kv_ref[:, 128 * g : 128 * g + 128] = jnp.where(lane < 64, k, v).astype(bf16)


def project(u, gain, cos, sin, idx, front):
    whole = lambda *shape: pl.BlockSpec(shape, lambda i, idx: (0,) * len(shape))
    return pl.pallas_call(
        project_kernel,
        name="project",
        grid_spec=pltpu.PrefetchScalarGridSpec(
            num_scalar_prefetch=1,
            grid=(1,),
            in_specs=[
                whole(R, D),
                whole(1, D),
                whole(R, 128),
                whole(R, 128),
                whole(16, HALF, 128),
                whole(16, HALF + 16, 128),
            ],
            out_specs=[whole(QPAD, R), whole(R, 768)],
        ),
        out_shape=[
            jax.ShapeDtypeStruct((QPAD, R), bf16),
            jax.ShapeDtypeStruct((R, 768), bf16),
        ],
        compiler_params=pltpu.CompilerParams(vmem_limit_bytes=48 << 20),
        cost_estimate=pl.CostEstimate(flops=400_000_000, bytes_accessed=6_000_000, transcendentals=0),
    )(idx, u, gain, cos, sin, *front)


def heads_wide(ref, low):
    top = jnp.concatenate([ref[64 * h : 64 * h + 64, :] for h in range(GRP)], axis=1)
    zero = jnp.zeros_like(top)
    return jnp.concatenate([top, zero] if low else [zero, top], axis=0)


def attend_kernel(qt_ref, kv_ref, bias_ref, mixed_ref, lse_ref, s_ref):
    q = heads_wide(qt_ref, True)
    peak = jnp.full((1, GRP * R), masked_fill, f32)
    for i in range(KEYS // CHUNK):
        rows = slice(CHUNK * i, CHUNK * i + CHUNK)
        b = bias_ref[rows, :]
        s = mm(kv_ref[rows, :], q) + jnp.concatenate([b, b, b], axis=1)
        s_ref[rows, :] = s
        peak = jnp.maximum(peak, jnp.max(s, axis=0, keepdims=True))
    total = jnp.zeros((1, GRP * R), f32)
    acc = jnp.zeros((128, GRP * R), f32)
    for i in range(KEYS // CHUNK):
        rows = slice(CHUNK * i, CHUNK * i + CHUNK)
        p = jnp.exp(s_ref[rows, :] - peak)
        total = total + jnp.sum(p, axis=0, keepdims=True)
        acc = acc + mm(kv_ref[rows, :].T, p.astype(bf16))
    lse_ref[0] = peak + jnp.log(total)
    o = (acc[64:] / total).astype(bf16)
    for h in range(GRP):
        mixed_ref[64 * h : 64 * h + 64, :] = o[:, 128 * h : 128 * h + 128]


def attend(qt, kv_all, bias):
    return pl.pallas_call(
        attend_kernel,
        name="attend",
        grid=(SIDE,),
        in_specs=[
            pl.BlockSpec((GRP * HD, R), lambda g: (g, 0)),
            pl.BlockSpec((KEYS, 128), lambda g: (0, g)),
            pl.BlockSpec((KEYS, R), lambda g: (0, 0)),
        ],
        out_specs=[
            pl.BlockSpec((GRP * HD, R), lambda g: (g, 0)),
            pl.BlockSpec((1, 1, GRP * R), lambda g: (g, 0, 0)),
        ],
        out_shape=[
            jax.ShapeDtypeStruct((QSIDE, R), bf16),
            jax.ShapeDtypeStruct((SIDE, 1, GRP * R), f32),
        ],
        scratch_shapes=[pltpu.VMEM((KEYS, GRP * R), f32)],
        compiler_params=pltpu.CompilerParams(vmem_limit_bytes=48 << 20),
        cost_estimate=pl.CostEstimate(
            flops=4_000_000_000, bytes_accessed=8_000_000, transcendentals=7_900_000
        ),
    )(qt, kv_all, bias)


def out_weight(refs, c):
    return jnp.concatenate(
        [ref[:, 160 * c : 160 * c + 160, :].reshape(320, 128) for ref in refs], axis=0
    )


def gu_weight(refs, c):
    gl, gh, ul, uh = refs
    gate = jnp.concatenate([gl[:, c].reshape(512, 128), gh[:, c].reshape(512, 128)], axis=0)
    up = jnp.concatenate([ul[:, c].reshape(512, 128), uh[:, c].reshape(512, 128)], axis=0)
    return jnp.concatenate([gate, up], axis=1)


def down_weight(ref, c):
    return ref[:, 160 * c : 160 * c + 160, :].reshape(640, 128)


WEIGHT_SPECS = (
    [pl.BlockSpec((2, ROWS, 128), lambda j, k=k: (5 + k, 0, 0)) for k in range(3)]
    + [
        pl.BlockSpec((16, 5, 32, 128), lambda j, d=d, o=o: (1 + d, o + j, 0, 0))
        for o in (0, 4)
        for d in (0, 1)
    ]
    + [pl.BlockSpec((4, ROWS, 128), lambda j: (12 + j, 0, 0))]
)


def weight_args(gathered):
    fine = gathered.reshape(SHARDS, 40, 32, 128)
    return [gathered] * 3 + [fine] * 4 + [gathered]


def feed_kernel(
    mixed_ref, u_ref, g_ref, pad_ref, o0, o1, o2, gl, gh, ul, uh, wd,
    y_ref, h_ref, nt_ref, gate_ref, up_ref, mt_ref, n_scr, y_scr,
):
    step = pl.program_id(0)

    @pl.when(step == 0)
    def _():
        mixed = mixed_ref[...].T
        for c in range(0, 8, 2):
            w = jnp.concatenate(
                [out_weight((o0, o1, o2), c), out_weight((o0, o1, o2), c + 1)], axis=1
            )
            y = mm(mixed, w)
            end = min(128 * c + 256, D)
            h_ref[:, 128 * c : end] = u_ref[:, 128 * c : end].astype(f32) + y[:, : end - 128 * c]
        _, n = normed_of(h_ref[...], g_ref[...])
        padded = mm(n, pad_ref[...])
        n_scr[...] = padded.astype(bf16)
        nt_ref[...] = padded.T.astype(bf16)
        y_scr[...] = jnp.zeros_like(y_scr)

    n = n_scr[...]
    inner = []
    for c in range(5):
        gu = mm(n, gu_weight((gl, gh, ul, uh), c))
        gate, up = gu[:, :128], gu[:, 128:]
        cols = slice(128 * c, 128 * c + 128)
        gate_ref[:, cols] = gate
        up_ref[:, cols] = up
        m = gate * jax.nn.sigmoid(gate) * up
        mt_ref[cols, :] = m.T.astype(bf16)
        inner.append(m.astype(bf16))
    inner = jnp.concatenate(inner, axis=1)
    for c in range(0, 8, 2):
        w = jnp.concatenate([down_weight(wd, c), down_weight(wd, c + 1)], axis=1)
        y_scr[:, 128 * c : 128 * c + 256] += mm(inner, w)

    @pl.when(step == 3)
    def _():
        y_ref[...] = (h_ref[...] + y_scr[:, :D]).astype(bf16)


def feed(mixed, u, gain, pad, gathered):
    whole = lambda *shape: pl.BlockSpec(shape, lambda j: (0,) * len(shape))
    return pl.pallas_call(
        feed_kernel,
        name="feed",
        grid=(4,),
        in_specs=[whole(D, R), whole(R, D), whole(1, D), whole(D, PADD)] + WEIGHT_SPECS,
        out_specs=[
            whole(R, D),
            whole(R, D),
            whole(PADD, R),
            pl.BlockSpec((R, 640), lambda j: (0, j)),
            pl.BlockSpec((R, 640), lambda j: (0, j)),
            pl.BlockSpec((640, R), lambda j: (j, 0)),
        ],
        out_shape=[
            jax.ShapeDtypeStruct((R, D), bf16),
            jax.ShapeDtypeStruct((R, D), f32),
            jax.ShapeDtypeStruct((PADD, R), bf16),
            jax.ShapeDtypeStruct((R, FF), f32),
            jax.ShapeDtypeStruct((R, FF), f32),
            jax.ShapeDtypeStruct((FF, R), bf16),
        ],
        scratch_shapes=[pltpu.VMEM((R, PADD), bf16), pltpu.VMEM((R, PADD), f32)],
        compiler_params=pltpu.CompilerParams(vmem_limit_bytes=48 << 20),
        cost_estimate=pl.CostEstimate(
            flops=2_200_000_000, bytes_accessed=22_000_000, transcendentals=400_000
        ),
    )(mixed, u, gain, pad, *weight_args(gathered))


def norm_back(d_out, values, gain):
    scales = lax.rsqrt(jnp.mean(values * values, axis=-1, keepdims=True) + eps)
    scaled = d_out * gain
    d_gain = jnp.sum(d_out * values * scales, axis=0, keepdims=True)
    d_values = scales * scaled - values * (scales * scales * scales) * jnp.mean(
        scaled * values, axis=-1, keepdims=True
    )
    return d_values, d_gain


def feed_back_kernel(
    c_ref, gate_ref, up_ref, h_ref, g_ref, pad_ref, o0, o1, o2, gl, gh, ul, uh, wd,
    dgate_ref, dup_ref, dh_ref, dhb_ref, dg_ref, dot_ref, cb_ref, dn_scr,
):
    step = pl.program_id(0)

    @pl.when(step == 0)
    def _():
        cb_ref[...] = jnp.zeros_like(cb_ref)
        cb_ref[:, :D] = c_ref[...].astype(bf16)
        dn_scr[...] = jnp.zeros_like(dn_scr)

    d_inner = jnp.zeros((R, 640), f32)
    for c in range(0, 8, 2):
        w = jnp.concatenate([down_weight(wd, c), down_weight(wd, c + 1)], axis=1)
        d_inner = d_inner + mm_nt(cb_ref[:, 128 * c : 128 * c + 256], w)
    for c in range(5):
        cols = slice(128 * c, 128 * c + 128)
        gate, up, dm = gate_ref[:, cols], up_ref[:, cols], d_inner[:, cols]
        sigma = jax.nn.sigmoid(gate)
        d_gate = (dm * up * sigma * (1.0 + gate * (1.0 - sigma))).astype(bf16)
        d_up = (dm * gate * sigma).astype(bf16)
        dgate_ref[:, cols] = d_gate
        dup_ref[:, cols] = d_up
        both = jnp.concatenate([d_gate, d_up], axis=1)
        dn_scr[...] += mm_nt(both, gu_weight((gl, gh, ul, uh), c))

    @pl.when(step == 3)
    def _():
        padded = dn_scr[...]
        high = padded.astype(bf16)
        low = (padded - high.astype(f32)).astype(bf16)
        dn = mm_nt(high, pad_ref[...]) + mm_nt(low, pad_ref[...])
        d_h, d_gain = norm_back(dn, h_ref[...], g_ref[...])
        d_h = c_ref[...] + d_h
        dg_ref[...] = d_gain
        dh_ref[...] = d_h
        dhb_ref[...] = jnp.zeros_like(dhb_ref)
        dhb_ref[:, :D] = d_h.astype(bf16)
        d_mixed = jnp.zeros((R, D), f32)
        for c in range(0, 8, 2):
            w = jnp.concatenate(
                [out_weight((o0, o1, o2), c), out_weight((o0, o1, o2), c + 1)], axis=1
            )
            d_mixed = d_mixed + mm_nt(dhb_ref[:, 128 * c : 128 * c + 256], w)
        dot_ref[:D, :] = d_mixed.T
        dot_ref[D:, :] = jnp.zeros((QPAD - D, R), f32)


def feed_back(cot, gate, up, hidden, gain, pad, gathered):
    whole = lambda *shape: pl.BlockSpec(shape, lambda j: (0,) * len(shape))
    block = pl.BlockSpec((R, 640), lambda j: (0, j))
    return pl.pallas_call(
        feed_back_kernel,
        name="feed_back",
        grid=(4,),
        in_specs=[whole(R, D), block, block, whole(R, D), whole(1, D), whole(D, PADD)]
        + WEIGHT_SPECS,
        out_specs=[
            block,
            block,
            whole(R, D),
            whole(R, PADD),
            whole(1, D),
            whole(QPAD, R),
            whole(R, PADD),
        ],
        out_shape=[
            jax.ShapeDtypeStruct((R, FF), bf16),
            jax.ShapeDtypeStruct((R, FF), bf16),
            jax.ShapeDtypeStruct((R, D), f32),
            jax.ShapeDtypeStruct((R, PADD), bf16),
            jax.ShapeDtypeStruct((1, D), f32),
            jax.ShapeDtypeStruct((QPAD, R), f32),
            jax.ShapeDtypeStruct((R, PADD), bf16),
        ],
        scratch_shapes=[pltpu.VMEM((R, PADD), f32)],
        compiler_params=pltpu.CompilerParams(vmem_limit_bytes=48 << 20),
        cost_estimate=pl.CostEstimate(
            flops=2_200_000_000, bytes_accessed=22_000_000, transcendentals=400_000
        ),
    )(cot, gate, up, hidden, gain, pad, *weight_args(gathered))


def attend_back_kernel(
    qt_ref, kv_ref, bias_ref, dot_ref, mixed_ref, lse_ref, dkv_ref, dqt_ref
):
    q = heads_wide(qt_ref, True)
    d_o = heads_wide(dot_ref, False)
    o = heads_wide(mixed_ref, False)
    delta = jnp.sum(d_o * o.astype(f32), axis=0, keepdims=True)
    d_o = d_o.astype(bf16)
    lse = lse_ref[0]
    both = jnp.concatenate([q, d_o], axis=1)
    acc = jnp.zeros((128, GRP * R), f32)
    for i in range(KEYS // CHUNK):
        rows = slice(CHUNK * i, CHUNK * i + CHUNK)
        b = bias_ref[rows, :]
        kv = kv_ref[rows, :]
        p = jnp.exp(mm(kv, q) + jnp.concatenate([b, b, b], axis=1) - lse)
        ds = (p * (mm(kv, d_o) - delta)).astype(bf16)
        dkv_ref[rows, :] = mm_nt(jnp.concatenate([ds, p.astype(bf16)], axis=1), both).astype(bf16)
        acc = acc + mm(kv.T, ds)
    acc = acc[:64] * 0.125
    for h in range(GRP):
        dqt_ref[64 * h : 64 * h + 64, :] = acc[:, 128 * h : 128 * h + 128]


def attend_back(qt, kv_all, bias, d_mixed, mixed, lse):
    heads = pl.BlockSpec((GRP * HD, R), lambda g: (g, 0))
    return pl.pallas_call(
        attend_back_kernel,
        name="attend_back",
        grid=(SIDE,),
        in_specs=[
            heads,
            pl.BlockSpec((KEYS, 128), lambda g: (0, g)),
            pl.BlockSpec((KEYS, R), lambda g: (0, 0)),
            heads,
            heads,
            pl.BlockSpec((1, 1, GRP * R), lambda g: (g, 0, 0)),
        ],
        out_specs=[pl.BlockSpec((KEYS, 128), lambda g: (0, g)), heads],
        out_shape=[
            jax.ShapeDtypeStruct((KEYS, SIDE * 128), bf16),
            jax.ShapeDtypeStruct((QSIDE, R), f32),
        ],
        compiler_params=pltpu.CompilerParams(vmem_limit_bytes=48 << 20),
        cost_estimate=pl.CostEstimate(
            flops=10_000_000_000, bytes_accessed=14_000_000, transcendentals=7_900_000
        ),
    )(qt, kv_all, bias, d_mixed, mixed, lse)


def project_back_kernel(
    dqt_ref, dkv_ref, cos_ref, sin_ref, u_ref, g_ref, dh_ref, w_ref,
    du_ref, dqkv_ref, at_ref, dg_ref,
):
    cos, sin = cos_ref[...], sin_ref[...]
    lane = lane_of((R, 128))
    dkv = [dkv_ref[:, 128 * g : 128 * g + 128] for g in range(KVH)]
    rolled = [pltpu.roll(b, 64, 1) for b in dkv]
    zero = jnp.zeros((R, 128), f32)
    blocks = [dqt_ref[128 * c : 128 * c + 128, :].T for c in range(7)]
    last = jnp.concatenate([dqt_ref[896:960, :], jnp.zeros((64, R), f32)], axis=0).T
    low = lane < 64
    blocks.append(jnp.where(low, last, rolled[0]))
    blocks.append(jnp.where(low, dkv[1], rolled[2]))
    blocks.append(jnp.where(low, dkv[3], rolled[4]))
    blocks = [b * cos - half_swapped(b) * sin for b in blocks]
    blocks.append(jnp.where(low, rolled[0], dkv[1]))
    blocks.append(jnp.where(low, rolled[2], dkv[3]))
    blocks.append(jnp.where(low, rolled[4], zero))
    da = jnp.zeros((R, D), f32)
    for c in range(0, 13, 2):
        if c + 1 < 13:
            d = jnp.concatenate([blocks[c], blocks[c + 1]], axis=1).astype(bf16)
            w = jnp.concatenate([qkv_weight(w_ref, c), qkv_weight(w_ref, c + 1)], axis=1)
        else:
            d, w = blocks[c].astype(bf16), qkv_weight(w_ref, c)
        dqkv_ref[:, 128 * c : 128 * c + d.shape[1]] = d
        da = da + mm_nt(d, w)
    u = u_ref[...].astype(f32)
    gain = g_ref[...]
    _, a = normed_of(u, gain)
    at_ref[...] = a.T
    d_u, d_gain = norm_back(da, u, gain)
    dg_ref[...] = d_gain
    du_ref[...] = dh_ref[...] + d_u


def project_back(d_query, d_kv, cos, sin, u, gain, d_hidden, weights):
    whole = lambda *shape: pl.BlockSpec(shape, lambda j: (0,) * len(shape))
    return pl.pallas_call(
        project_back_kernel,
        name="project_back",
        grid=(1,),
        in_specs=[
            whole(D, R),
            whole(R, 640),
            whole(R, 128),
            whole(R, 128),
            whole(R, D),
            whole(1, D),
            whole(R, D),
            whole(10, ROWS, 128),
        ],
        out_specs=[whole(R, D), whole(R, 13 * 128), whole(D, R), whole(1, D)],
        out_shape=[
            jax.ShapeDtypeStruct((R, D), f32),
            jax.ShapeDtypeStruct((R, 13 * 128), bf16),
            jax.ShapeDtypeStruct((D, R), bf16),
            jax.ShapeDtypeStruct((1, D), f32),
        ],
        compiler_params=pltpu.CompilerParams(vmem_limit_bytes=48 << 20),
        cost_estimate=pl.CostEstimate(flops=400_000_000, bytes_accessed=5_000_000, transcendentals=0),
    )(d_query, d_kv, cos, sin, u, gain, d_hidden, weights)


def outer_kernel(
    slot_ref, at_ref, dqkv_ref, mixed_ref, dhb_ref, nt_ref, dgate_ref, dup_ref, mt_ref, cb_ref,
    gain_ref, k0, k1, k2, s0, s1, s2, stage, sems,
):
    step = pl.program_id(0)
    buf = step % 2
    slot_y, slot_x = slot_ref[step // 4], slot_ref[4 + step % 4]
    zslot = [slot_ref[8 + k] for k in range(4)]
    out_ref = stage.at[buf]
    (a0, b0), (a1, b1), (a2, b2) = PART_ROWS

    def copy(i, buf, half=0):
        src = stage.at[buf]
        if i == 0:
            src, dst = src.at[:, a0:b0], (k0, s0)[half].at[slot_y % 2, slot_x]
        elif i == 1:
            src, dst = src.at[:, a1:b1], (k1, s1)[half].at[slot_x % 2, :, slot_y]
        elif i == 2:
            src, dst = src.at[0:2, a2:b2], k2.at[:, slot_y, slot_x]
        else:
            src, dst = src.at[2:4, a2:b2], s2.at[:, slot_y, slot_x]
        return pltpu.make_async_copy(src, dst, sems.at[buf, i])

    @pl.when(step >= 2)
    def _():
        for i in range(4):
            copy(i, buf).wait()

    def row_of(k, count, at):
        row = lax.broadcasted_iota(jnp.int32, (count, 128), 0)
        return jnp.where(row == at, gain_ref[pl.ds(4 * step + k, 1), :], 0.0)

    def narrow(start, ks):
        count = len(ks)
        rows = at_ref[pl.ds(pl.multiple_of(start, 32), 96 * count), :]
        for c in range(0, 13, 2):
            width = min(256, 1664 - 128 * c)
            res = mm(rows, dqkv_ref[:, 128 * c : 128 * c + width])
            for i, k in enumerate(ks):
                for h in range(width // 128):
                    out_ref[zslot[k], 96 * (c + h) : 96 * (c + h) + 96, :] = res[
                        96 * i : 96 * i + 96, 128 * h : 128 * h + 128
                    ].astype(bf16)
        for k in ks:
            out_ref[zslot[k], 1248:1280, :] = row_of(k, 32, 0).astype(bf16)

    def wide(ref, start, cot_ref, ks):
        rows = ref[pl.ds(pl.multiple_of(start, 32), 160 * len(ks)), :]
        for c in range(0, 8, 2):
            res = mm(rows, cot_ref[:, 128 * c : 128 * c + 256])
            for i, k in enumerate(ks):
                for h in range(2):
                    b = res[160 * i : 160 * i + 160, 128 * h : 128 * h + 128]
                    if c + h == 7:
                        b = b + row_of(k, 160, 0)
                    at = 160 * (c + h)
                    out_ref[zslot[k], at : at + 160, :] = b.astype(bf16)

    @pl.when(step < 2)
    def _():
        narrow(384 * step, (0, 1, 2, 3))

    @pl.when(step == 2)
    def _():
        narrow(768, (0, 1))
        wide(mixed_ref, 0, dhb_ref, (2, 3))

    @pl.when(step == 3)
    def _():
        wide(mixed_ref, 320, dhb_ref, (0, 1, 2, 3))

    @pl.when((step >= 4) & (step < 12))
    def _():
        rows = nt_ref[pl.ds(pl.multiple_of(128 * (step - 4), 128), 128), :]
        for part, ref in enumerate((dgate_ref, dup_ref)):
            for c in range(0, 20, 2):
                res = mm(rows, ref[:, 128 * c : 128 * c + 256])
                for k in range(4):
                    for h in range(2):
                        b = res[32 * k : 32 * k + 32, 128 * h : 128 * h + 128]
                        at = 32 * (20 * part + c + h)
                        if at == 0:
                            b = b + row_of(k, 32, 30)
                        out_ref[zslot[k], at : at + 32, :] = b.astype(bf16)

    @pl.when(step >= 12)
    def _():
        wide(mt_ref, 640 * (step - 12), cb_ref, (0, 1, 2, 3))

    for half in range(2):

        @pl.when(slot_y // 2 == half)
        def _(half=half):
            copy(0, buf, half).start()

        @pl.when(slot_x // 2 == half)
        def _(half=half):
            copy(1, buf, half).start()

    copy(2, buf).start()
    copy(3, buf).start()

    @pl.when(step == 15)
    def _():
        for last in (0, 1):
            for i in range(4):
                copy(i, last).wait()


def outer(slots, at, dqkv, mixed, dhb, nt, dgate, dup, mt, cb, gains):
    whole = lambda v: pl.BlockSpec(v.shape, lambda s, slot: (0,) * v.ndim)
    args = (at, dqkv, mixed, dhb, nt, dgate, dup, mt, cb, gains)
    shapes = [
        jax.ShapeDtypeStruct((2, 4, 4, end - begin, 128), bf16) for begin, end in PART_ROWS
    ]
    out = pl.pallas_call(
        outer_kernel,
        name="outer",
        grid_spec=pltpu.PrefetchScalarGridSpec(
            num_scalar_prefetch=1,
            grid=(16,),
            in_specs=[whole(v) for v in args],
            out_specs=[pl.BlockSpec(memory_space=pl.ANY)] * 6,
            scratch_shapes=[
                pltpu.VMEM((2, 4, ROWS, 128), bf16),
                pltpu.SemaphoreType.DMA((2, 4)),
            ],
        ),
        out_shape=shapes * 2,
        compiler_params=pltpu.CompilerParams(vmem_limit_bytes=48 << 20),
        cost_estimate=pl.CostEstimate(
            flops=2_600_000_000, bytes_accessed=24_000_000, transcendentals=0
        ),
    )(slots, *args)
    return out[:3], out[3:]


def shard_kind(rank):
    return jnp.where(rank < 10, 0, jnp.where((rank >= 16) & (rank < 48), 2, 1))


def shard_blocks(flat, rank):
    def narrow(_):
        w = jnp.pad(flat.reshape(96, 1600), ((0, 0), (0, 64)))
        w = w.reshape(96, 13, 128).transpose(1, 0, 2).reshape(1248, 128)
        return jnp.pad(w, ((0, 32), (0, 0)))

    def square(_):
        w = jnp.pad(flat.reshape(160, 960), ((0, 0), (0, 64)))
        return w.reshape(160, 8, 128).transpose(1, 0, 2).reshape(ROWS, 128)

    def broad(_):
        w = jnp.pad(flat.reshape(30, 40, 128), ((0, 2), (0, 0), (0, 0)))
        return w.transpose(1, 0, 2).reshape(ROWS, 128)

    return lax.switch(shard_kind(rank), [narrow, square, broad], 0)


def blocks_shard(blocks, rank):
    def narrow(_):
        w = blocks[:1248].reshape(13, 96, 128).transpose(1, 0, 2).reshape(96, 1664)[:, :1600]
        return w.reshape(SHARD), blocks[1248, :30]

    def square(_):
        w = blocks.reshape(8, 160, 128).transpose(1, 0, 2).reshape(160, 1024)[:, :960]
        return w.reshape(SHARD), blocks[1120, 64:94]

    def broad(_):
        w = blocks.reshape(40, 32, 128).transpose(1, 0, 2)[:30]
        return w.reshape(SHARD), blocks[30, :30]

    return lax.switch(shard_kind(rank), [narrow, square, broad], 0)


def per_device(layer_in, out_grad, segment_ids, block_pair, params, norm_gains):
    phase = lax.axis_index("phase")
    ctx = lax.axis_index("ctx")
    rank = ctx * 2 + lax.axis_index("fsdp")
    y, x, z = rank // 16, (rank // 4) % 4, rank % 4
    zh = z // 2

    own = shard_blocks(params[0], rank)
    gathered = lax.all_gather(own, ("ctx", "fsdp"), axis=0)

    seg_row = segment_ids[0]
    pair = lax.dynamic_index_in_dim(block_pair, ctx, 0, keepdims=False)
    within = jnp.arange(HD, dtype=jnp.int32)
    place_q = jnp.concatenate([pair * 64 + within, (63 - pair) * 64 + within])
    seg_q = jnp.concatenate(
        [
            lax.dynamic_slice_in_dim(seg_row, pair * 64, 64),
            lax.dynamic_slice_in_dim(seg_row, (63 - pair) * 64, 64),
        ]
    )
    start_q = jnp.sum((seg_row[:, None] < seg_q[None, :]).astype(jnp.int32), axis=0)
    pairs_k = block_pair[key_order(y, x, zh, phase)]
    place_k = (
        jnp.stack([pairs_k, 63 - pairs_k], axis=1)[:, :, None] * 64 + within[None, None, :]
    ).reshape(KEYS)
    bias = jnp.where(
        (place_k[:, None] <= place_q[None, :]) & (place_k[:, None] >= start_q[None, :]),
        0.0,
        masked_fill,
    ).astype(f32)
    frequency = rope_theta ** (-2.0 * jnp.arange(HD // 2, dtype=f32) / HD)
    angles = (place_q - start_q).astype(f32)[:, None] * frequency[None, :]
    cosine, sine = jnp.cos(angles), jnp.sin(angles)
    cos = jnp.concatenate([cosine] * 4, axis=1)
    sin = jnp.concatenate([-sine, sine, -sine, sine], axis=1)
    spread = jnp.arange(PADD, dtype=jnp.int32)
    target = jnp.where(spread % 32 < 30, (spread // 32) * 30 + spread % 32, -1)
    pad = (jnp.arange(D, dtype=jnp.int32)[:, None] == target[None, :]).astype(bf16)

    front = gather_front(own, norm_gains[0], y, phase)
    four = jnp.arange(4, dtype=jnp.int32)
    slots_y, slots_x, slots_z = (slot_of(four ^ at_axis, phase) for at_axis in (y, x, z))
    idx = jnp.concatenate(
        [
            (slots_x[:, None] + 4 * slots_z[None, :]).reshape(16),
            (4 * slots_x[:, None] + slots_z[None, :]).reshape(16),
        ]
    )
    gains = front[1][:, HALF : HALF + 4, :30][idx[16:]].astype(f32)
    gains = gains.transpose(1, 0, 2).reshape(1, 2 * D)
    gain_one, gain_two = gains[:, :D], gains[:, D:]
    first = phase == 0

    u = layer_in[0]
    mixed = None
    kept = []
    for tick in range(2):
        active = phase == tick
        qt, kv = project(u, gain_one, cos, sin, idx, front)
        kv_side = jnp.where(active, kv[:, :384], over(kv[:, 384:], tick))
        qt_side = jnp.where(active, qt[:QSIDE], over(qt[QSIDE:], tick))
        kv_all = gather_keys(kv_side)
        mixed_side, lse = attend(qt_side, kv_all, bias)
        kept.append((qt_side, kv_all, mixed_side, lse))
        far = over(mixed_side[: D - QSIDE], 1 - tick)
        whole = jnp.concatenate([mixed_side, far])
        mixed = whole if tick == 0 else jnp.where(active, whole, mixed)
        result, hidden, nt, gate, up, mt = feed(mixed, u, gain_two, pad, gathered)
        if tick == 0:
            u = jnp.where(first, u, over(result, 0))

    cot = out_grad[0]
    d_query = d_kv = None
    for tick in range(2):
        layer = 1 - tick
        active = phase == layer
        qt_side, kv_all, mixed_side, lse = kept[layer]
        dgate, dup, dh, dhb, dg_two, d_mixed, cb = feed_back(
            cot, gate, up, hidden, gain_two, pad, gathered
        )
        d_side = jnp.where(active, d_mixed[:QSIDE], over(d_mixed[QSIDE:], layer))
        d_kv_all, dq_side = attend_back(qt_side, kv_all, bias, d_side, mixed_side, lse)
        dq_new = jnp.concatenate([dq_side, over(dq_side[: D - QSIDE], tick)])
        dkv_side = scatter_keys(d_kv_all)
        dkv_new = jnp.concatenate([dkv_side, over(dkv_side[:, :256], tick)], axis=1)
        d_query = dq_new if tick == 0 else jnp.where(active, dq_new, d_query)
        d_kv = dkv_new if tick == 0 else jnp.where(active, dkv_new, d_kv)
        d_u, dqkv, at, dg_one = project_back(
            d_query, d_kv, cos, sin, u, gain_one, dh, gathered
        )
        if tick == 0:
            cot = jnp.where(first, over(d_u.astype(bf16), 1).astype(f32), cot)

    gains = jnp.concatenate([dg_one, dg_two], axis=1).reshape(SHARDS, 30)
    shards = jnp.arange(SHARDS, dtype=jnp.int32)
    square = (((shards >= 10) & (shards < 16)) | (shards >= 48))[:, None]
    gains = jnp.where(
        square, jnp.pad(gains, ((0, 0), (64, 34))), jnp.pad(gains, ((0, 0), (0, 98)))
    )
    slots = jnp.concatenate([slots_y, slots_x, slots_z])
    keep, send = outer(slots, at, dqkv, mixed, dhb, nt, dgate, dup, mt, cb, gains)
    total = scatter_grads(keep, send)
    param_part, gain_part = blocks_shard(total, rank)
    return (result[None, None], d_u[None, None], param_part[None], gain_part[None])


def solution(mesh):
    return jax.shard_map(
        per_device,
        mesh=mesh,
        in_specs=(
            P("fsdp", "ctx", None),
            P("fsdp", "ctx", None),
            P("fsdp", None),
            P(),
            P("phase", ("ctx", "fsdp")),
            P("phase", ("ctx", "fsdp")),
        ),
        out_specs=(
            P("phase", "fsdp", "ctx", None),
            P("phase", "fsdp", "ctx", None),
            P("phase", ("ctx", "fsdp")),
            P("phase", ("ctx", "fsdp")),
        ),
        check_vma=False,
    )
```

```python
import functools

import jax
import jax.numpy as jnp
from jax import lax
from jax.experimental import pallas as pl
from jax.experimental.pallas import tpu as pltpu
from jax.sharding import PartitionSpec as P

H = 15
KVH = 5
HD = 64
D = 960
FF = 2560
GRP = H // KVH
R = 128
SHARDS = 64
SHARD = 153600
ROWS = 1280
KEYS = 4096
CHUNK = 512
PADD = 1024
SIDE = 3
QSIDE = SIDE * GRP * HD
QPAD = 2 * QSIDE

eps = 1e-05
rope_theta = 100000.0
masked_fill = -1e30
f32 = jnp.float32
bf16 = jnp.bfloat16
ALL = ("phase", "ctx", "fsdp")

NT = (((1,), (1,)), ((), ()))


def mm(a, b):
    return jnp.dot(a, b, preferred_element_type=f32)


def mm_nt(a, b):
    return lax.dot_general(a, b, NT, preferred_element_type=f32)


STEPS = ((1, 3), (3, 1))


def swapped(block, way):
    pairs = []
    for p in range(2):
        dy, dx, dz = way(p)
        for y in range(4):
            for x in range(4):
                for z in range(4):
                    to = ((y ^ dy) * 4 + (x ^ dx)) * 4 + (z ^ dz)
                    pairs.append((p * 64 + (y * 4 + x) * 4 + z, p * 64 + to))
    return lax.ppermute(block, ALL, pairs)


def over(block, source):
    return lax.ppermute(block, "phase", [(source, 1 - source)])


def along(axes, number):
    def way(p):
        shift = [0, 0, 0]
        shift[axes[p]] = STEPS[p][number]
        return tuple(shift)

    return way


def far_z(p):
    return (0, 0, 2)


def gather_keys(kv):
    tail = kv.shape
    far = swapped(kv, far_z)
    near = kv
    orders = (((0, 1), (1, 0)), ((1, 0), (0, 1)))
    blocks = [near[None], far[None]]
    for leg in range(2):
        for number in range(2):
            if leg and number:
                blocks = list(lax.optimization_barrier(tuple(blocks)))
            for k in range(2):
                got = swapped(blocks[k], along(orders[k][leg], number))
                blocks[k] = jnp.concatenate([blocks[k], got], axis=0)
    return jnp.concatenate(blocks, axis=0).reshape(KEYS, tail[1])


def scatter_keys(d_kv):
    parts = d_kv.reshape(2, 16, R, d_kv.shape[1])
    orders = (((0, 1), (1, 0)), ((1, 0), (0, 1)))
    blocks = [parts[0], parts[1]]
    for leg in (1, 0):
        for number in (1, 0):
            for k in (1, 0):
                half = blocks[k].shape[0] // 2
                got = swapped(blocks[k][half:], along(orders[k][leg], number))
                total = blocks[k][:half].astype(f32) + got.astype(f32)
                last = k == 0 and half == 1
                blocks[k] = total if last else total.astype(bf16)
    return blocks[0][0] + swapped(blocks[1][0], far_z).astype(f32)


def slot_offsets(phase):
    return jnp.where(phase == 0, jnp.array([0, 1, 3, 2]), jnp.array([0, 3, 1, 2]))


def slot_of(offset, phase):
    at = jnp.where(phase == 0, jnp.array([0, 1, 3, 2]), jnp.array([0, 2, 3, 1]))
    return at[offset]


def key_order(y, x, zh, phase):
    off = slot_offsets(phase)
    outer = jnp.repeat(off, 4)
    inner = jnp.tile(off, 4)
    out = []
    for k in range(2):
        first_y = phase == k
        oy = jnp.where(first_y, inner, outer)
        ox = jnp.where(first_y, outer, inner)
        out.append((y ^ oy) * 8 + (x ^ ox) * 2 + (zh ^ k))
    return jnp.concatenate(out)


HALF = ROWS // 2


def gather_front(own, gains, y, phase):
    row = jnp.pad(gains[None], ((0, 15), (0, 98)))
    block = jnp.concatenate([own, row])[None]
    for number in range(2):
        block = jnp.concatenate([block, swapped(block, along((0, 0), number))])
    block, own = lax.optimization_barrier((block, own))
    at = slot_of(jnp.arange(4, dtype=jnp.int32) ^ y, phase)
    front = lax.dynamic_index_in_dim(block, at[0], 0, keepdims=False)
    rows = jnp.pad(block[:, ROWS][at], ((0, 12), (0, 0)))
    blocks = [front[None, :HALF], jnp.concatenate([front[HALF:ROWS], rows])[None]]
    axes = ((1, 2), (2, 1))
    for leg in range(2):
        for number in range(2):
            for part in range(2):
                axis = axes[part][leg]
                got = swapped(blocks[part], along((axis, axis), number))
                blocks[part] = jnp.concatenate([blocks[part], got])
    return blocks, own


PART_ROWS = ((0, 432), (432, 864), (864, 1280))


PART_AXES = ((0, 1, 2), (1, 2, 0), (2, 0, 1))


def scatter_grads(keep, send):
    keep, send = list(keep), list(send)
    for leg in range(3):
        for number in (1, 0):
            for part, axes in enumerate(PART_AXES):
                axis = axes[leg]
                got = swapped(send[part], along((axis, axis), number))
                mine = keep[part]

                def total(at, mine=mine, got=got):
                    return mine[at].astype(f32) + got[at].astype(f32)

                if number:
                    keep[part] = total(0).astype(bf16)
                    send[part] = total(1).astype(bf16)
                elif leg < 2:
                    keep[part] = total(slice(0, 2)).astype(bf16)
                    send[part] = total(slice(2, 4)).astype(bf16)
                else:
                    keep[part] = total(slice(None))
    return jnp.concatenate(keep)


def lane_of(shape):
    return lax.broadcasted_iota(jnp.int32, shape, len(shape) - 1)


def half_swapped(block):
    lane = lane_of(block.shape)
    return jnp.where(lane % HD < HD // 2, pltpu.roll(block, 96, 1), pltpu.roll(block, 32, 1))


def qkv_weight(w_ref, c):
    return w_ref[:, 96 * c : 96 * c + 96, :].reshape(D, 128)


def normed_of(u, gain):
    scale = lax.rsqrt(jnp.mean(u * u, axis=-1, keepdims=True) + eps)
    return scale, (u * scale * gain).astype(bf16)


def front_weight(idx_ref, wa_ref, wb_ref, c):
    pieces = []
    for d in range(10):
        low, high = 96 * c, 96 * c + 96
        if low < HALF:
            pieces.append(wa_ref[idx_ref[d], low : min(high, HALF), :])
        if high > HALF:
            pieces.append(wb_ref[idx_ref[16 + d], max(low, HALF) - HALF : high - HALF, :])
    return jnp.concatenate(pieces, axis=0)


def project_kernel(idx_ref, u_ref, g_ref, cos_ref, sin_ref, wa_ref, wb_ref, qt_ref, kv_ref):
    u = u_ref[...].astype(f32)
    _, a = normed_of(u, g_ref[...])
    cos, sin = cos_ref[...], sin_ref[...]
    blocks = []
    for c in range(0, 13, 2):
        w = front_weight(idx_ref, wa_ref, wb_ref, c)
        if c + 1 < 13:
            w = jnp.concatenate([w, front_weight(idx_ref, wa_ref, wb_ref, c + 1)], axis=1)
        y = mm(a, w)
        for k in range(w.shape[1] // 128):
            b = y[:, 128 * k : 128 * k + 128]
            if c + k < 10:
                b = b * cos + half_swapped(b) * sin
            blocks.append(b)
    for c in range(8):
        t = (blocks[c].astype(bf16).astype(f32) * 0.125).T.astype(bf16)
        count = 128 if c < 7 else 64
        qt_ref[128 * c : 128 * c + count, :] = t[:count]
    qt_ref[D:, :] = jnp.zeros((QPAD - D, R), bf16)
    kv_ref[:, 640:] = jnp.zeros((R, 128), bf16)
    lane = lane_of((R, 128))
    for g in range(KVH):
        k, v = blocks[(15 + g) // 2], blocks[(20 + g) // 2]
        if (15 + g) % 2:
            k = pltpu.roll(k, 64, 1)
        if (20 + g) % 2 == 0:
            v = pltpu.roll(v, 64, 1)
        kv_ref[:, 128 * g : 128 * g + 128] = jnp.where(lane < 64, k, v).astype(bf16)


def project(u, gain, cos, sin, idx, front):
    whole = lambda *shape: pl.BlockSpec(shape, lambda i, idx: (0,) * len(shape))
    return pl.pallas_call(
        project_kernel,
        name="project",
        grid_spec=pltpu.PrefetchScalarGridSpec(
            num_scalar_prefetch=1,
            grid=(1,),
            in_specs=[
                whole(R, D),
                whole(1, D),
                whole(R, 128),
                whole(R, 128),
                whole(16, HALF, 128),
                whole(16, HALF + 16, 128),
            ],
            out_specs=[whole(QPAD, R), whole(R, 768)],
        ),
        out_shape=[
            jax.ShapeDtypeStruct((QPAD, R), bf16),
            jax.ShapeDtypeStruct((R, 768), bf16),
        ],
        compiler_params=pltpu.CompilerParams(vmem_limit_bytes=48 << 20),
        cost_estimate=pl.CostEstimate(flops=400_000_000, bytes_accessed=6_000_000, transcendentals=0),
    )(idx, u, gain, cos, sin, *front)


def heads_wide(ref, low):
    top = jnp.concatenate([ref[64 * h : 64 * h + 64, :] for h in range(GRP)], axis=1)
    zero = jnp.zeros_like(top)
    return jnp.concatenate([top, zero] if low else [zero, top], axis=0)


SMALL = 64
LANES = GRP * R


def chunk_of(kv_ref, need_ref, i):
    rows = [
        kv_ref[pl.ds(pl.multiple_of(need_ref[CHUNK // SMALL * i + k] * SMALL, SMALL), SMALL), :]
        for k in range(CHUNK // SMALL)
    ]
    return jnp.concatenate(rows, axis=0)


def chunk_rows(i):
    return pl.ds(pl.multiple_of(i * CHUNK, CHUNK), CHUNK)


def attend_kernel(need_ref, qt_ref, kv_ref, bias_ref, mixed_ref, lse_ref, s_ref, c_ref):
    q = heads_wide(qt_ref, True)
    count = need_ref[KEYS // SMALL]

    def score(i, peak):
        kv = chunk_of(kv_ref, need_ref, i)
        c_ref[chunk_rows(i), :] = kv
        b = bias_ref[chunk_rows(i), :]
        s = mm(kv, q) + jnp.concatenate([b, b, b], axis=1)
        s_ref[chunk_rows(i), :] = s
        return jnp.maximum(peak, jnp.max(s, axis=0, keepdims=True))

    peak = lax.fori_loop(0, count, score, jnp.full((1, LANES), masked_fill, f32))

    def mix(i, state):
        total, acc = state
        p = jnp.exp(s_ref[chunk_rows(i), :] - peak)
        total = total + jnp.sum(p, axis=0, keepdims=True)
        return total, acc + mm(c_ref[chunk_rows(i), :].T, p.astype(bf16))

    total, acc = lax.fori_loop(
        0, count, mix, (jnp.zeros((1, LANES), f32), jnp.zeros((128, LANES), f32))
    )
    lse_ref[0] = peak + jnp.log(total)
    o = (acc[64:] / total).astype(bf16)
    for h in range(GRP):
        mixed_ref[64 * h : 64 * h + 64, :] = o[:, 128 * h : 128 * h + 128]


def attend(need, qt, kv_all, bias):
    return pl.pallas_call(
        attend_kernel,
        name="attend",
        grid_spec=pltpu.PrefetchScalarGridSpec(
            num_scalar_prefetch=1,
            grid=(SIDE,),
            in_specs=[
                pl.BlockSpec((GRP * HD, R), lambda g, n: (g, 0)),
                pl.BlockSpec((KEYS, 128), lambda g, n: (0, g)),
                pl.BlockSpec((KEYS, R), lambda g, n: (0, 0)),
            ],
            out_specs=[
                pl.BlockSpec((GRP * HD, R), lambda g, n: (g, 0)),
                pl.BlockSpec((1, 1, LANES), lambda g, n: (g, 0, 0)),
            ],
            scratch_shapes=[pltpu.VMEM((KEYS, LANES), f32), pltpu.VMEM((KEYS, 128), bf16)],
        ),
        out_shape=[
            jax.ShapeDtypeStruct((QSIDE, R), bf16),
            jax.ShapeDtypeStruct((SIDE, 1, LANES), f32),
        ],
        compiler_params=pltpu.CompilerParams(vmem_limit_bytes=48 << 20),
        cost_estimate=pl.CostEstimate(
            flops=2_400_000_000, bytes_accessed=6_000_000, transcendentals=4_700_000
        ),
    )(need, qt, kv_all, bias)


def out_weight(refs, c):
    return jnp.concatenate(
        [ref[:, 160 * c : 160 * c + 160, :].reshape(320, 128) for ref in refs], axis=0
    )


def gu_weight(refs, c):
    gl, gh, ul, uh = refs
    gate = jnp.concatenate([gl[:, c].reshape(512, 128), gh[:, c].reshape(512, 128)], axis=0)
    up = jnp.concatenate([ul[:, c].reshape(512, 128), uh[:, c].reshape(512, 128)], axis=0)
    return jnp.concatenate([gate, up], axis=1)


def down_weight(ref, c):
    return ref[:, 160 * c : 160 * c + 160, :].reshape(640, 128)


WEIGHT_SPECS = (
    [pl.BlockSpec((2, ROWS, 128), lambda j, k=k: (5 + k, 0, 0)) for k in range(3)]
    + [
        pl.BlockSpec((16, 5, 32, 128), lambda j, d=d, o=o: (1 + d, o + j, 0, 0))
        for o in (0, 4)
        for d in (0, 1)
    ]
    + [pl.BlockSpec((4, ROWS, 128), lambda j: (12 + j, 0, 0))]
)


def weight_args(gathered):
    fine = gathered.reshape(SHARDS, 40, 32, 128)
    return [gathered] * 3 + [fine] * 4 + [gathered]


def feed_kernel(
    mixed_ref, u_ref, g_ref, pad_ref, o0, o1, o2, gl, gh, ul, uh, wd,
    y_ref, h_ref, nt_ref, gate_ref, up_ref, mt_ref, n_scr, y_scr,
):
    step = pl.program_id(0)

    @pl.when(step == 0)
    def _():
        mixed = mixed_ref[...].T
        for c in range(0, 8, 2):
            w = jnp.concatenate(
                [out_weight((o0, o1, o2), c), out_weight((o0, o1, o2), c + 1)], axis=1
            )
            y = mm(mixed, w)
            end = min(128 * c + 256, D)
            h_ref[:, 128 * c : end] = u_ref[:, 128 * c : end].astype(f32) + y[:, : end - 128 * c]
        _, n = normed_of(h_ref[...], g_ref[...])
        padded = mm(n, pad_ref[...])
        n_scr[...] = padded.astype(bf16)
        nt_ref[...] = padded.T.astype(bf16)
        y_scr[...] = jnp.zeros_like(y_scr)

    n = n_scr[...]
    inner = []
    for c in range(5):
        gu = mm(n, gu_weight((gl, gh, ul, uh), c))
        gate, up = gu[:, :128], gu[:, 128:]
        cols = slice(128 * c, 128 * c + 128)
        gate_ref[:, cols] = gate
        up_ref[:, cols] = up
        m = gate * jax.nn.sigmoid(gate) * up
        mt_ref[cols, :] = m.T.astype(bf16)
        inner.append(m.astype(bf16))
    inner = jnp.concatenate(inner, axis=1)
    for c in range(0, 8, 2):
        w = jnp.concatenate([down_weight(wd, c), down_weight(wd, c + 1)], axis=1)
        y_scr[:, 128 * c : 128 * c + 256] += mm(inner, w)

    @pl.when(step == 3)
    def _():
        y_ref[...] = (h_ref[...] + y_scr[:, :D]).astype(bf16)


def feed(mixed, u, gain, pad, gathered):
    whole = lambda *shape: pl.BlockSpec(shape, lambda j: (0,) * len(shape))
    return pl.pallas_call(
        feed_kernel,
        name="feed",
        grid=(4,),
        in_specs=[whole(D, R), whole(R, D), whole(1, D), whole(D, PADD)] + WEIGHT_SPECS,
        out_specs=[
            whole(R, D),
            whole(R, D),
            whole(PADD, R),
            pl.BlockSpec((R, 640), lambda j: (0, j)),
            pl.BlockSpec((R, 640), lambda j: (0, j)),
            pl.BlockSpec((640, R), lambda j: (j, 0)),
        ],
        out_shape=[
            jax.ShapeDtypeStruct((R, D), bf16),
            jax.ShapeDtypeStruct((R, D), f32),
            jax.ShapeDtypeStruct((PADD, R), bf16),
            jax.ShapeDtypeStruct((R, FF), f32),
            jax.ShapeDtypeStruct((R, FF), f32),
            jax.ShapeDtypeStruct((FF, R), bf16),
        ],
        scratch_shapes=[pltpu.VMEM((R, PADD), bf16), pltpu.VMEM((R, PADD), f32)],
        compiler_params=pltpu.CompilerParams(vmem_limit_bytes=48 << 20),
        cost_estimate=pl.CostEstimate(
            flops=2_200_000_000, bytes_accessed=22_000_000, transcendentals=400_000
        ),
    )(mixed, u, gain, pad, *weight_args(gathered))


def norm_back(d_out, values, gain):
    scales = lax.rsqrt(jnp.mean(values * values, axis=-1, keepdims=True) + eps)
    scaled = d_out * gain
    d_gain = jnp.sum(d_out * values * scales, axis=0, keepdims=True)
    d_values = scales * scaled - values * (scales * scales * scales) * jnp.mean(
        scaled * values, axis=-1, keepdims=True
    )
    return d_values, d_gain


def feed_back_kernel(
    c_ref, gate_ref, up_ref, h_ref, g_ref, pad_ref, o0, o1, o2, gl, gh, ul, uh, wd,
    dgate_ref, dup_ref, dh_ref, dhb_ref, dg_ref, dot_ref, cb_ref, dn_scr,
):
    step = pl.program_id(0)

    @pl.when(step == 0)
    def _():
        cb_ref[...] = jnp.zeros_like(cb_ref)
        cb_ref[:, :D] = c_ref[...].astype(bf16)
        dn_scr[...] = jnp.zeros_like(dn_scr)

    d_inner = jnp.zeros((R, 640), f32)
    for c in range(0, 8, 2):
        w = jnp.concatenate([down_weight(wd, c), down_weight(wd, c + 1)], axis=1)
        d_inner = d_inner + mm_nt(cb_ref[:, 128 * c : 128 * c + 256], w)
    for c in range(5):
        cols = slice(128 * c, 128 * c + 128)
        gate, up, dm = gate_ref[:, cols], up_ref[:, cols], d_inner[:, cols]
        sigma = jax.nn.sigmoid(gate)
        d_gate = (dm * up * sigma * (1.0 + gate * (1.0 - sigma))).astype(bf16)
        d_up = (dm * gate * sigma).astype(bf16)
        dgate_ref[:, cols] = d_gate
        dup_ref[:, cols] = d_up
        both = jnp.concatenate([d_gate, d_up], axis=1)
        dn_scr[...] += mm_nt(both, gu_weight((gl, gh, ul, uh), c))

    @pl.when(step == 3)
    def _():
        padded = dn_scr[...]
        high = padded.astype(bf16)
        low = (padded - high.astype(f32)).astype(bf16)
        dn = mm_nt(high, pad_ref[...]) + mm_nt(low, pad_ref[...])
        d_h, d_gain = norm_back(dn, h_ref[...], g_ref[...])
        d_h = c_ref[...] + d_h
        dg_ref[...] = d_gain
        dh_ref[...] = d_h
        dhb_ref[...] = jnp.zeros_like(dhb_ref)
        dhb_ref[:, :D] = d_h.astype(bf16)
        d_mixed = jnp.zeros((R, D), f32)
        for c in range(0, 8, 2):
            w = jnp.concatenate(
                [out_weight((o0, o1, o2), c), out_weight((o0, o1, o2), c + 1)], axis=1
            )
            d_mixed = d_mixed + mm_nt(dhb_ref[:, 128 * c : 128 * c + 256], w)
        dot_ref[:D, :] = d_mixed.T
        dot_ref[D:, :] = jnp.zeros((QPAD - D, R), f32)


def feed_back(cot, gate, up, hidden, gain, pad, gathered):
    whole = lambda *shape: pl.BlockSpec(shape, lambda j: (0,) * len(shape))
    block = pl.BlockSpec((R, 640), lambda j: (0, j))
    return pl.pallas_call(
        feed_back_kernel,
        name="feed_back",
        grid=(4,),
        in_specs=[whole(R, D), block, block, whole(R, D), whole(1, D), whole(D, PADD)]
        + WEIGHT_SPECS,
        out_specs=[
            block,
            block,
            whole(R, D),
            whole(R, PADD),
            whole(1, D),
            whole(QPAD, R),
            whole(R, PADD),
        ],
        out_shape=[
            jax.ShapeDtypeStruct((R, FF), bf16),
            jax.ShapeDtypeStruct((R, FF), bf16),
            jax.ShapeDtypeStruct((R, D), f32),
            jax.ShapeDtypeStruct((R, PADD), bf16),
            jax.ShapeDtypeStruct((1, D), f32),
            jax.ShapeDtypeStruct((QPAD, R), f32),
            jax.ShapeDtypeStruct((R, PADD), bf16),
        ],
        scratch_shapes=[pltpu.VMEM((R, PADD), f32)],
        compiler_params=pltpu.CompilerParams(vmem_limit_bytes=48 << 20),
        cost_estimate=pl.CostEstimate(
            flops=2_200_000_000, bytes_accessed=22_000_000, transcendentals=400_000
        ),
    )(cot, gate, up, hidden, gain, pad, *weight_args(gathered))


def attend_back_kernel(
    need_ref, qt_ref, kv_ref, bias_ref, dot_ref, mixed_ref, lse_ref, dkv_ref, dqt_ref
):
    q = heads_wide(qt_ref, True)
    d_o = heads_wide(dot_ref, False)
    o = heads_wide(mixed_ref, False)
    delta = jnp.sum(d_o * o.astype(f32), axis=0, keepdims=True)
    d_o = d_o.astype(bf16)
    lse = lse_ref[0]
    both = jnp.concatenate([q, d_o], axis=1)
    dkv_ref[...] = jnp.zeros_like(dkv_ref)

    def fold(i, acc):
        kv = chunk_of(kv_ref, need_ref, i)
        b = bias_ref[chunk_rows(i), :]
        p = jnp.exp(mm(kv, q) + jnp.concatenate([b, b, b], axis=1) - lse)
        ds = (p * (mm(kv, d_o) - delta)).astype(bf16)
        part = mm_nt(jnp.concatenate([ds, p.astype(bf16)], axis=1), both).astype(bf16)
        for k in range(CHUNK // SMALL):
            at = pl.multiple_of(need_ref[CHUNK // SMALL * i + k] * SMALL, SMALL)
            dkv_ref[pl.ds(at, SMALL), :] = part[SMALL * k : SMALL * k + SMALL]
        return acc + mm(kv.T, ds)

    acc = lax.fori_loop(0, need_ref[KEYS // SMALL], fold, jnp.zeros((128, LANES), f32))
    acc = acc[:64] * 0.125
    for h in range(GRP):
        dqt_ref[64 * h : 64 * h + 64, :] = acc[:, 128 * h : 128 * h + 128]


def attend_back(need, qt, kv_all, bias, d_mixed, mixed, lse):
    heads = pl.BlockSpec((GRP * HD, R), lambda g, n: (g, 0))
    return pl.pallas_call(
        attend_back_kernel,
        name="attend_back",
        grid_spec=pltpu.PrefetchScalarGridSpec(
            num_scalar_prefetch=1,
            grid=(SIDE,),
            in_specs=[
                heads,
                pl.BlockSpec((KEYS, 128), lambda g, n: (0, g)),
                pl.BlockSpec((KEYS, R), lambda g, n: (0, 0)),
                heads,
                heads,
                pl.BlockSpec((1, 1, LANES), lambda g, n: (g, 0, 0)),
            ],
            out_specs=[pl.BlockSpec((KEYS, 128), lambda g, n: (0, g)), heads],
        ),
        out_shape=[
            jax.ShapeDtypeStruct((KEYS, SIDE * 128), bf16),
            jax.ShapeDtypeStruct((QSIDE, R), f32),
        ],
        compiler_params=pltpu.CompilerParams(vmem_limit_bytes=48 << 20),
        cost_estimate=pl.CostEstimate(
            flops=6_000_000_000, bytes_accessed=10_000_000, transcendentals=4_700_000
        ),
    )(need, qt, kv_all, bias, d_mixed, mixed, lse)


def project_back_kernel(
    dqt_ref, dkv_ref, cos_ref, sin_ref, u_ref, g_ref, dh_ref, w_ref,
    du_ref, dqkv_ref, at_ref, dg_ref,
):
    cos, sin = cos_ref[...], sin_ref[...]
    lane = lane_of((R, 128))
    dkv = [dkv_ref[:, 128 * g : 128 * g + 128] for g in range(KVH)]
    rolled = [pltpu.roll(b, 64, 1) for b in dkv]
    zero = jnp.zeros((R, 128), f32)
    blocks = [dqt_ref[128 * c : 128 * c + 128, :].T for c in range(7)]
    last = jnp.concatenate([dqt_ref[896:960, :], jnp.zeros((64, R), f32)], axis=0).T
    low = lane < 64
    blocks.append(jnp.where(low, last, rolled[0]))
    blocks.append(jnp.where(low, dkv[1], rolled[2]))
    blocks.append(jnp.where(low, dkv[3], rolled[4]))
    blocks = [b * cos - half_swapped(b) * sin for b in blocks]
    blocks.append(jnp.where(low, rolled[0], dkv[1]))
    blocks.append(jnp.where(low, rolled[2], dkv[3]))
    blocks.append(jnp.where(low, rolled[4], zero))
    da = jnp.zeros((R, D), f32)
    for c in range(0, 13, 2):
        if c + 1 < 13:
            d = jnp.concatenate([blocks[c], blocks[c + 1]], axis=1).astype(bf16)
            w = jnp.concatenate([qkv_weight(w_ref, c), qkv_weight(w_ref, c + 1)], axis=1)
        else:
            d, w = blocks[c].astype(bf16), qkv_weight(w_ref, c)
        dqkv_ref[:, 128 * c : 128 * c + d.shape[1]] = d
        da = da + mm_nt(d, w)
    u = u_ref[...].astype(f32)
    gain = g_ref[...]
    _, a = normed_of(u, gain)
    at_ref[...] = a.T
    d_u, d_gain = norm_back(da, u, gain)
    dg_ref[...] = d_gain
    du_ref[...] = dh_ref[...] + d_u


def project_back(d_query, d_kv, cos, sin, u, gain, d_hidden, weights):
    whole = lambda *shape: pl.BlockSpec(shape, lambda j: (0,) * len(shape))
    return pl.pallas_call(
        project_back_kernel,
        name="project_back",
        grid=(1,),
        in_specs=[
            whole(D, R),
            whole(R, 640),
            whole(R, 128),
            whole(R, 128),
            whole(R, D),
            whole(1, D),
            whole(R, D),
            whole(10, ROWS, 128),
        ],
        out_specs=[whole(R, D), whole(R, 13 * 128), whole(D, R), whole(1, D)],
        out_shape=[
            jax.ShapeDtypeStruct((R, D), f32),
            jax.ShapeDtypeStruct((R, 13 * 128), bf16),
            jax.ShapeDtypeStruct((D, R), bf16),
            jax.ShapeDtypeStruct((1, D), f32),
        ],
        compiler_params=pltpu.CompilerParams(vmem_limit_bytes=48 << 20),
        cost_estimate=pl.CostEstimate(flops=400_000_000, bytes_accessed=5_000_000, transcendentals=0),
    )(d_query, d_kv, cos, sin, u, gain, d_hidden, weights)


def outer_kernel(
    slot_ref, at_ref, dqkv_ref, mixed_ref, dhb_ref, nt_ref, dgate_ref, dup_ref, mt_ref, cb_ref,
    gain_ref, k0, k1, k2, s0, s1, s2, stage, sems,
):
    step = pl.program_id(0)
    buf = step % 2
    slot_y, slot_x = slot_ref[step // 4], slot_ref[4 + step % 4]
    zslot = [slot_ref[8 + k] for k in range(4)]
    out_ref = stage.at[buf]
    (a0, b0), (a1, b1), (a2, b2) = PART_ROWS

    def copy(i, buf, half=0):
        src = stage.at[buf]
        if i == 0:
            src, dst = src.at[:, a0:b0], (k0, s0)[half].at[slot_y % 2, slot_x]
        elif i == 1:
            src, dst = src.at[:, a1:b1], (k1, s1)[half].at[slot_x % 2, :, slot_y]
        elif i == 2:
            src, dst = src.at[0:2, a2:b2], k2.at[:, slot_y, slot_x]
        else:
            src, dst = src.at[2:4, a2:b2], s2.at[:, slot_y, slot_x]
        return pltpu.make_async_copy(src, dst, sems.at[buf, i])

    @pl.when(step >= 2)
    def _():
        for i in range(4):
            copy(i, buf).wait()

    def row_of(k, count, at):
        row = lax.broadcasted_iota(jnp.int32, (count, 128), 0)
        return jnp.where(row == at, gain_ref[pl.ds(4 * step + k, 1), :], 0.0)

    def narrow(start, ks):
        count = len(ks)
        rows = at_ref[pl.ds(pl.multiple_of(start, 32), 96 * count), :]
        for c in range(0, 13, 2):
            width = min(256, 1664 - 128 * c)
            res = mm(rows, dqkv_ref[:, 128 * c : 128 * c + width])
            for i, k in enumerate(ks):
                for h in range(width // 128):
                    out_ref[zslot[k], 96 * (c + h) : 96 * (c + h) + 96, :] = res[
                        96 * i : 96 * i + 96, 128 * h : 128 * h + 128
                    ].astype(bf16)
        for k in ks:
            out_ref[zslot[k], 1248:1280, :] = row_of(k, 32, 0).astype(bf16)

    def wide(ref, start, cot_ref, ks):
        rows = ref[pl.ds(pl.multiple_of(start, 32), 160 * len(ks)), :]
        for c in range(0, 8, 2):
            res = mm(rows, cot_ref[:, 128 * c : 128 * c + 256])
            for i, k in enumerate(ks):
                for h in range(2):
                    b = res[160 * i : 160 * i + 160, 128 * h : 128 * h + 128]
                    if c + h == 7:
                        b = b + row_of(k, 160, 0)
                    at = 160 * (c + h)
                    out_ref[zslot[k], at : at + 160, :] = b.astype(bf16)

    @pl.when(step < 2)
    def _():
        narrow(384 * step, (0, 1, 2, 3))

    @pl.when(step == 2)
    def _():
        narrow(768, (0, 1))
        wide(mixed_ref, 0, dhb_ref, (2, 3))

    @pl.when(step == 3)
    def _():
        wide(mixed_ref, 320, dhb_ref, (0, 1, 2, 3))

    @pl.when((step >= 4) & (step < 12))
    def _():
        rows = nt_ref[pl.ds(pl.multiple_of(128 * (step - 4), 128), 128), :]
        for part, ref in enumerate((dgate_ref, dup_ref)):
            for c in range(0, 20, 2):
                res = mm(rows, ref[:, 128 * c : 128 * c + 256])
                for k in range(4):
                    for h in range(2):
                        b = res[32 * k : 32 * k + 32, 128 * h : 128 * h + 128]
                        at = 32 * (20 * part + c + h)
                        if at == 0:
                            b = b + row_of(k, 32, 30)
                        out_ref[zslot[k], at : at + 32, :] = b.astype(bf16)

    @pl.when(step >= 12)
    def _():
        wide(mt_ref, 640 * (step - 12), cb_ref, (0, 1, 2, 3))

    for half in range(2):

        @pl.when(slot_y // 2 == half)
        def _(half=half):
            copy(0, buf, half).start()

        @pl.when(slot_x // 2 == half)
        def _(half=half):
            copy(1, buf, half).start()

    copy(2, buf).start()
    copy(3, buf).start()

    @pl.when(step == 15)
    def _():
        for last in (0, 1):
            for i in range(4):
                copy(i, last).wait()


def outer(slots, at, dqkv, mixed, dhb, nt, dgate, dup, mt, cb, gains):
    whole = lambda v: pl.BlockSpec(v.shape, lambda s, slot: (0,) * v.ndim)
    args = (at, dqkv, mixed, dhb, nt, dgate, dup, mt, cb, gains)
    shapes = [
        jax.ShapeDtypeStruct((2, 4, 4, end - begin, 128), bf16) for begin, end in PART_ROWS
    ]
    out = pl.pallas_call(
        outer_kernel,
        name="outer",
        grid_spec=pltpu.PrefetchScalarGridSpec(
            num_scalar_prefetch=1,
            grid=(16,),
            in_specs=[whole(v) for v in args],
            out_specs=[pl.BlockSpec(memory_space=pl.ANY)] * 6,
            scratch_shapes=[
                pltpu.VMEM((2, 4, ROWS, 128), bf16),
                pltpu.SemaphoreType.DMA((2, 4)),
            ],
        ),
        out_shape=shapes * 2,
        compiler_params=pltpu.CompilerParams(vmem_limit_bytes=48 << 20),
        cost_estimate=pl.CostEstimate(
            flops=2_600_000_000, bytes_accessed=24_000_000, transcendentals=0
        ),
    )(slots, *args)
    return out[:3], out[3:]


def shard_kind(rank):
    return jnp.where(rank < 10, 0, jnp.where((rank >= 16) & (rank < 48), 2, 1))


def shard_blocks(flat, rank):
    def narrow(_):
        w = jnp.pad(flat.reshape(96, 1600), ((0, 0), (0, 64)))
        w = w.reshape(96, 13, 128).transpose(1, 0, 2).reshape(1248, 128)
        return jnp.pad(w, ((0, 32), (0, 0)))

    def square(_):
        w = jnp.pad(flat.reshape(160, 960), ((0, 0), (0, 64)))
        return w.reshape(160, 8, 128).transpose(1, 0, 2).reshape(ROWS, 128)

    def broad(_):
        w = jnp.pad(flat.reshape(30, 40, 128), ((0, 2), (0, 0), (0, 0)))
        return w.transpose(1, 0, 2).reshape(ROWS, 128)

    return lax.switch(shard_kind(rank), [narrow, square, broad], 0)


def blocks_shard(blocks, rank):
    def narrow(_):
        w = blocks[:1248].reshape(13, 96, 128).transpose(1, 0, 2).reshape(96, 1664)[:, :1600]
        return w.reshape(SHARD), blocks[1248, :30]

    def square(_):
        w = blocks.reshape(8, 160, 128).transpose(1, 0, 2).reshape(160, 1024)[:, :960]
        return w.reshape(SHARD), blocks[1120, 64:94]

    def broad(_):
        w = blocks.reshape(40, 32, 128).transpose(1, 0, 2)[:30]
        return w.reshape(SHARD), blocks[30, :30]

    return lax.switch(shard_kind(rank), [narrow, square, broad], 0)


def per_device(layer_in, out_grad, segment_ids, block_pair, params, norm_gains):
    phase = lax.axis_index("phase")
    ctx = lax.axis_index("ctx")
    rank = ctx * 2 + lax.axis_index("fsdp")
    y, x, z = rank // 16, (rank // 4) % 4, rank % 4
    zh = z // 2

    own = shard_blocks(params[0], rank)
    front, own = gather_front(own, norm_gains[0], y, phase)
    gathered = lax.all_gather(own, ("ctx", "fsdp"), axis=0)

    seg_row = segment_ids[0]
    pair = lax.dynamic_index_in_dim(block_pair, ctx, 0, keepdims=False)
    within = jnp.arange(HD, dtype=jnp.int32)
    place_q = jnp.concatenate([pair * 64 + within, (63 - pair) * 64 + within])
    seg_q = jnp.concatenate(
        [
            lax.dynamic_slice_in_dim(seg_row, pair * 64, 64),
            lax.dynamic_slice_in_dim(seg_row, (63 - pair) * 64, 64),
        ]
    )
    start_q = jnp.sum((seg_row[:, None] < seg_q[None, :]).astype(jnp.int32), axis=0)
    pairs_k = block_pair[key_order(y, x, zh, phase)]
    spot_k = jnp.stack([pairs_k, 63 - pairs_k], axis=1).reshape(64)
    seen_by = lambda at, spot: (spot_k <= spot) & (spot_k * 64 + 63 >= start_q[at])
    seen = seen_by(0, pair) | seen_by(64, 63 - pair)
    seen_count = jnp.sum(seen.astype(jnp.int32))
    before = jnp.arange(64)[:, None] > jnp.arange(64)[None, :]
    rank_seen = jnp.sum((before & seen[None, :]).astype(jnp.int32), axis=1)
    rank_k = jnp.where(seen, rank_seen, seen_count + jnp.arange(64) - rank_seen)
    chosen = rank_k[None, :] == jnp.arange(64)[:, None]
    order_k = jnp.sum(jnp.where(chosen, jnp.arange(64)[None, :], 0), axis=1)
    spot_k = jnp.sum(jnp.where(chosen & seen[None, :], spot_k[None, :], 0), axis=1)
    spot_k = jnp.where(jnp.arange(64) < seen_count, spot_k, 1 << 16)
    need = jnp.concatenate([order_k, ((seen_count + 7) // 8)[None]]).astype(jnp.int32)
    place_k = (spot_k[:, None] * 64 + within[None, :]).reshape(KEYS)
    bias = jnp.where(
        (place_k[:, None] <= place_q[None, :]) & (place_k[:, None] >= start_q[None, :]),
        0.0,
        masked_fill,
    ).astype(f32)
    frequency = rope_theta ** (-2.0 * jnp.arange(HD // 2, dtype=f32) / HD)
    angles = (place_q - start_q).astype(f32)[:, None] * frequency[None, :]
    cosine, sine = jnp.cos(angles), jnp.sin(angles)
    cos = jnp.concatenate([cosine] * 4, axis=1)
    sin = jnp.concatenate([-sine, sine, -sine, sine], axis=1)
    spread = jnp.arange(PADD, dtype=jnp.int32)
    target = jnp.where(spread % 32 < 30, (spread // 32) * 30 + spread % 32, -1)
    pad = (jnp.arange(D, dtype=jnp.int32)[:, None] == target[None, :]).astype(bf16)

    four = jnp.arange(4, dtype=jnp.int32)
    slots_y, slots_x, slots_z = (slot_of(four ^ at_axis, phase) for at_axis in (y, x, z))
    idx = jnp.concatenate(
        [
            (slots_x[:, None] + 4 * slots_z[None, :]).reshape(16),
            (4 * slots_x[:, None] + slots_z[None, :]).reshape(16),
        ]
    )
    gains = front[1][:, HALF : HALF + 4, :30][idx[16:]].astype(f32)
    gains = gains.transpose(1, 0, 2).reshape(1, 2 * D)
    gain_one, gain_two = gains[:, :D], gains[:, D:]
    first = phase == 0

    u = layer_in[0]
    mixed = None
    kept = []
    for tick in range(2):
        active = phase == tick
        qt, kv = project(u, gain_one, cos, sin, idx, front)
        kv_side = jnp.where(active, kv[:, :384], over(kv[:, 384:], tick))
        qt_side = jnp.where(active, qt[:QSIDE], over(qt[QSIDE:], tick))
        kv_all = gather_keys(kv_side)
        mixed_side, lse = attend(need, qt_side, kv_all, bias)
        kept.append((qt_side, kv_all, mixed_side, lse))
        far = over(mixed_side[: D - QSIDE], 1 - tick)
        whole = jnp.concatenate([mixed_side, far])
        mixed = whole if tick == 0 else jnp.where(active, whole, mixed)
        result, hidden, nt, gate, up, mt = feed(mixed, u, gain_two, pad, gathered)
        if tick == 0:
            u = jnp.where(first, u, over(result, 0))

    cot = out_grad[0]
    d_query = d_kv = None
    for tick in range(2):
        layer = 1 - tick
        active = phase == layer
        qt_side, kv_all, mixed_side, lse = kept[layer]
        dgate, dup, dh, dhb, dg_two, d_mixed, cb = feed_back(
            cot, gate, up, hidden, gain_two, pad, gathered
        )
        d_side = jnp.where(active, d_mixed[:QSIDE], over(d_mixed[QSIDE:], layer))
        d_kv_all, dq_side = attend_back(need, qt_side, kv_all, bias, d_side, mixed_side, lse)
        dq_new = jnp.concatenate([dq_side, over(dq_side[: D - QSIDE], tick)])
        dkv_side = scatter_keys(d_kv_all)
        dkv_new = jnp.concatenate([dkv_side, over(dkv_side[:, :256], tick)], axis=1)
        d_query = dq_new if tick == 0 else jnp.where(active, dq_new, d_query)
        d_kv = dkv_new if tick == 0 else jnp.where(active, dkv_new, d_kv)
        d_u, dqkv, at, dg_one = project_back(
            d_query, d_kv, cos, sin, u, gain_one, dh, gathered
        )
        if tick == 0:
            cot = jnp.where(first, over(d_u.astype(bf16), 1).astype(f32), cot)

    gains = jnp.concatenate([dg_one, dg_two], axis=1).reshape(SHARDS, 30)
    shards = jnp.arange(SHARDS, dtype=jnp.int32)
    square = (((shards >= 10) & (shards < 16)) | (shards >= 48))[:, None]
    gains = jnp.where(
        square, jnp.pad(gains, ((0, 0), (64, 34))), jnp.pad(gains, ((0, 0), (0, 98)))
    )
    slots = jnp.concatenate([slots_y, slots_x, slots_z])
    keep, send = outer(slots, at, dqkv, mixed, dhb, nt, dgate, dup, mt, cb, gains)
    total = scatter_grads(keep, send)
    param_part, gain_part = blocks_shard(total, rank)
    return (result[None, None], d_u[None, None], param_part[None], gain_part[None])


def solution(mesh):
    return jax.shard_map(
        per_device,
        mesh=mesh,
        in_specs=(
            P("fsdp", "ctx", None),
            P("fsdp", "ctx", None),
            P("fsdp", None),
            P(),
            P("phase", ("ctx", "fsdp")),
            P("phase", ("ctx", "fsdp")),
        ),
        out_specs=(
            P("phase", "fsdp", "ctx", None),
            P("phase", "fsdp", "ctx", None),
            P("phase", ("ctx", "fsdp")),
            P("phase", ("ctx", "fsdp")),
        ),
        check_vma=False,
    )
```

```python
import functools

import jax
import jax.numpy as jnp
from jax import lax
from jax.experimental import pallas as pl
from jax.experimental.pallas import tpu as pltpu
from jax.sharding import PartitionSpec as P

H = 15
KVH = 5
HD = 64
D = 960
FF = 2560
GRP = H // KVH
R = 128
SHARDS = 64
SHARD = 153600
ROWS = 1280
KEYS = 4096
CHUNK = 512
PADD = 1024
SIDE = 3
QSIDE = SIDE * GRP * HD
QPAD = 2 * QSIDE

eps = 1e-05
rope_theta = 100000.0
masked_fill = -1e30
f32 = jnp.float32
bf16 = jnp.bfloat16
ALL = ("phase", "ctx", "fsdp")

NT = (((1,), (1,)), ((), ()))


def mm(a, b):
    return jnp.dot(a, b, preferred_element_type=f32)


def mm_nt(a, b):
    return lax.dot_general(a, b, NT, preferred_element_type=f32)


STEPS = ((1, 3), (3, 1))


def swapped(block, way):
    pairs = []
    for p in range(2):
        dy, dx, dz = way(p)
        for y in range(4):
            for x in range(4):
                for z in range(4):
                    to = ((y ^ dy) * 4 + (x ^ dx)) * 4 + (z ^ dz)
                    pairs.append((p * 64 + (y * 4 + x) * 4 + z, p * 64 + to))
    return lax.ppermute(block, ALL, pairs)


def over(block, source):
    return lax.ppermute(block, "phase", [(source, 1 - source)])


def along(axes, number):
    def way(p):
        shift = [0, 0, 0]
        shift[axes[p]] = STEPS[p][number]
        return tuple(shift)

    return way


def far_z(p):
    return (0, 0, 2)


def gather_keys(kv):
    tail = kv.shape
    far = swapped(kv, far_z)
    near = kv
    orders = (((0, 1), (1, 0)), ((1, 0), (0, 1)))
    blocks = [near[None], far[None]]
    for leg in range(2):
        for number in range(2):
            if leg and number:
                blocks = list(lax.optimization_barrier(tuple(blocks)))
            for k in range(2):
                got = swapped(blocks[k], along(orders[k][leg], number))
                blocks[k] = jnp.concatenate([blocks[k], got], axis=0)
    return jnp.concatenate(blocks, axis=0).reshape(KEYS, tail[1])


def scatter_keys(d_kv, beside=None):
    parts = d_kv.reshape(2, 16, R, d_kv.shape[1])
    orders = (((0, 1), (1, 0)), ((1, 0), (0, 1)))
    blocks = [parts[0], parts[1]]
    for leg in (1, 0):
        for number in (1, 0):
            for k in (1, 0):
                half = blocks[k].shape[0] // 2
                got = swapped(blocks[k][half:], along(orders[k][leg], number))
                total = blocks[k][:half].astype(f32) + got.astype(f32)
                last = k == 0 and half == 1
                blocks[k] = total if last else total.astype(bf16)
            if beside is not None and leg and number:
                blocks, beside = lax.optimization_barrier((blocks, beside))
    return blocks[0][0] + swapped(blocks[1][0], far_z).astype(f32), beside


def slot_offsets(phase):
    return jnp.where(phase == 0, jnp.array([0, 1, 3, 2]), jnp.array([0, 3, 1, 2]))


def slot_of(offset, phase):
    at = jnp.where(phase == 0, jnp.array([0, 1, 3, 2]), jnp.array([0, 2, 3, 1]))
    return at[offset]


def key_order(y, x, zh, phase):
    off = slot_offsets(phase)
    outer = jnp.repeat(off, 4)
    inner = jnp.tile(off, 4)
    out = []
    for k in range(2):
        first_y = phase == k
        oy = jnp.where(first_y, inner, outer)
        ox = jnp.where(first_y, outer, inner)
        out.append((y ^ oy) * 8 + (x ^ ox) * 2 + (zh ^ k))
    return jnp.concatenate(out)


HALF = ROWS // 2


def gather_front(own, gains, y, phase):
    row = jnp.pad(gains[None], ((0, 15), (0, 98)))
    block = jnp.concatenate([own, row])[None]
    for number in range(2):
        block = jnp.concatenate([block, swapped(block, along((0, 0), number))])
    block, own = lax.optimization_barrier((block, own))
    at = slot_of(jnp.arange(4, dtype=jnp.int32) ^ y, phase)
    front = lax.dynamic_index_in_dim(block, at[0], 0, keepdims=False)
    rows = jnp.pad(block[:, ROWS][at], ((0, 12), (0, 0)))
    blocks = [front[None, :HALF], jnp.concatenate([front[HALF:ROWS], rows])[None]]
    axes = ((1, 2), (2, 1))
    for leg in range(2):
        for number in range(2):
            for part in range(2):
                axis = axes[part][leg]
                got = swapped(blocks[part], along((axis, axis), number))
                blocks[part] = jnp.concatenate([blocks[part], got])
    return blocks, own


PART_ROWS = ((0, 432), (432, 864), (864, 1280))


PART_AXES = ((0, 1, 2), (1, 2, 0), (2, 0, 1))


def scatter_grads(keep, send):
    keep, send = list(keep), list(send)
    for leg in range(3):
        for number in (1, 0):
            for part, axes in enumerate(PART_AXES):
                axis = axes[leg]
                got = swapped(send[part], along((axis, axis), number))
                mine = keep[part]

                def total(at, mine=mine, got=got):
                    return mine[at].astype(f32) + got[at].astype(f32)

                if number:
                    keep[part] = total(0).astype(bf16)
                    send[part] = total(1).astype(bf16)
                elif leg < 2:
                    keep[part] = total(slice(0, 2)).astype(bf16)
                    send[part] = total(slice(2, 4)).astype(bf16)
                else:
                    keep[part] = total(slice(None))
    return jnp.concatenate(keep)


def lane_of(shape):
    return lax.broadcasted_iota(jnp.int32, shape, len(shape) - 1)


def half_swapped(block):
    lane = lane_of(block.shape)
    return jnp.where(lane % HD < HD // 2, pltpu.roll(block, 96, 1), pltpu.roll(block, 32, 1))


def qkv_weight(w_ref, c):
    return w_ref[:, 96 * c : 96 * c + 96, :].reshape(D, 128)


def normed_of(u, gain):
    scale = lax.rsqrt(jnp.mean(u * u, axis=-1, keepdims=True) + eps)
    return scale, (u * scale * gain).astype(bf16)


def front_weight(idx_ref, wa_ref, wb_ref, c):
    pieces = []
    for d in range(10):
        low, high = 96 * c, 96 * c + 96
        if low < HALF:
            pieces.append(wa_ref[idx_ref[d], low : min(high, HALF), :])
        if high > HALF:
            pieces.append(wb_ref[idx_ref[16 + d], max(low, HALF) - HALF : high - HALF, :])
    return jnp.concatenate(pieces, axis=0)


def project_kernel(idx_ref, u_ref, g_ref, cos_ref, sin_ref, wa_ref, wb_ref, qt_ref, kv_ref):
    u = u_ref[...].astype(f32)
    _, a = normed_of(u, g_ref[...])
    cos, sin = cos_ref[...], sin_ref[...]
    blocks = []
    for c in range(0, 13, 2):
        w = front_weight(idx_ref, wa_ref, wb_ref, c)
        if c + 1 < 13:
            w = jnp.concatenate([w, front_weight(idx_ref, wa_ref, wb_ref, c + 1)], axis=1)
        y = mm(a, w)
        for k in range(w.shape[1] // 128):
            b = y[:, 128 * k : 128 * k + 128]
            if c + k < 10:
                b = b * cos + half_swapped(b) * sin
            blocks.append(b)
    for c in range(8):
        t = (blocks[c].astype(bf16).astype(f32) * 0.125).T.astype(bf16)
        count = 128 if c < 7 else 64
        qt_ref[128 * c : 128 * c + count, :] = t[:count]
    qt_ref[D:, :] = jnp.zeros((QPAD - D, R), bf16)
    kv_ref[:, 640:] = jnp.zeros((R, 128), bf16)
    lane = lane_of((R, 128))
    for g in range(KVH):
        k, v = blocks[(15 + g) // 2], blocks[(20 + g) // 2]
        if (15 + g) % 2:
            k = pltpu.roll(k, 64, 1)
        if (20 + g) % 2 == 0:
            v = pltpu.roll(v, 64, 1)
        kv_ref[:, 128 * g : 128 * g + 128] = jnp.where(lane < 64, k, v).astype(bf16)


def project(u, gain, cos, sin, idx, front):
    whole = lambda *shape: pl.BlockSpec(shape, lambda i, idx: (0,) * len(shape))
    return pl.pallas_call(
        project_kernel,
        name="project",
        grid_spec=pltpu.PrefetchScalarGridSpec(
            num_scalar_prefetch=1,
            grid=(1,),
            in_specs=[
                whole(R, D),
                whole(1, D),
                whole(R, 128),
                whole(R, 128),
                whole(16, HALF, 128),
                whole(16, HALF + 16, 128),
            ],
            out_specs=[whole(QPAD, R), whole(R, 768)],
        ),
        out_shape=[
            jax.ShapeDtypeStruct((QPAD, R), bf16),
            jax.ShapeDtypeStruct((R, 768), bf16),
        ],
        compiler_params=pltpu.CompilerParams(vmem_limit_bytes=48 << 20),
        cost_estimate=pl.CostEstimate(flops=400_000_000, bytes_accessed=6_000_000, transcendentals=0),
    )(idx, u, gain, cos, sin, *front)


def heads_wide(ref, low):
    top = jnp.concatenate([ref[64 * h : 64 * h + 64, :] for h in range(GRP)], axis=1)
    zero = jnp.zeros_like(top)
    return jnp.concatenate([top, zero] if low else [zero, top], axis=0)


SMALL = 64
LANES = GRP * R


def chunk_of(kv_ref, need_ref, i):
    rows = [
        kv_ref[pl.ds(pl.multiple_of(need_ref[CHUNK // SMALL * i + k] * SMALL, SMALL), SMALL), :]
        for k in range(CHUNK // SMALL)
    ]
    return jnp.concatenate(rows, axis=0)


def chunk_rows(i):
    return pl.ds(pl.multiple_of(i * CHUNK, CHUNK), CHUNK)


def attend_kernel(need_ref, qt_ref, kv_ref, bias_ref, mixed_ref, lse_ref, s_ref, c_ref):
    q = heads_wide(qt_ref, True)
    count = need_ref[KEYS // SMALL]

    def score(pair, peak):
        for i in (2 * pair, 2 * pair + 1):
            kv = chunk_of(kv_ref, need_ref, i)
            c_ref[chunk_rows(i), :] = kv
            b = bias_ref[chunk_rows(i), :]
            s = mm(kv, q) + jnp.concatenate([b, b, b], axis=1)
            s_ref[chunk_rows(i), :] = s
            peak = jnp.maximum(peak, jnp.max(s, axis=0, keepdims=True))
        return peak

    peak = lax.fori_loop(0, count, score, jnp.full((1, LANES), masked_fill, f32))

    def mix(pair, state):
        total, acc = state
        for i in (2 * pair, 2 * pair + 1):
            p = jnp.exp(s_ref[chunk_rows(i), :] - peak)
            total = total + jnp.sum(p, axis=0, keepdims=True)
            acc = acc + mm(c_ref[chunk_rows(i), :].T, p.astype(bf16))
        return total, acc

    total, acc = lax.fori_loop(
        0, count, mix, (jnp.zeros((1, LANES), f32), jnp.zeros((128, LANES), f32))
    )
    lse_ref[0] = peak + jnp.log(total)
    o = (acc[64:] / total).astype(bf16)
    for h in range(GRP):
        mixed_ref[64 * h : 64 * h + 64, :] = o[:, 128 * h : 128 * h + 128]


def attend(need, qt, kv_all, bias):
    return pl.pallas_call(
        attend_kernel,
        name="attend",
        grid_spec=pltpu.PrefetchScalarGridSpec(
            num_scalar_prefetch=1,
            grid=(SIDE,),
            in_specs=[
                pl.BlockSpec((GRP * HD, R), lambda g, n: (g, 0)),
                pl.BlockSpec((KEYS, 128), lambda g, n: (0, g)),
                pl.BlockSpec((KEYS, R), lambda g, n: (0, 0)),
            ],
            out_specs=[
                pl.BlockSpec((GRP * HD, R), lambda g, n: (g, 0)),
                pl.BlockSpec((1, 1, LANES), lambda g, n: (g, 0, 0)),
            ],
            scratch_shapes=[pltpu.VMEM((KEYS, LANES), f32), pltpu.VMEM((KEYS, 128), bf16)],
        ),
        out_shape=[
            jax.ShapeDtypeStruct((QSIDE, R), bf16),
            jax.ShapeDtypeStruct((SIDE, 1, LANES), f32),
        ],
        compiler_params=pltpu.CompilerParams(vmem_limit_bytes=48 << 20),
        cost_estimate=pl.CostEstimate(
            flops=2_400_000_000, bytes_accessed=6_000_000, transcendentals=4_700_000
        ),
    )(need, qt, kv_all, bias)


def out_weight(refs, c):
    return jnp.concatenate(
        [ref[:, 160 * c : 160 * c + 160, :].reshape(320, 128) for ref in refs], axis=0
    )


def gu_weight(refs, c):
    gl, gh, ul, uh = refs
    gate = jnp.concatenate([gl[:, c].reshape(512, 128), gh[:, c].reshape(512, 128)], axis=0)
    up = jnp.concatenate([ul[:, c].reshape(512, 128), uh[:, c].reshape(512, 128)], axis=0)
    return jnp.concatenate([gate, up], axis=1)


def down_weight(ref, c):
    return ref[:, 160 * c : 160 * c + 160, :].reshape(640, 128)


WEIGHT_SPECS = (
    [pl.BlockSpec((2, ROWS, 128), lambda j, k=k: (5 + k, 0, 0)) for k in range(3)]
    + [
        pl.BlockSpec((16, 5, 32, 128), lambda j, d=d, o=o: (1 + d, o + j, 0, 0))
        for o in (0, 4)
        for d in (0, 1)
    ]
    + [pl.BlockSpec((4, ROWS, 128), lambda j: (12 + j, 0, 0))]
)


def weight_args(gathered):
    fine = gathered.reshape(SHARDS, 40, 32, 128)
    return [gathered] * 3 + [fine] * 4 + [gathered]


def feed_kernel(
    mixed_ref, u_ref, g_ref, pad_ref, o0, o1, o2, gl, gh, ul, uh, wd,
    y_ref, h_ref, nt_ref, gate_ref, up_ref, mt_ref, n_scr, y_scr,
):
    step = pl.program_id(0)

    @pl.when(step == 0)
    def _():
        mixed = mixed_ref[...].T
        for c in range(0, 8, 2):
            w = jnp.concatenate(
                [out_weight((o0, o1, o2), c), out_weight((o0, o1, o2), c + 1)], axis=1
            )
            y = mm(mixed, w)
            end = min(128 * c + 256, D)
            h_ref[:, 128 * c : end] = u_ref[:, 128 * c : end].astype(f32) + y[:, : end - 128 * c]
        _, n = normed_of(h_ref[...], g_ref[...])
        padded = mm(n, pad_ref[...])
        n_scr[...] = padded.astype(bf16)
        nt_ref[...] = padded.T.astype(bf16)
        y_scr[...] = jnp.zeros_like(y_scr)

    n = n_scr[...]
    inner = []
    for c in range(5):
        gu = mm(n, gu_weight((gl, gh, ul, uh), c))
        gate, up = gu[:, :128], gu[:, 128:]
        cols = slice(128 * c, 128 * c + 128)
        gate_ref[:, cols] = gate
        up_ref[:, cols] = up
        m = gate * jax.nn.sigmoid(gate) * up
        mt_ref[cols, :] = m.T.astype(bf16)
        inner.append(m.astype(bf16))
    inner = jnp.concatenate(inner, axis=1)
    for c in range(0, 8, 2):
        w = jnp.concatenate([down_weight(wd, c), down_weight(wd, c + 1)], axis=1)
        y_scr[:, 128 * c : 128 * c + 256] += mm(inner, w)

    @pl.when(step == 3)
    def _():
        y_ref[...] = (h_ref[...] + y_scr[:, :D]).astype(bf16)


def feed(mixed, u, gain, pad, gathered):
    whole = lambda *shape: pl.BlockSpec(shape, lambda j: (0,) * len(shape))
    return pl.pallas_call(
        feed_kernel,
        name="feed",
        grid=(4,),
        in_specs=[whole(D, R), whole(R, D), whole(1, D), whole(D, PADD)] + WEIGHT_SPECS,
        out_specs=[
            whole(R, D),
            whole(R, D),
            whole(PADD, R),
            pl.BlockSpec((R, 640), lambda j: (0, j)),
            pl.BlockSpec((R, 640), lambda j: (0, j)),
            pl.BlockSpec((640, R), lambda j: (j, 0)),
        ],
        out_shape=[
            jax.ShapeDtypeStruct((R, D), bf16),
            jax.ShapeDtypeStruct((R, D), f32),
            jax.ShapeDtypeStruct((PADD, R), bf16),
            jax.ShapeDtypeStruct((R, FF), f32),
            jax.ShapeDtypeStruct((R, FF), f32),
            jax.ShapeDtypeStruct((FF, R), bf16),
        ],
        scratch_shapes=[pltpu.VMEM((R, PADD), bf16), pltpu.VMEM((R, PADD), f32)],
        compiler_params=pltpu.CompilerParams(vmem_limit_bytes=48 << 20),
        cost_estimate=pl.CostEstimate(
            flops=2_200_000_000, bytes_accessed=22_000_000, transcendentals=400_000
        ),
    )(mixed, u, gain, pad, *weight_args(gathered))


def norm_back(d_out, values, gain):
    scales = lax.rsqrt(jnp.mean(values * values, axis=-1, keepdims=True) + eps)
    scaled = d_out * gain
    d_gain = jnp.sum(d_out * values * scales, axis=0, keepdims=True)
    d_values = scales * scaled - values * (scales * scales * scales) * jnp.mean(
        scaled * values, axis=-1, keepdims=True
    )
    return d_values, d_gain


def feed_back_kernel(
    c_ref, gate_ref, up_ref, h_ref, g_ref, pad_ref, o0, o1, o2, gl, gh, ul, uh, wd,
    dgate_ref, dup_ref, dh_ref, dhb_ref, dg_ref, dot_ref, cb_ref, dn_scr,
):
    step = pl.program_id(0)

    @pl.when(step == 0)
    def _():
        cb_ref[...] = jnp.zeros_like(cb_ref)
        cb_ref[:, :D] = c_ref[...].astype(bf16)
        dn_scr[...] = jnp.zeros_like(dn_scr)

    d_inner = jnp.zeros((R, 640), f32)
    for c in range(0, 8, 2):
        w = jnp.concatenate([down_weight(wd, c), down_weight(wd, c + 1)], axis=1)
        d_inner = d_inner + mm_nt(cb_ref[:, 128 * c : 128 * c + 256], w)
    for c in range(5):
        cols = slice(128 * c, 128 * c + 128)
        gate, up, dm = gate_ref[:, cols], up_ref[:, cols], d_inner[:, cols]
        sigma = jax.nn.sigmoid(gate)
        d_gate = (dm * up * sigma * (1.0 + gate * (1.0 - sigma))).astype(bf16)
        d_up = (dm * gate * sigma).astype(bf16)
        dgate_ref[:, cols] = d_gate
        dup_ref[:, cols] = d_up
        both = jnp.concatenate([d_gate, d_up], axis=1)
        dn_scr[...] += mm_nt(both, gu_weight((gl, gh, ul, uh), c))

    @pl.when(step == 3)
    def _():
        padded = dn_scr[...]
        high = padded.astype(bf16)
        low = (padded - high.astype(f32)).astype(bf16)
        dn = mm_nt(high, pad_ref[...]) + mm_nt(low, pad_ref[...])
        d_h, d_gain = norm_back(dn, h_ref[...], g_ref[...])
        d_h = c_ref[...] + d_h
        dg_ref[...] = d_gain
        dh_ref[...] = d_h
        dhb_ref[...] = jnp.zeros_like(dhb_ref)
        dhb_ref[:, :D] = d_h.astype(bf16)
        d_mixed = jnp.zeros((R, D), f32)
        for c in range(0, 8, 2):
            w = jnp.concatenate(
                [out_weight((o0, o1, o2), c), out_weight((o0, o1, o2), c + 1)], axis=1
            )
            d_mixed = d_mixed + mm_nt(dhb_ref[:, 128 * c : 128 * c + 256], w)
        dot_ref[:D, :] = d_mixed.T
        dot_ref[D:, :] = jnp.zeros((QPAD - D, R), f32)


def feed_back(cot, gate, up, hidden, gain, pad, gathered):
    whole = lambda *shape: pl.BlockSpec(shape, lambda j: (0,) * len(shape))
    block = pl.BlockSpec((R, 640), lambda j: (0, j))
    return pl.pallas_call(
        feed_back_kernel,
        name="feed_back",
        grid=(4,),
        in_specs=[whole(R, D), block, block, whole(R, D), whole(1, D), whole(D, PADD)]
        + WEIGHT_SPECS,
        out_specs=[
            block,
            block,
            whole(R, D),
            whole(R, PADD),
            whole(1, D),
            whole(QPAD, R),
            whole(R, PADD),
        ],
        out_shape=[
            jax.ShapeDtypeStruct((R, FF), bf16),
            jax.ShapeDtypeStruct((R, FF), bf16),
            jax.ShapeDtypeStruct((R, D), f32),
            jax.ShapeDtypeStruct((R, PADD), bf16),
            jax.ShapeDtypeStruct((1, D), f32),
            jax.ShapeDtypeStruct((QPAD, R), f32),
            jax.ShapeDtypeStruct((R, PADD), bf16),
        ],
        scratch_shapes=[pltpu.VMEM((R, PADD), f32)],
        compiler_params=pltpu.CompilerParams(vmem_limit_bytes=48 << 20),
        cost_estimate=pl.CostEstimate(
            flops=2_200_000_000, bytes_accessed=22_000_000, transcendentals=400_000
        ),
    )(cot, gate, up, hidden, gain, pad, *weight_args(gathered))


def attend_back_kernel(
    need_ref, qt_ref, kv_ref, bias_ref, dot_ref, mixed_ref, lse_ref, dkv_ref, dqt_ref
):
    q = heads_wide(qt_ref, True)
    d_o = heads_wide(dot_ref, False)
    o = heads_wide(mixed_ref, False)
    delta = jnp.sum(d_o * o.astype(f32), axis=0, keepdims=True)
    d_o = d_o.astype(bf16)
    lse = lse_ref[0]
    both = jnp.concatenate([q, d_o], axis=1)
    dkv_ref[...] = jnp.zeros_like(dkv_ref)

    def fold(pair, acc):
        for i in (2 * pair, 2 * pair + 1):
            kv = chunk_of(kv_ref, need_ref, i)
            b = bias_ref[chunk_rows(i), :]
            p = jnp.exp(mm(kv, q) + jnp.concatenate([b, b, b], axis=1) - lse)
            ds = (p * (mm(kv, d_o) - delta)).astype(bf16)
            part = mm_nt(jnp.concatenate([ds, p.astype(bf16)], axis=1), both).astype(bf16)
            for k in range(CHUNK // SMALL):
                at = pl.multiple_of(need_ref[CHUNK // SMALL * i + k] * SMALL, SMALL)
                dkv_ref[pl.ds(at, SMALL), :] = part[SMALL * k : SMALL * k + SMALL]
            acc = acc + mm(kv.T, ds)
        return acc

    acc = lax.fori_loop(0, need_ref[KEYS // SMALL], fold, jnp.zeros((128, LANES), f32))
    acc = acc[:64] * 0.125
    for h in range(GRP):
        dqt_ref[64 * h : 64 * h + 64, :] = acc[:, 128 * h : 128 * h + 128]


def attend_back(need, qt, kv_all, bias, d_mixed, mixed, lse):
    heads = pl.BlockSpec((GRP * HD, R), lambda g, n: (g, 0))
    return pl.pallas_call(
        attend_back_kernel,
        name="attend_back",
        grid_spec=pltpu.PrefetchScalarGridSpec(
            num_scalar_prefetch=1,
            grid=(SIDE,),
            in_specs=[
                heads,
                pl.BlockSpec((KEYS, 128), lambda g, n: (0, g)),
                pl.BlockSpec((KEYS, R), lambda g, n: (0, 0)),
                heads,
                heads,
                pl.BlockSpec((1, 1, LANES), lambda g, n: (g, 0, 0)),
            ],
            out_specs=[pl.BlockSpec((KEYS, 128), lambda g, n: (0, g)), heads],
        ),
        out_shape=[
            jax.ShapeDtypeStruct((KEYS, SIDE * 128), bf16),
            jax.ShapeDtypeStruct((QSIDE, R), f32),
        ],
        compiler_params=pltpu.CompilerParams(vmem_limit_bytes=48 << 20),
        cost_estimate=pl.CostEstimate(
            flops=6_000_000_000, bytes_accessed=10_000_000, transcendentals=4_700_000
        ),
    )(need, qt, kv_all, bias, d_mixed, mixed, lse)


def project_back_kernel(
    dqt_ref, dkv_ref, cos_ref, sin_ref, u_ref, g_ref, dh_ref, w_ref,
    du_ref, dqkv_ref, at_ref, dg_ref,
):
    cos, sin = cos_ref[...], sin_ref[...]
    lane = lane_of((R, 128))
    dkv = [dkv_ref[:, 128 * g : 128 * g + 128] for g in range(KVH)]
    rolled = [pltpu.roll(b, 64, 1) for b in dkv]
    zero = jnp.zeros((R, 128), f32)
    blocks = [dqt_ref[128 * c : 128 * c + 128, :].T for c in range(7)]
    last = jnp.concatenate([dqt_ref[896:960, :], jnp.zeros((64, R), f32)], axis=0).T
    low = lane < 64
    blocks.append(jnp.where(low, last, rolled[0]))
    blocks.append(jnp.where(low, dkv[1], rolled[2]))
    blocks.append(jnp.where(low, dkv[3], rolled[4]))
    blocks = [b * cos - half_swapped(b) * sin for b in blocks]
    blocks.append(jnp.where(low, rolled[0], dkv[1]))
    blocks.append(jnp.where(low, rolled[2], dkv[3]))
    blocks.append(jnp.where(low, rolled[4], zero))
    da = jnp.zeros((R, D), f32)
    for c in range(0, 13, 2):
        if c + 1 < 13:
            d = jnp.concatenate([blocks[c], blocks[c + 1]], axis=1).astype(bf16)
            w = jnp.concatenate([qkv_weight(w_ref, c), qkv_weight(w_ref, c + 1)], axis=1)
        else:
            d, w = blocks[c].astype(bf16), qkv_weight(w_ref, c)
        dqkv_ref[:, 128 * c : 128 * c + d.shape[1]] = d
        da = da + mm_nt(d, w)
    u = u_ref[...].astype(f32)
    gain = g_ref[...]
    _, a = normed_of(u, gain)
    at_ref[...] = a.T
    d_u, d_gain = norm_back(da, u, gain)
    dg_ref[...] = d_gain
    du_ref[...] = dh_ref[...] + d_u


def project_back(d_query, d_kv, cos, sin, u, gain, d_hidden, weights):
    whole = lambda *shape: pl.BlockSpec(shape, lambda j: (0,) * len(shape))
    return pl.pallas_call(
        project_back_kernel,
        name="project_back",
        grid=(1,),
        in_specs=[
            whole(D, R),
            whole(R, 640),
            whole(R, 128),
            whole(R, 128),
            whole(R, D),
            whole(1, D),
            whole(R, D),
            whole(10, ROWS, 128),
        ],
        out_specs=[whole(R, D), whole(R, 13 * 128), whole(D, R), whole(1, D)],
        out_shape=[
            jax.ShapeDtypeStruct((R, D), f32),
            jax.ShapeDtypeStruct((R, 13 * 128), bf16),
            jax.ShapeDtypeStruct((D, R), bf16),
            jax.ShapeDtypeStruct((1, D), f32),
        ],
        compiler_params=pltpu.CompilerParams(vmem_limit_bytes=48 << 20),
        cost_estimate=pl.CostEstimate(flops=400_000_000, bytes_accessed=5_000_000, transcendentals=0),
    )(d_query, d_kv, cos, sin, u, gain, d_hidden, weights)


def outer_steps(begin, end, refs, slot_ref, outs, stage, sems):
    step = pl.program_id(0) + begin
    buf = step % 2
    slot_y, slot_x = slot_ref[step // 4], slot_ref[4 + step % 4]
    zslot = [slot_ref[8 + k] for k in range(4)]
    out_ref = stage.at[buf]
    (a0, b0), (a1, b1), (a2, b2) = PART_ROWS
    k0, k1, k2, s0, s1, s2 = outs
    gain_ref, nt_ref, dgate_ref, dup_ref = refs[:4]

    def copy(i, buf, half=0):
        src = stage.at[buf]
        if i == 0:
            src, dst = src.at[:, a0:b0], (k0, s0)[half].at[slot_y % 2, slot_x]
        elif i == 1:
            src, dst = src.at[:, a1:b1], (k1, s1)[half].at[slot_x % 2, :, slot_y]
        elif i == 2:
            src, dst = src.at[0:2, a2:b2], k2.at[:, slot_y, slot_x]
        else:
            src, dst = src.at[2:4, a2:b2], s2.at[:, slot_y, slot_x]
        return pltpu.make_async_copy(src, dst, sems.at[buf, i])

    @pl.when(step >= begin + 2)
    def _():
        for i in range(4):
            copy(i, buf).wait()

    def row_of(k, count, at):
        row = lax.broadcasted_iota(jnp.int32, (count, 128), 0)
        return jnp.where(row == at, gain_ref[pl.ds(4 * step + k, 1), :], 0.0)

    def narrow(start, ks):
        count = len(ks)
        rows = at_ref[pl.ds(pl.multiple_of(start, 32), 96 * count), :]
        for c in range(0, 13, 2):
            width = min(256, 1664 - 128 * c)
            res = mm(rows, dqkv_ref[:, 128 * c : 128 * c + width])
            for i, k in enumerate(ks):
                for h in range(width // 128):
                    out_ref[zslot[k], 96 * (c + h) : 96 * (c + h) + 96, :] = res[
                        96 * i : 96 * i + 96, 128 * h : 128 * h + 128
                    ].astype(bf16)
        for k in ks:
            out_ref[zslot[k], 1248:1280, :] = row_of(k, 32, 0).astype(bf16)

    def wide(ref, start, cot_ref, ks):
        rows = ref[pl.ds(pl.multiple_of(start, 32), 160 * len(ks)), :]
        for c in range(0, 8, 2):
            res = mm(rows, cot_ref[:, 128 * c : 128 * c + 256])
            for i, k in enumerate(ks):
                for h in range(2):
                    b = res[160 * i : 160 * i + 160, 128 * h : 128 * h + 128]
                    if c + h == 7:
                        b = b + row_of(k, 160, 0)
                    at = 160 * (c + h)
                    out_ref[zslot[k], at : at + 160, :] = b.astype(bf16)

    def broad():
        rows = nt_ref[pl.ds(pl.multiple_of(128 * (step - 4), 128), 128), :]
        for part, ref in enumerate((dgate_ref, dup_ref)):
            for c in range(0, 20, 2):
                res = mm(rows, ref[:, 128 * c : 128 * c + 256])
                for k in range(4):
                    for h in range(2):
                        b = res[32 * k : 32 * k + 32, 128 * h : 128 * h + 128]
                        at = 32 * (20 * part + c + h)
                        if at == 0:
                            b = b + row_of(k, 32, 30)
                        out_ref[zslot[k], at : at + 32, :] = b.astype(bf16)

    if begin == 0:
        at_ref, dqkv_ref, mixed_ref, dhb_ref = refs[4:]

        @pl.when(step < 2)
        def _():
            narrow(384 * step, (0, 1, 2, 3))

        @pl.when(step == 2)
        def _():
            narrow(768, (0, 1))
            wide(mixed_ref, 0, dhb_ref, (2, 3))

        @pl.when(step == 3)
        def _():
            wide(mixed_ref, 320, dhb_ref, (0, 1, 2, 3))

        @pl.when(step >= 4)
        def _():
            broad()

    else:
        mt_ref, cb_ref = refs[4:]

        @pl.when(step < 12)
        def _():
            broad()

        @pl.when(step >= 12)
        def _():
            wide(mt_ref, 640 * (step - 12), cb_ref, (0, 1, 2, 3))

    for half in range(2):

        @pl.when(slot_y // 2 == half)
        def _(half=half):
            copy(0, buf, half).start()

        @pl.when(slot_x // 2 == half)
        def _(half=half):
            copy(1, buf, half).start()

    copy(2, buf).start()
    copy(3, buf).start()

    @pl.when(step == end - 1)
    def _():
        for last in (0, 1):
            for i in range(4):
                copy(i, last).wait()


def outer_late_kernel(slot_ref, *refs):
    outer_steps(0, 8, refs[:8], slot_ref, refs[14:20], *refs[20:])


def outer_early_kernel(slot_ref, *refs):
    outer_steps(8, 16, refs[:6], slot_ref, refs[6:12], *refs[12:])


def outer(slots, args, made=None):
    whole = lambda v: pl.BlockSpec(v.shape, lambda s, slot: (0,) * v.ndim)
    shapes = [
        jax.ShapeDtypeStruct((2, 4, 4, end - begin, 128), bf16) for begin, end in PART_ROWS
    ]
    made = made or []
    return pl.pallas_call(
        outer_late_kernel if made else outer_early_kernel,
        name="outer_late" if made else "outer_early",
        grid_spec=pltpu.PrefetchScalarGridSpec(
            num_scalar_prefetch=1,
            grid=(8,),
            in_specs=[whole(v) for v in args] + [pl.BlockSpec(memory_space=pl.ANY)] * len(made),
            out_specs=[pl.BlockSpec(memory_space=pl.ANY)] * 6,
            scratch_shapes=[
                pltpu.VMEM((2, 4, ROWS, 128), bf16),
                pltpu.SemaphoreType.DMA((2, 4)),
            ],
        ),
        out_shape=shapes * 2,
        input_output_aliases={1 + len(args) + i: i for i in range(len(made))},
        compiler_params=pltpu.CompilerParams(vmem_limit_bytes=48 << 20),
        cost_estimate=pl.CostEstimate(
            flops=1_300_000_000, bytes_accessed=12_000_000, transcendentals=0
        ),
    )(slots, *args, *made)


def shard_kind(rank):
    return jnp.where(rank < 10, 0, jnp.where((rank >= 16) & (rank < 48), 2, 1))


def shard_blocks(flat, rank):
    def narrow(_):
        w = jnp.pad(flat.reshape(96, 1600), ((0, 0), (0, 64)))
        w = w.reshape(96, 13, 128).transpose(1, 0, 2).reshape(1248, 128)
        return jnp.pad(w, ((0, 32), (0, 0)))

    def square(_):
        w = jnp.pad(flat.reshape(160, 960), ((0, 0), (0, 64)))
        return w.reshape(160, 8, 128).transpose(1, 0, 2).reshape(ROWS, 128)

    def broad(_):
        w = jnp.pad(flat.reshape(30, 40, 128), ((0, 2), (0, 0), (0, 0)))
        return w.transpose(1, 0, 2).reshape(ROWS, 128)

    return lax.switch(shard_kind(rank), [narrow, square, broad], 0)


def blocks_shard(blocks, rank):
    def narrow(_):
        w = blocks[:1248].reshape(13, 96, 128).transpose(1, 0, 2).reshape(96, 1664)[:, :1600]
        return w.reshape(SHARD), blocks[1248, :30]

    def square(_):
        w = blocks.reshape(8, 160, 128).transpose(1, 0, 2).reshape(160, 1024)[:, :960]
        return w.reshape(SHARD), blocks[1120, 64:94]

    def broad(_):
        w = blocks.reshape(40, 32, 128).transpose(1, 0, 2)[:30]
        return w.reshape(SHARD), blocks[30, :30]

    return lax.switch(shard_kind(rank), [narrow, square, broad], 0)


def gain_rows(one, two):
    gains = jnp.concatenate([one, two], axis=1).reshape(SHARDS, 30)
    shards = jnp.arange(SHARDS, dtype=jnp.int32)
    square = (((shards >= 10) & (shards < 16)) | (shards >= 48))[:, None]
    return jnp.where(
        square, jnp.pad(gains, ((0, 0), (64, 34))), jnp.pad(gains, ((0, 0), (0, 98)))
    )


def per_device(layer_in, out_grad, segment_ids, block_pair, params, norm_gains):
    phase = lax.axis_index("phase")
    ctx = lax.axis_index("ctx")
    rank = ctx * 2 + lax.axis_index("fsdp")
    y, x, z = rank // 16, (rank // 4) % 4, rank % 4
    zh = z // 2

    own = shard_blocks(params[0], rank)
    front, own = gather_front(own, norm_gains[0], y, phase)
    gathered = lax.all_gather(own, ("ctx", "fsdp"), axis=0)

    seg_row = segment_ids[0]
    pair = lax.dynamic_index_in_dim(block_pair, ctx, 0, keepdims=False)
    within = jnp.arange(HD, dtype=jnp.int32)
    place_q = jnp.concatenate([pair * 64 + within, (63 - pair) * 64 + within])
    seg_q = jnp.concatenate(
        [
            lax.dynamic_slice_in_dim(seg_row, pair * 64, 64),
            lax.dynamic_slice_in_dim(seg_row, (63 - pair) * 64, 64),
        ]
    )
    start_q = jnp.sum((seg_row[:, None] < seg_q[None, :]).astype(jnp.int32), axis=0)
    pairs_k = block_pair[key_order(y, x, zh, phase)]
    spot_k = jnp.stack([pairs_k, 63 - pairs_k], axis=1).reshape(64)
    seen_by = lambda at, spot: (spot_k <= spot) & (spot_k * 64 + 63 >= start_q[at])
    seen = seen_by(0, pair) | seen_by(64, 63 - pair)
    seen_count = jnp.sum(seen.astype(jnp.int32))
    before = jnp.arange(64)[:, None] > jnp.arange(64)[None, :]
    rank_seen = jnp.sum((before & seen[None, :]).astype(jnp.int32), axis=1)
    rank_k = jnp.where(seen, rank_seen, seen_count + jnp.arange(64) - rank_seen)
    chosen = rank_k[None, :] == jnp.arange(64)[:, None]
    order_k = jnp.sum(jnp.where(chosen, jnp.arange(64)[None, :], 0), axis=1)
    spot_k = jnp.sum(jnp.where(chosen & seen[None, :], spot_k[None, :], 0), axis=1)
    spot_k = jnp.where(jnp.arange(64) < seen_count, spot_k, 1 << 16)
    need = jnp.concatenate([order_k, ((seen_count + 15) // 16)[None]]).astype(jnp.int32)
    place_k = (spot_k[:, None] * 64 + within[None, :]).reshape(KEYS)
    bias = jnp.where(
        (place_k[:, None] <= place_q[None, :]) & (place_k[:, None] >= start_q[None, :]),
        0.0,
        masked_fill,
    ).astype(f32)
    frequency = rope_theta ** (-2.0 * jnp.arange(HD // 2, dtype=f32) / HD)
    angles = (place_q - start_q).astype(f32)[:, None] * frequency[None, :]
    cosine, sine = jnp.cos(angles), jnp.sin(angles)
    cos = jnp.concatenate([cosine] * 4, axis=1)
    sin = jnp.concatenate([-sine, sine, -sine, sine], axis=1)
    spread = jnp.arange(PADD, dtype=jnp.int32)
    target = jnp.where(spread % 32 < 30, (spread // 32) * 30 + spread % 32, -1)
    pad = (jnp.arange(D, dtype=jnp.int32)[:, None] == target[None, :]).astype(bf16)

    four = jnp.arange(4, dtype=jnp.int32)
    slots_y, slots_x, slots_z = (slot_of(four ^ at_axis, phase) for at_axis in (y, x, z))
    idx = jnp.concatenate(
        [
            (slots_x[:, None] + 4 * slots_z[None, :]).reshape(16),
            (4 * slots_x[:, None] + slots_z[None, :]).reshape(16),
        ]
    )
    slots = jnp.concatenate([slots_y, slots_x, slots_z])
    gains = front[1][:, HALF : HALF + 4, :30][idx[16:]].astype(f32)
    gains = gains.transpose(1, 0, 2).reshape(1, 2 * D)
    gain_one, gain_two = gains[:, :D], gains[:, D:]
    first = phase == 0

    u = layer_in[0]
    mixed = None
    kept = []
    for tick in range(2):
        active = phase == tick
        qt, kv = project(u, gain_one, cos, sin, idx, front)
        kv_side = jnp.where(active, kv[:, :384], over(kv[:, 384:], tick))
        qt_side = jnp.where(active, qt[:QSIDE], over(qt[QSIDE:], tick))
        kv_all = gather_keys(kv_side)
        mixed_side, lse = attend(need, qt_side, kv_all, bias)
        kept.append((qt_side, kv_all, mixed_side, lse))
        far = over(mixed_side[: D - QSIDE], 1 - tick)
        whole = jnp.concatenate([mixed_side, far])
        mixed = whole if tick == 0 else jnp.where(active, whole, mixed)
        result, hidden, nt, gate, up, mt = feed(mixed, u, gain_two, pad, gathered)
        if tick == 0:
            u = jnp.where(first, u, over(result, 0))

    cot = out_grad[0]
    d_query = d_kv = made = None
    for tick in range(2):
        layer = 1 - tick
        active = phase == layer
        qt_side, kv_all, mixed_side, lse = kept[layer]
        dgate, dup, dh, dhb, dg_two, d_mixed, cb = feed_back(
            cot, gate, up, hidden, gain_two, pad, gathered
        )
        d_side = jnp.where(active, d_mixed[:QSIDE], over(d_mixed[QSIDE:], layer))
        if tick:
            made = outer(slots, (gain_rows(dg_two, dg_two), nt, dgate, dup, mt, cb))
        d_kv_all, dq_side = attend_back(need, qt_side, kv_all, bias, d_side, mixed_side, lse)
        dq_new = jnp.concatenate([dq_side, over(dq_side[: D - QSIDE], tick)])
        dkv_side, made = scatter_keys(d_kv_all, made)
        dkv_new = jnp.concatenate([dkv_side, over(dkv_side[:, :256], tick)], axis=1)
        d_query = dq_new if tick == 0 else jnp.where(active, dq_new, d_query)
        d_kv = dkv_new if tick == 0 else jnp.where(active, dkv_new, d_kv)
        d_u, dqkv, at, dg_one = project_back(
            d_query, d_kv, cos, sin, u, gain_one, dh, gathered
        )
        if tick == 0:
            cot = jnp.where(first, over(d_u.astype(bf16), 1).astype(f32), cot)

    made = outer(
        slots, (gain_rows(dg_one, dg_two), nt, dgate, dup, at, dqkv, mixed, dhb), list(made)
    )
    total = scatter_grads(made[:3], made[3:])
    param_part, gain_part = blocks_shard(total, rank)
    return (result[None, None], d_u[None, None], param_part[None], gain_part[None])


def solution(mesh):
    return jax.shard_map(
        per_device,
        mesh=mesh,
        in_specs=(
            P("fsdp", "ctx", None),
            P("fsdp", "ctx", None),
            P("fsdp", None),
            P(),
            P("phase", ("ctx", "fsdp")),
            P("phase", ("ctx", "fsdp")),
        ),
        out_specs=(
            P("phase", "fsdp", "ctx", None),
            P("phase", "fsdp", "ctx", None),
            P("phase", ("ctx", "fsdp")),
            P("phase", ("ctx", "fsdp")),
        ),
        check_vma=False,
    )
```

```python
import functools

import jax
import jax.numpy as jnp
from jax import lax
from jax.experimental import pallas as pl
from jax.experimental.pallas import tpu as pltpu
from jax.sharding import PartitionSpec as P

H = 15
KVH = 5
HD = 64
D = 960
FF = 2560
GRP = H // KVH
R = 128
SHARDS = 64
SHARD = 153600
ROWS = 1280
KEYS = 4096
CHUNK = 512
PADD = 1024
SIDE = 3
QSIDE = SIDE * GRP * HD
QPAD = 2 * QSIDE

eps = 1e-05
rope_theta = 100000.0
masked_fill = -1e30
f32 = jnp.float32
bf16 = jnp.bfloat16
ALL = ("phase", "ctx", "fsdp")

NT = (((1,), (1,)), ((), ()))


def mm(a, b):
    return jnp.dot(a, b, preferred_element_type=f32)


def mm_nt(a, b):
    return lax.dot_general(a, b, NT, preferred_element_type=f32)


STEPS = ((1, 3), (3, 1))


def swapped(block, way):
    pairs = []
    for p in range(2):
        dy, dx, dz = way(p)
        for y in range(4):
            for x in range(4):
                for z in range(4):
                    to = ((y ^ dy) * 4 + (x ^ dx)) * 4 + (z ^ dz)
                    pairs.append((p * 64 + (y * 4 + x) * 4 + z, p * 64 + to))
    return lax.ppermute(block, ALL, pairs)


def over(block, source):
    return lax.ppermute(block, "phase", [(source, 1 - source)])


def along(axes, number):
    def way(p):
        shift = [0, 0, 0]
        shift[axes[p]] = STEPS[p][number]
        return tuple(shift)

    return way


def far_z(p):
    return (0, 0, 2)


def gather_keys(kv):
    tail = kv.shape
    far = swapped(kv, far_z)
    near = kv
    orders = (((0, 1), (1, 0)), ((1, 0), (0, 1)))
    blocks = [near[None], far[None]]
    for leg in range(2):
        for number in range(2):
            if leg and number:
                blocks = list(lax.optimization_barrier(tuple(blocks)))
            for k in range(2):
                got = swapped(blocks[k], along(orders[k][leg], number))
                blocks[k] = jnp.concatenate([blocks[k], got], axis=0)
    return jnp.concatenate(blocks, axis=0).reshape(KEYS, tail[1])


def scatter_keys(d_kv, beside=None):
    parts = d_kv.reshape(2, 16, R, d_kv.shape[1])
    orders = (((0, 1), (1, 0)), ((1, 0), (0, 1)))
    blocks = [parts[0], parts[1]]
    for leg in (1, 0):
        for number in (1, 0):
            for k in (1, 0):
                half = blocks[k].shape[0] // 2
                got = swapped(blocks[k][half:], along(orders[k][leg], number))
                total = blocks[k][:half].astype(f32) + got.astype(f32)
                last = k == 0 and half == 1
                blocks[k] = total if last else total.astype(bf16)
            if beside is not None and leg and number:
                blocks, beside = lax.optimization_barrier((blocks, beside))
    return blocks[0][0] + swapped(blocks[1][0], far_z).astype(f32), beside


def slot_offsets(phase):
    return jnp.where(phase == 0, jnp.array([0, 1, 3, 2]), jnp.array([0, 3, 1, 2]))


def slot_of(offset, phase):
    at = jnp.where(phase == 0, jnp.array([0, 1, 3, 2]), jnp.array([0, 2, 3, 1]))
    return at[offset]


def key_order(y, x, zh, phase):
    off = slot_offsets(phase)
    outer = jnp.repeat(off, 4)
    inner = jnp.tile(off, 4)
    out = []
    for k in range(2):
        first_y = phase == k
        oy = jnp.where(first_y, inner, outer)
        ox = jnp.where(first_y, outer, inner)
        out.append((y ^ oy) * 8 + (x ^ ox) * 2 + (zh ^ k))
    return jnp.concatenate(out)


HALF = ROWS // 2


def gather_front(own, gains, y, phase):
    row = jnp.pad(gains[None], ((0, 15), (0, 98)))
    block = jnp.concatenate([own, row])[None]
    for number in range(2):
        block = jnp.concatenate([block, swapped(block, along((0, 0), number))])
    at = slot_of(jnp.arange(4, dtype=jnp.int32) ^ y, phase)
    front = lax.dynamic_index_in_dim(block, at[0], 0, keepdims=False)
    rows = jnp.pad(block[:, ROWS][at], ((0, 12), (0, 0)))
    blocks = [front[None, :HALF], jnp.concatenate([front[HALF:ROWS], rows])[None]]
    axes = ((1, 2), (2, 1))
    for leg in range(2):
        for number in range(2):
            for part in range(2):
                axis = axes[part][leg]
                got = swapped(blocks[part], along((axis, axis), number))
                blocks[part] = jnp.concatenate([blocks[part], got])
    return blocks, own


PART_ROWS = ((0, 432), (432, 864), (864, 1280))


PART_AXES = ((0, 1, 2), (1, 2, 0), (2, 0, 1))


def scatter_grads(keep, send):
    keep, send = list(keep), list(send)
    for leg in range(3):
        for number in (1, 0):
            for part, axes in enumerate(PART_AXES):
                axis = axes[leg]
                got = swapped(send[part], along((axis, axis), number))
                mine = keep[part]

                def total(at, mine=mine, got=got):
                    return mine[at].astype(f32) + got[at].astype(f32)

                if number:
                    keep[part] = total(0).astype(bf16)
                    send[part] = total(1).astype(bf16)
                elif leg < 2:
                    keep[part] = total(slice(0, 2)).astype(bf16)
                    send[part] = total(slice(2, 4)).astype(bf16)
                else:
                    keep[part] = total(slice(None))
    return jnp.concatenate(keep)


def lane_of(shape):
    return lax.broadcasted_iota(jnp.int32, shape, len(shape) - 1)


def half_swapped(block):
    lane = lane_of(block.shape)
    return jnp.where(lane % HD < HD // 2, pltpu.roll(block, 96, 1), pltpu.roll(block, 32, 1))


def normed_of(u, gain):
    scale = lax.rsqrt(jnp.mean(u * u, axis=-1, keepdims=True) + eps)
    return scale, (u * scale * gain).astype(bf16)


def front_weight(idx_ref, wa_ref, wb_ref, c):
    pieces = []
    for d in range(10):
        low, high = 96 * c, 96 * c + 96
        if low < HALF:
            pieces.append(wa_ref[idx_ref[d], low : min(high, HALF), :])
        if high > HALF:
            pieces.append(wb_ref[idx_ref[16 + d], max(low, HALF) - HALF : high - HALF, :])
    return jnp.concatenate(pieces, axis=0)


def project_kernel(idx_ref, u_ref, g_ref, cos_ref, sin_ref, wa_ref, wb_ref, qt_ref, kv_ref):
    u = u_ref[...].astype(f32)
    _, a = normed_of(u, g_ref[...])
    cos, sin = cos_ref[...], sin_ref[...]
    blocks = []
    for c in range(0, 13, 2):
        w = front_weight(idx_ref, wa_ref, wb_ref, c)
        if c + 1 < 13:
            w = jnp.concatenate([w, front_weight(idx_ref, wa_ref, wb_ref, c + 1)], axis=1)
        y = mm(a, w)
        for k in range(w.shape[1] // 128):
            b = y[:, 128 * k : 128 * k + 128]
            if c + k < 10:
                b = b * cos + half_swapped(b) * sin
            blocks.append(b)
    for c in range(8):
        t = (blocks[c].astype(bf16).astype(f32) * 0.125).T.astype(bf16)
        count = 128 if c < 7 else 64
        qt_ref[128 * c : 128 * c + count, :] = t[:count]
    qt_ref[D:, :] = jnp.zeros((QPAD - D, R), bf16)
    kv_ref[:, 640:] = jnp.zeros((R, 128), bf16)
    lane = lane_of((R, 128))
    for g in range(KVH):
        k, v = blocks[(15 + g) // 2], blocks[(20 + g) // 2]
        if (15 + g) % 2:
            k = pltpu.roll(k, 64, 1)
        if (20 + g) % 2 == 0:
            v = pltpu.roll(v, 64, 1)
        kv_ref[:, 128 * g : 128 * g + 128] = jnp.where(lane < 64, k, v).astype(bf16)


def project(u, gain, cos, sin, idx, front):
    whole = lambda *shape: pl.BlockSpec(shape, lambda i, idx: (0,) * len(shape))
    return pl.pallas_call(
        project_kernel,
        name="project",
        grid_spec=pltpu.PrefetchScalarGridSpec(
            num_scalar_prefetch=1,
            grid=(1,),
            in_specs=[
                whole(R, D),
                whole(1, D),
                whole(R, 128),
                whole(R, 128),
                whole(16, HALF, 128),
                whole(16, HALF + 16, 128),
            ],
            out_specs=[whole(QPAD, R), whole(R, 768)],
        ),
        out_shape=[
            jax.ShapeDtypeStruct((QPAD, R), bf16),
            jax.ShapeDtypeStruct((R, 768), bf16),
        ],
        compiler_params=pltpu.CompilerParams(vmem_limit_bytes=22 << 20),
        cost_estimate=pl.CostEstimate(flops=400_000_000, bytes_accessed=6_000_000, transcendentals=0),
    )(idx, u, gain, cos, sin, *front)


def heads_wide(ref, low):
    top = jnp.concatenate([ref[64 * h : 64 * h + 64, :] for h in range(GRP)], axis=1)
    zero = jnp.zeros_like(top)
    return jnp.concatenate([top, zero] if low else [zero, top], axis=0)


SMALL = 64
LANES = GRP * R


def chunk_of(kv_ref, need_ref, i):
    rows = [
        kv_ref[pl.ds(pl.multiple_of(need_ref[CHUNK // SMALL * i + k] * SMALL, SMALL), SMALL), :]
        for k in range(CHUNK // SMALL)
    ]
    return jnp.concatenate(rows, axis=0)


def chunk_rows(i):
    return pl.ds(pl.multiple_of(i * CHUNK, CHUNK), CHUNK)


def attend_kernel(need_ref, qt_ref, kv_ref, bias_ref, mixed_ref, lse_ref, s_ref, c_ref):
    q = heads_wide(qt_ref, True)
    count = need_ref[KEYS // SMALL]

    def score(pair, peak):
        for i in (2 * pair, 2 * pair + 1):
            kv = chunk_of(kv_ref, need_ref, i)
            c_ref[chunk_rows(i), :] = kv
            b = bias_ref[chunk_rows(i), :]
            s = mm(kv, q) + jnp.concatenate([b, b, b], axis=1)
            s_ref[chunk_rows(i), :] = s
            peak = jnp.maximum(peak, jnp.max(s, axis=0, keepdims=True))
        return peak

    peak = lax.fori_loop(0, count, score, jnp.full((1, LANES), masked_fill, f32))

    def mix(pair, state):
        total, acc = state
        for i in (2 * pair, 2 * pair + 1):
            p = jnp.exp(s_ref[chunk_rows(i), :] - peak)
            total = total + jnp.sum(p, axis=0, keepdims=True)
            acc = acc + mm(c_ref[chunk_rows(i), :].T, p.astype(bf16))
        return total, acc

    total, acc = lax.fori_loop(
        0, count, mix, (jnp.zeros((1, LANES), f32), jnp.zeros((128, LANES), f32))
    )
    lse_ref[0] = peak + jnp.log(total)
    o = (acc[64:] / total).astype(bf16)
    for h in range(GRP):
        mixed_ref[64 * h : 64 * h + 64, :] = o[:, 128 * h : 128 * h + 128]


def attend(need, qt, kv_all, bias):
    return pl.pallas_call(
        attend_kernel,
        name="attend",
        grid_spec=pltpu.PrefetchScalarGridSpec(
            num_scalar_prefetch=1,
            grid=(SIDE,),
            in_specs=[
                pl.BlockSpec((GRP * HD, R), lambda g, n: (g, 0)),
                pl.BlockSpec((KEYS, 128), lambda g, n: (0, g)),
                pl.BlockSpec((KEYS, R), lambda g, n: (0, 0)),
            ],
            out_specs=[
                pl.BlockSpec((GRP * HD, R), lambda g, n: (g, 0)),
                pl.BlockSpec((1, 1, LANES), lambda g, n: (g, 0, 0)),
            ],
            scratch_shapes=[pltpu.VMEM((KEYS, LANES), f32), pltpu.VMEM((KEYS, 128), bf16)],
        ),
        out_shape=[
            jax.ShapeDtypeStruct((QSIDE, R), bf16),
            jax.ShapeDtypeStruct((SIDE, 1, LANES), f32),
        ],
        compiler_params=pltpu.CompilerParams(vmem_limit_bytes=24 << 20),
        cost_estimate=pl.CostEstimate(
            flops=2_400_000_000, bytes_accessed=6_000_000, transcendentals=4_700_000
        ),
    )(need, qt, kv_all, bias)


def out_weight(refs, c):
    return jnp.concatenate(
        [ref[:, 160 * c : 160 * c + 160, :].reshape(320, 128) for ref in refs], axis=0
    )


def gu_weight(refs, c):
    gl, gh, ul, uh = refs
    gate = jnp.concatenate([gl[:, c].reshape(512, 128), gh[:, c].reshape(512, 128)], axis=0)
    up = jnp.concatenate([ul[:, c].reshape(512, 128), uh[:, c].reshape(512, 128)], axis=0)
    return jnp.concatenate([gate, up], axis=1)


def down_weight(ref, c):
    return ref[:, 160 * c : 160 * c + 160, :].reshape(640, 128)


WEIGHT_SPECS = (
    [pl.BlockSpec((2, ROWS, 128), lambda j, k=k: (5 + k, 0, 0)) for k in range(3)]
    + [
        pl.BlockSpec((16, 5, 32, 128), lambda j, d=d, o=o: (1 + d, o + j, 0, 0))
        for o in (0, 4)
        for d in (0, 1)
    ]
    + [pl.BlockSpec((4, ROWS, 128), lambda j: (12 + j, 0, 0))]
)


def weight_args(gathered):
    fine = gathered.reshape(SHARDS, 40, 32, 128)
    return [gathered] * 3 + [fine] * 4 + [gathered]


def feed_kernel(
    mixed_ref, u_ref, g_ref, pad_ref, o0, o1, o2, gl, gh, ul, uh, wd,
    y_ref, h_ref, nt_ref, gate_ref, up_ref, mt_ref, n_scr, y_scr,
):
    step = pl.program_id(0)

    @pl.when(step == 0)
    def _():
        mixed = mixed_ref[...].T
        for c in range(0, 8, 2):
            w = jnp.concatenate(
                [out_weight((o0, o1, o2), c), out_weight((o0, o1, o2), c + 1)], axis=1
            )
            y = mm(mixed, w)
            end = min(128 * c + 256, D)
            h_ref[:, 128 * c : end] = u_ref[:, 128 * c : end].astype(f32) + y[:, : end - 128 * c]
        _, n = normed_of(h_ref[...], g_ref[...])
        padded = mm(n, pad_ref[...])
        n_scr[...] = padded.astype(bf16)
        nt_ref[...] = padded.T.astype(bf16)
        y_scr[...] = jnp.zeros_like(y_scr)

    n = n_scr[...]
    inner = []
    for c in range(5):
        gu = mm(n, gu_weight((gl, gh, ul, uh), c))
        gate, up = gu[:, :128], gu[:, 128:]
        cols = slice(128 * c, 128 * c + 128)
        gate_ref[:, cols] = gate
        up_ref[:, cols] = up
        m = gate * jax.nn.sigmoid(gate) * up
        mt_ref[cols, :] = m.T.astype(bf16)
        inner.append(m.astype(bf16))
    inner = jnp.concatenate(inner, axis=1)
    for c in range(0, 8, 2):
        w = jnp.concatenate([down_weight(wd, c), down_weight(wd, c + 1)], axis=1)
        y_scr[:, 128 * c : 128 * c + 256] += mm(inner, w)

    @pl.when(step == 3)
    def _():
        y_ref[...] = (h_ref[...] + y_scr[:, :D]).astype(bf16)


def feed(mixed, u, gain, pad, gathered):
    whole = lambda *shape: pl.BlockSpec(shape, lambda j: (0,) * len(shape))
    return pl.pallas_call(
        feed_kernel,
        name="feed",
        grid=(4,),
        in_specs=[whole(D, R), whole(R, D), whole(1, D), whole(D, PADD)] + WEIGHT_SPECS,
        out_specs=[
            whole(R, D),
            whole(R, D),
            whole(PADD, R),
            pl.BlockSpec((R, 640), lambda j: (0, j)),
            pl.BlockSpec((R, 640), lambda j: (0, j)),
            pl.BlockSpec((640, R), lambda j: (j, 0)),
        ],
        out_shape=[
            jax.ShapeDtypeStruct((R, D), bf16),
            jax.ShapeDtypeStruct((R, D), f32),
            jax.ShapeDtypeStruct((PADD, R), bf16),
            jax.ShapeDtypeStruct((R, FF), f32),
            jax.ShapeDtypeStruct((R, FF), f32),
            jax.ShapeDtypeStruct((FF, R), bf16),
        ],
        scratch_shapes=[pltpu.VMEM((R, PADD), bf16), pltpu.VMEM((R, PADD), f32)],
        compiler_params=pltpu.CompilerParams(vmem_limit_bytes=30 << 20),
        cost_estimate=pl.CostEstimate(
            flops=2_200_000_000, bytes_accessed=22_000_000, transcendentals=400_000
        ),
    )(mixed, u, gain, pad, *weight_args(gathered))


def norm_back(d_out, values, gain):
    scales = lax.rsqrt(jnp.mean(values * values, axis=-1, keepdims=True) + eps)
    scaled = d_out * gain
    d_gain = jnp.sum(d_out * values * scales, axis=0, keepdims=True)
    d_values = scales * scaled - values * (scales * scales * scales) * jnp.mean(
        scaled * values, axis=-1, keepdims=True
    )
    return d_values, d_gain


def feed_back_kernel(
    c_ref, gate_ref, up_ref, h_ref, g_ref, pad_ref, o0, o1, o2, gl, gh, ul, uh, wd,
    dgate_ref, dup_ref, dh_ref, dhb_ref, dg_ref, dot_ref, cb_ref, dn_scr,
):
    step = pl.program_id(0)

    @pl.when(step == 0)
    def _():
        cb_ref[...] = jnp.zeros_like(cb_ref)
        cb_ref[:, :D] = c_ref[...].astype(bf16)
        dn_scr[...] = jnp.zeros_like(dn_scr)

    d_inner = jnp.zeros((R, 640), f32)
    for c in range(0, 8, 2):
        w = jnp.concatenate([down_weight(wd, c), down_weight(wd, c + 1)], axis=1)
        d_inner = d_inner + mm_nt(cb_ref[:, 128 * c : 128 * c + 256], w)
    for c in range(5):
        cols = slice(128 * c, 128 * c + 128)
        gate, up, dm = gate_ref[:, cols], up_ref[:, cols], d_inner[:, cols]
        sigma = jax.nn.sigmoid(gate)
        d_gate = (dm * up * sigma * (1.0 + gate * (1.0 - sigma))).astype(bf16)
        d_up = (dm * gate * sigma).astype(bf16)
        dgate_ref[:, cols] = d_gate
        dup_ref[:, cols] = d_up
        both = jnp.concatenate([d_gate, d_up], axis=1)
        dn_scr[...] += mm_nt(both, gu_weight((gl, gh, ul, uh), c))

    @pl.when(step == 3)
    def _():
        padded = dn_scr[...]
        high = padded.astype(bf16)
        low = (padded - high.astype(f32)).astype(bf16)
        dn = mm_nt(high, pad_ref[...]) + mm_nt(low, pad_ref[...])
        d_h, d_gain = norm_back(dn, h_ref[...], g_ref[...])
        d_h = c_ref[...] + d_h
        dg_ref[...] = d_gain
        dh_ref[...] = d_h
        dhb_ref[...] = jnp.zeros_like(dhb_ref)
        dhb_ref[:, :D] = d_h.astype(bf16)
        d_mixed = jnp.zeros((R, D), f32)
        for c in range(0, 8, 2):
            w = jnp.concatenate(
                [out_weight((o0, o1, o2), c), out_weight((o0, o1, o2), c + 1)], axis=1
            )
            d_mixed = d_mixed + mm_nt(dhb_ref[:, 128 * c : 128 * c + 256], w)
        dot_ref[:D, :] = d_mixed.T
        dot_ref[D:, :] = jnp.zeros((QPAD - D, R), f32)


def feed_back(cot, gate, up, hidden, gain, pad, gathered):
    whole = lambda *shape: pl.BlockSpec(shape, lambda j: (0,) * len(shape))
    block = pl.BlockSpec((R, 640), lambda j: (0, j))
    return pl.pallas_call(
        feed_back_kernel,
        name="feed_back",
        grid=(4,),
        in_specs=[whole(R, D), block, block, whole(R, D), whole(1, D), whole(D, PADD)]
        + WEIGHT_SPECS,
        out_specs=[
            block,
            block,
            whole(R, D),
            whole(R, PADD),
            whole(1, D),
            whole(QPAD, R),
            whole(R, PADD),
        ],
        out_shape=[
            jax.ShapeDtypeStruct((R, FF), bf16),
            jax.ShapeDtypeStruct((R, FF), bf16),
            jax.ShapeDtypeStruct((R, D), f32),
            jax.ShapeDtypeStruct((R, PADD), bf16),
            jax.ShapeDtypeStruct((1, D), f32),
            jax.ShapeDtypeStruct((QPAD, R), f32),
            jax.ShapeDtypeStruct((R, PADD), bf16),
        ],
        scratch_shapes=[pltpu.VMEM((R, PADD), f32)],
        compiler_params=pltpu.CompilerParams(vmem_limit_bytes=30 << 20),
        cost_estimate=pl.CostEstimate(
            flops=2_200_000_000, bytes_accessed=22_000_000, transcendentals=400_000
        ),
    )(cot, gate, up, hidden, gain, pad, *weight_args(gathered))


def attend_back_kernel(
    need_ref, qt_ref, kv_ref, bias_ref, dot_ref, mixed_ref, lse_ref, dkv_ref, dqt_ref
):
    q = heads_wide(qt_ref, True)
    d_o = heads_wide(dot_ref, False)
    o = heads_wide(mixed_ref, False)
    delta = jnp.sum(d_o * o.astype(f32), axis=0, keepdims=True)
    d_o = d_o.astype(bf16)
    lse = lse_ref[0]
    both = jnp.concatenate([q, d_o], axis=1)
    dkv_ref[...] = jnp.zeros_like(dkv_ref)

    def fold(i, acc):
        kv = chunk_of(kv_ref, need_ref, i)
        b = bias_ref[chunk_rows(i), :]
        p = jnp.exp(mm(kv, q) + jnp.concatenate([b, b, b], axis=1) - lse)
        ds = (p * (mm(kv, d_o) - delta)).astype(bf16)
        part = mm_nt(jnp.concatenate([ds, p.astype(bf16)], axis=1), both).astype(bf16)
        for k in range(CHUNK // SMALL):
            at = pl.multiple_of(need_ref[CHUNK // SMALL * i + k] * SMALL, SMALL)
            dkv_ref[pl.ds(at, SMALL), :] = part[SMALL * k : SMALL * k + SMALL]
        return acc + mm(kv.T, ds)

    acc = lax.fori_loop(0, need_ref[KEYS // SMALL + 1], fold, jnp.zeros((128, LANES), f32))
    acc = acc[:64] * 0.125
    for h in range(GRP):
        dqt_ref[64 * h : 64 * h + 64, :] = acc[:, 128 * h : 128 * h + 128]


def attend_back(need, qt, kv_all, bias, d_mixed, mixed, lse):
    heads = pl.BlockSpec((GRP * HD, R), lambda g, n: (g, 0))
    return pl.pallas_call(
        attend_back_kernel,
        name="attend_back",
        grid_spec=pltpu.PrefetchScalarGridSpec(
            num_scalar_prefetch=1,
            grid=(SIDE,),
            in_specs=[
                heads,
                pl.BlockSpec((KEYS, 128), lambda g, n: (0, g)),
                pl.BlockSpec((KEYS, R), lambda g, n: (0, 0)),
                heads,
                heads,
                pl.BlockSpec((1, 1, LANES), lambda g, n: (g, 0, 0)),
            ],
            out_specs=[pl.BlockSpec((KEYS, 128), lambda g, n: (0, g)), heads],
        ),
        out_shape=[
            jax.ShapeDtypeStruct((KEYS, SIDE * 128), bf16),
            jax.ShapeDtypeStruct((QSIDE, R), f32),
        ],
        compiler_params=pltpu.CompilerParams(vmem_limit_bytes=24 << 20),
        cost_estimate=pl.CostEstimate(
            flops=6_000_000_000, bytes_accessed=10_000_000, transcendentals=4_700_000
        ),
    )(need, qt, kv_all, bias, d_mixed, mixed, lse)


def project_back_kernel(
    idx_ref, dqt_ref, dkv_ref, cos_ref, sin_ref, u_ref, g_ref, dh_ref, wa_ref, wb_ref,
    du_ref, dqkv_ref, at_ref, dg_ref,
):
    cos, sin = cos_ref[...], sin_ref[...]
    lane = lane_of((R, 128))
    dkv = [dkv_ref[:, 128 * g : 128 * g + 128] for g in range(KVH)]
    rolled = [pltpu.roll(b, 64, 1) for b in dkv]
    zero = jnp.zeros((R, 128), f32)
    blocks = [dqt_ref[128 * c : 128 * c + 128, :].T for c in range(7)]
    last = jnp.concatenate([dqt_ref[896:960, :], jnp.zeros((64, R), f32)], axis=0).T
    low = lane < 64
    blocks.append(jnp.where(low, last, rolled[0]))
    blocks.append(jnp.where(low, dkv[1], rolled[2]))
    blocks.append(jnp.where(low, dkv[3], rolled[4]))
    blocks = [b * cos - half_swapped(b) * sin for b in blocks]
    blocks.append(jnp.where(low, rolled[0], dkv[1]))
    blocks.append(jnp.where(low, rolled[2], dkv[3]))
    blocks.append(jnp.where(low, rolled[4], zero))
    da = jnp.zeros((R, D), f32)
    for c in range(0, 13, 2):
        d, w = blocks[c].astype(bf16), front_weight(idx_ref, wa_ref, wb_ref, c)
        if c + 1 < 13:
            d = jnp.concatenate([d, blocks[c + 1].astype(bf16)], axis=1)
            w = jnp.concatenate([w, front_weight(idx_ref, wa_ref, wb_ref, c + 1)], axis=1)
        dqkv_ref[:, 128 * c : 128 * c + d.shape[1]] = d
        da = da + mm_nt(d, w)
    u = u_ref[...].astype(f32)
    gain = g_ref[...]
    _, a = normed_of(u, gain)
    at_ref[...] = a.T
    d_u, d_gain = norm_back(da, u, gain)
    dg_ref[...] = d_gain
    du_ref[...] = dh_ref[...] + d_u


def project_back(d_query, d_kv, cos, sin, u, gain, d_hidden, idx, front):
    whole = lambda *shape: pl.BlockSpec(shape, lambda j, idx: (0,) * len(shape))
    return pl.pallas_call(
        project_back_kernel,
        name="project_back",
        grid_spec=pltpu.PrefetchScalarGridSpec(
            num_scalar_prefetch=1,
            grid=(1,),
            in_specs=[
                whole(D, R),
                whole(R, 640),
                whole(R, 128),
                whole(R, 128),
                whole(R, D),
                whole(1, D),
                whole(R, D),
                whole(16, HALF, 128),
                whole(16, HALF + 16, 128),
            ],
            out_specs=[whole(R, D), whole(R, 13 * 128), whole(D, R), whole(1, D)],
        ),
        out_shape=[
            jax.ShapeDtypeStruct((R, D), f32),
            jax.ShapeDtypeStruct((R, 13 * 128), bf16),
            jax.ShapeDtypeStruct((D, R), bf16),
            jax.ShapeDtypeStruct((1, D), f32),
        ],
        compiler_params=pltpu.CompilerParams(vmem_limit_bytes=24 << 20),
        cost_estimate=pl.CostEstimate(flops=400_000_000, bytes_accessed=7_000_000, transcendentals=0),
    )(idx, d_query, d_kv, cos, sin, u, gain, d_hidden, *front)


def outer_steps(begin, end, refs, slot_ref, outs, stage, sems):
    step = pl.program_id(0) + begin
    buf = step % 2
    slot_y, slot_x = slot_ref[step // 4], slot_ref[4 + step % 4]
    zslot = [slot_ref[8 + k] for k in range(4)]
    out_ref = stage.at[buf]
    (a0, b0), (a1, b1), (a2, b2) = PART_ROWS
    k0, k1, k2, s0, s1, s2 = outs
    gain_ref, nt_ref, dgate_ref, dup_ref = refs[:4]

    def copy(i, buf, half=0):
        src = stage.at[buf]
        if i == 0:
            src, dst = src.at[:, a0:b0], (k0, s0)[half].at[slot_y % 2, slot_x]
        elif i == 1:
            src, dst = src.at[:, a1:b1], (k1, s1)[half].at[slot_x % 2, :, slot_y]
        elif i == 2:
            src, dst = src.at[0:2, a2:b2], k2.at[:, slot_y, slot_x]
        else:
            src, dst = src.at[2:4, a2:b2], s2.at[:, slot_y, slot_x]
        return pltpu.make_async_copy(src, dst, sems.at[buf, i])

    @pl.when(step >= begin + 2)
    def _():
        for i in range(4):
            copy(i, buf).wait()

    def row_of(k, count, at):
        row = lax.broadcasted_iota(jnp.int32, (count, 128), 0)
        return jnp.where(row == at, gain_ref[pl.ds(4 * step + k, 1), :], 0.0)

    def narrow(start, ks):
        count = len(ks)
        rows = at_ref[pl.ds(pl.multiple_of(start, 32), 96 * count), :]
        for c in range(0, 13, 2):
            width = min(256, 1664 - 128 * c)
            res = mm(rows, dqkv_ref[:, 128 * c : 128 * c + width])
            for i, k in enumerate(ks):
                for h in range(width // 128):
                    out_ref[zslot[k], 96 * (c + h) : 96 * (c + h) + 96, :] = res[
                        96 * i : 96 * i + 96, 128 * h : 128 * h + 128
                    ].astype(bf16)
        for k in ks:
            out_ref[zslot[k], 1248:1280, :] = row_of(k, 32, 0).astype(bf16)

    def wide(ref, start, cot_ref, ks):
        rows = ref[pl.ds(pl.multiple_of(start, 32), 160 * len(ks)), :]
        for c in range(0, 8, 2):
            res = mm(rows, cot_ref[:, 128 * c : 128 * c + 256])
            for i, k in enumerate(ks):
                for h in range(2):
                    b = res[160 * i : 160 * i + 160, 128 * h : 128 * h + 128]
                    if c + h == 7:
                        b = b + row_of(k, 160, 0)
                    at = 160 * (c + h)
                    out_ref[zslot[k], at : at + 160, :] = b.astype(bf16)

    def broad():
        rows = nt_ref[pl.ds(pl.multiple_of(128 * (step - 4), 128), 128), :]
        for part, ref in enumerate((dgate_ref, dup_ref)):
            for c in range(0, 20, 2):
                res = mm(rows, ref[:, 128 * c : 128 * c + 256])
                for k in range(4):
                    for h in range(2):
                        b = res[32 * k : 32 * k + 32, 128 * h : 128 * h + 128]
                        at = 32 * (20 * part + c + h)
                        if at == 0:
                            b = b + row_of(k, 32, 30)
                        out_ref[zslot[k], at : at + 32, :] = b.astype(bf16)

    if begin == 0:
        at_ref, dqkv_ref, mixed_ref, dhb_ref = refs[4:]

        @pl.when(step < 2)
        def _():
            narrow(384 * step, (0, 1, 2, 3))

        @pl.when(step == 2)
        def _():
            narrow(768, (0, 1))
            wide(mixed_ref, 0, dhb_ref, (2, 3))

        @pl.when(step == 3)
        def _():
            wide(mixed_ref, 320, dhb_ref, (0, 1, 2, 3))

        @pl.when(step >= 4)
        def _():
            broad()

    else:
        mt_ref, cb_ref = refs[4:]

        @pl.when(step < 12)
        def _():
            broad()

        @pl.when(step >= 12)
        def _():
            wide(mt_ref, 640 * (step - 12), cb_ref, (0, 1, 2, 3))

    for half in range(2):

        @pl.when(slot_y // 2 == half)
        def _(half=half):
            copy(0, buf, half).start()

        @pl.when(slot_x // 2 == half)
        def _(half=half):
            copy(1, buf, half).start()

    copy(2, buf).start()
    copy(3, buf).start()

    @pl.when(step == end - 1)
    def _():
        for last in (0, 1):
            for i in range(4):
                copy(i, last).wait()


def outer_late_kernel(slot_ref, *refs):
    outer_steps(0, 8, refs[:8], slot_ref, refs[14:20], *refs[20:])


def outer_early_kernel(slot_ref, *refs):
    outer_steps(8, 16, refs[:6], slot_ref, refs[6:12], *refs[12:])


def outer(slots, args, made=None):
    whole = lambda v: pl.BlockSpec(v.shape, lambda s, slot: (0,) * v.ndim)
    shapes = [
        jax.ShapeDtypeStruct((2, 4, 4, end - begin, 128), bf16) for begin, end in PART_ROWS
    ]
    made = made or []
    return pl.pallas_call(
        outer_late_kernel if made else outer_early_kernel,
        name="outer_late" if made else "outer_early",
        grid_spec=pltpu.PrefetchScalarGridSpec(
            num_scalar_prefetch=1,
            grid=(8,),
            in_specs=[whole(v) for v in args] + [pl.BlockSpec(memory_space=pl.ANY)] * len(made),
            out_specs=[pl.BlockSpec(memory_space=pl.ANY)] * 6,
            scratch_shapes=[
                pltpu.VMEM((2, 4, ROWS, 128), bf16),
                pltpu.SemaphoreType.DMA((2, 4)),
            ],
        ),
        out_shape=shapes * 2,
        input_output_aliases={1 + len(args) + i: i for i in range(len(made))},
        compiler_params=pltpu.CompilerParams(vmem_limit_bytes=20 << 20),
        cost_estimate=pl.CostEstimate(
            flops=1_300_000_000, bytes_accessed=12_000_000, transcendentals=0
        ),
    )(slots, *args, *made)


def shard_kind(rank):
    return jnp.where(rank < 10, 0, jnp.where((rank >= 16) & (rank < 48), 2, 1))


def shard_blocks(flat, rank):
    def narrow(_):
        w = jnp.pad(flat.reshape(96, 1600), ((0, 0), (0, 64)))
        w = w.reshape(96, 13, 128).transpose(1, 0, 2).reshape(1248, 128)
        return jnp.pad(w, ((0, 32), (0, 0)))

    def square(_):
        w = jnp.pad(flat.reshape(160, 960), ((0, 0), (0, 64)))
        return w.reshape(160, 8, 128).transpose(1, 0, 2).reshape(ROWS, 128)

    def broad(_):
        w = jnp.pad(flat.reshape(30, 40, 128), ((0, 2), (0, 0), (0, 0)))
        return w.transpose(1, 0, 2).reshape(ROWS, 128)

    return lax.switch(shard_kind(rank), [narrow, square, broad], 0)


def blocks_shard(blocks, rank):
    def narrow(_):
        w = blocks[:1248].reshape(13, 96, 128).transpose(1, 0, 2).reshape(96, 1664)[:, :1600]
        return w.reshape(SHARD), blocks[1248, :30]

    def square(_):
        w = blocks.reshape(8, 160, 128).transpose(1, 0, 2).reshape(160, 1024)[:, :960]
        return w.reshape(SHARD), blocks[1120, 64:94]

    def broad(_):
        w = blocks.reshape(40, 32, 128).transpose(1, 0, 2)[:30]
        return w.reshape(SHARD), blocks[30, :30]

    return lax.switch(shard_kind(rank), [narrow, square, broad], 0)


def gain_rows(one, two):
    gains = jnp.concatenate([one, two], axis=1).reshape(SHARDS, 30)
    shards = jnp.arange(SHARDS, dtype=jnp.int32)
    square = (((shards >= 10) & (shards < 16)) | (shards >= 48))[:, None]
    return jnp.where(
        square, jnp.pad(gains, ((0, 0), (64, 34))), jnp.pad(gains, ((0, 0), (0, 98)))
    )


def per_device(layer_in, out_grad, segment_ids, block_pair, params, norm_gains):
    phase = lax.axis_index("phase")
    ctx = lax.axis_index("ctx")
    rank = ctx * 2 + lax.axis_index("fsdp")
    y, x, z = rank // 16, (rank // 4) % 4, rank % 4
    zh = z // 2

    own = shard_blocks(params[0], rank)
    front, own = gather_front(own, norm_gains[0], y, phase)
    gathered = lax.all_gather(own, ("ctx", "fsdp"), axis=0)

    seg_row = segment_ids[0]
    pair = lax.dynamic_index_in_dim(block_pair, ctx, 0, keepdims=False)
    within = jnp.arange(HD, dtype=jnp.int32)
    place_q = jnp.concatenate([pair * 64 + within, (63 - pair) * 64 + within])
    seg_q = jnp.concatenate(
        [
            lax.dynamic_slice_in_dim(seg_row, pair * 64, 64),
            lax.dynamic_slice_in_dim(seg_row, (63 - pair) * 64, 64),
        ]
    )
    start_q = jnp.sum((seg_row[:, None] < seg_q[None, :]).astype(jnp.int32), axis=0)
    pairs_k = block_pair[key_order(y, x, zh, phase)]
    spot_k = jnp.stack([pairs_k, 63 - pairs_k], axis=1).reshape(64)
    seen_by = lambda at, spot: (spot_k <= spot) & (spot_k * 64 + 63 >= start_q[at])
    seen = seen_by(0, pair) | seen_by(64, 63 - pair)
    seen_count = jnp.sum(seen.astype(jnp.int32))
    before = jnp.arange(64)[:, None] > jnp.arange(64)[None, :]
    rank_seen = jnp.sum((before & seen[None, :]).astype(jnp.int32), axis=1)
    rank_k = jnp.where(seen, rank_seen, seen_count + jnp.arange(64) - rank_seen)
    chosen = rank_k[None, :] == jnp.arange(64)[:, None]
    order_k = jnp.sum(jnp.where(chosen, jnp.arange(64)[None, :], 0), axis=1)
    spot_k = jnp.sum(jnp.where(chosen & seen[None, :], spot_k[None, :], 0), axis=1)
    spot_k = jnp.where(jnp.arange(64) < seen_count, spot_k, 1 << 16)
    turns = jnp.stack([(seen_count + 15) // 16, (seen_count + 7) // 8])
    need = jnp.concatenate([order_k, turns]).astype(jnp.int32)
    place_k = (spot_k[:, None] * 64 + within[None, :]).reshape(KEYS)
    bias = jnp.where(
        (place_k[:, None] <= place_q[None, :]) & (place_k[:, None] >= start_q[None, :]),
        0.0,
        masked_fill,
    ).astype(f32)
    frequency = rope_theta ** (-2.0 * jnp.arange(HD // 2, dtype=f32) / HD)
    angles = (place_q - start_q).astype(f32)[:, None] * frequency[None, :]
    cosine, sine = jnp.cos(angles), jnp.sin(angles)
    cos = jnp.concatenate([cosine] * 4, axis=1)
    sin = jnp.concatenate([-sine, sine, -sine, sine], axis=1)
    spread = jnp.arange(PADD, dtype=jnp.int32)
    target = jnp.where(spread % 32 < 30, (spread // 32) * 30 + spread % 32, -1)
    pad = (jnp.arange(D, dtype=jnp.int32)[:, None] == target[None, :]).astype(bf16)

    four = jnp.arange(4, dtype=jnp.int32)
    slots_y, slots_x, slots_z = (slot_of(four ^ at_axis, phase) for at_axis in (y, x, z))
    idx = jnp.concatenate(
        [
            (slots_x[:, None] + 4 * slots_z[None, :]).reshape(16),
            (4 * slots_x[:, None] + slots_z[None, :]).reshape(16),
        ]
    )
    slots = jnp.concatenate([slots_y, slots_x, slots_z])
    gains = front[1][:, HALF : HALF + 4, :30][idx[16:]].astype(f32)
    gains = gains.transpose(1, 0, 2).reshape(1, 2 * D)
    gain_one, gain_two = gains[:, :D], gains[:, D:]
    first = phase == 0

    u = layer_in[0]
    mixed = None
    kept = []
    for tick in range(2):
        active = phase == tick
        qt, kv = project(u, gain_one, cos, sin, idx, front)
        kv_side = jnp.where(active, kv[:, :384], over(kv[:, 384:], tick))
        qt_side = jnp.where(active, qt[:QSIDE], over(qt[QSIDE:], tick))
        kv_all = gather_keys(kv_side)
        mixed_side, lse = attend(need, qt_side, kv_all, bias)
        kept.append((qt_side, kv_all, mixed_side, lse))
        far = over(mixed_side[: D - QSIDE], 1 - tick)
        whole = jnp.concatenate([mixed_side, far])
        mixed = whole if tick == 0 else jnp.where(active, whole, mixed)
        result, hidden, nt, gate, up, mt = feed(mixed, u, gain_two, pad, gathered)
        if tick == 0:
            u = jnp.where(first, u, over(result, 0))

    cot = out_grad[0]
    d_query = d_kv = made = None
    for tick in range(2):
        layer = 1 - tick
        active = phase == layer
        qt_side, kv_all, mixed_side, lse = kept[layer]
        dgate, dup, dh, dhb, dg_two, d_mixed, cb = feed_back(
            cot, gate, up, hidden, gain_two, pad, gathered
        )
        d_side = jnp.where(active, d_mixed[:QSIDE], over(d_mixed[QSIDE:], layer))
        if tick:
            made = outer(slots, (gain_rows(dg_two, dg_two), nt, dgate, dup, mt, cb))
        d_kv_all, dq_side = attend_back(need, qt_side, kv_all, bias, d_side, mixed_side, lse)
        dq_new = jnp.concatenate([dq_side, over(dq_side[: D - QSIDE], tick)])
        dkv_side, made = scatter_keys(d_kv_all, made)
        dkv_new = jnp.concatenate([dkv_side, over(dkv_side[:, :256], tick)], axis=1)
        d_query = dq_new if tick == 0 else jnp.where(active, dq_new, d_query)
        d_kv = dkv_new if tick == 0 else jnp.where(active, dkv_new, d_kv)
        d_u, dqkv, at, dg_one = project_back(
            d_query, d_kv, cos, sin, u, gain_one, dh, idx, front
        )
        if tick == 0:
            cot = jnp.where(first, over(d_u.astype(bf16), 1).astype(f32), cot)

    made = outer(
        slots, (gain_rows(dg_one, dg_two), nt, dgate, dup, at, dqkv, mixed, dhb), list(made)
    )
    total = scatter_grads(made[:3], made[3:])
    param_part, gain_part = blocks_shard(total, rank)
    return (result[None, None], d_u[None, None], param_part[None], gain_part[None])


def solution(mesh):
    return jax.shard_map(
        per_device,
        mesh=mesh,
        in_specs=(
            P("fsdp", "ctx", None),
            P("fsdp", "ctx", None),
            P("fsdp", None),
            P(),
            P("phase", ("ctx", "fsdp")),
            P("phase", ("ctx", "fsdp")),
        ),
        out_specs=(
            P("phase", "fsdp", "ctx", None),
            P("phase", "fsdp", "ctx", None),
            P("phase", ("ctx", "fsdp")),
            P("phase", ("ctx", "fsdp")),
        ),
        check_vma=False,
    )
```

```python
import functools

import jax
import jax.numpy as jnp
from jax import lax
from jax.experimental import pallas as pl
from jax.experimental.pallas import tpu as pltpu
from jax.sharding import PartitionSpec as P

H = 15
KVH = 5
HD = 64
D = 960
FF = 2560
GRP = H // KVH
R = 128
SHARDS = 64
SHARD = 153600
ROWS = 1280
KEYS = 4096
CHUNK = 512
PADD = 1024
SIDE = 3
QSIDE = SIDE * GRP * HD
QPAD = 2 * QSIDE

eps = 1e-05
rope_theta = 100000.0
masked_fill = -1e30
f32 = jnp.float32
bf16 = jnp.bfloat16
ALL = ("phase", "ctx", "fsdp")

NT = (((1,), (1,)), ((), ()))


def mm(a, b):
    return jnp.dot(a, b, preferred_element_type=f32)


def mm_nt(a, b):
    return lax.dot_general(a, b, NT, preferred_element_type=f32)


STEPS = ((1, 3), (3, 1))


def swapped(block, way):
    pairs = []
    for p in range(2):
        dy, dx, dz = way(p)
        for y in range(4):
            for x in range(4):
                for z in range(4):
                    to = ((y ^ dy) * 4 + (x ^ dx)) * 4 + (z ^ dz)
                    pairs.append((p * 64 + (y * 4 + x) * 4 + z, p * 64 + to))
    return lax.ppermute(block, ALL, pairs)


def over(block, source):
    return lax.ppermute(block, "phase", [(source, 1 - source)])


def along(axes, number):
    def way(p):
        shift = [0, 0, 0]
        shift[axes[p]] = STEPS[p][number]
        return tuple(shift)

    return way


def far_z(p):
    return (0, 0, 2)


def gather_keys(kv):
    tail = kv.shape
    far = swapped(kv, far_z)
    near = kv
    orders = (((0, 1), (1, 0)), ((1, 0), (0, 1)))
    blocks = [near[None], far[None]]
    for leg in range(2):
        for number in range(2):
            if leg and number:
                blocks = list(lax.optimization_barrier(tuple(blocks)))
            for k in range(2):
                got = swapped(blocks[k], along(orders[k][leg], number))
                blocks[k] = jnp.concatenate([blocks[k], got], axis=0)
    return jnp.concatenate(blocks, axis=0).reshape(KEYS, tail[1])


def scatter_keys(d_kv):
    parts = d_kv.reshape(2, 16, R, d_kv.shape[1])
    orders = (((0, 1), (1, 0)), ((1, 0), (0, 1)))
    blocks = [parts[0], parts[1]]
    for leg in (1, 0):
        for number in (1, 0):
            for k in (1, 0):
                half = blocks[k].shape[0] // 2
                got = swapped(blocks[k][half:], along(orders[k][leg], number))
                total = blocks[k][:half].astype(f32) + got.astype(f32)
                last = k == 0 and half == 1
                blocks[k] = total if last else total.astype(bf16)
    return blocks[0][0] + swapped(blocks[1][0], far_z).astype(f32)


def slot_offsets(phase):
    return jnp.where(phase == 0, jnp.array([0, 1, 3, 2]), jnp.array([0, 3, 1, 2]))


def slot_of(offset, phase):
    at = jnp.where(phase == 0, jnp.array([0, 1, 3, 2]), jnp.array([0, 2, 3, 1]))
    return at[offset]


def key_order(y, x, zh, phase):
    off = slot_offsets(phase)
    outer = jnp.repeat(off, 4)
    inner = jnp.tile(off, 4)
    out = []
    for k in range(2):
        first_y = phase == k
        oy = jnp.where(first_y, inner, outer)
        ox = jnp.where(first_y, outer, inner)
        out.append((y ^ oy) * 8 + (x ^ ox) * 2 + (zh ^ k))
    return jnp.concatenate(out)


HALF = ROWS // 2


def gather_front(own, gains, y, phase):
    row = jnp.pad(gains[None], ((0, 15), (0, 98)))
    block = jnp.concatenate([own, row])[None]
    for number in range(2):
        block = jnp.concatenate([block, swapped(block, along((0, 0), number))])
    at = slot_of(jnp.arange(4, dtype=jnp.int32) ^ y, phase)
    front = lax.dynamic_index_in_dim(block, at[0], 0, keepdims=False)
    rows = jnp.pad(block[:, ROWS][at], ((0, 12), (0, 0)))
    blocks = [front[None, :HALF], jnp.concatenate([front[HALF:ROWS], rows])[None]]
    axes = ((1, 2), (2, 1))
    for leg in range(2):
        for number in range(2):
            for part in range(2):
                axis = axes[part][leg]
                got = swapped(blocks[part], along((axis, axis), number))
                blocks[part] = jnp.concatenate([blocks[part], got])
    return blocks, own


PART_ROWS = ((0, 432), (432, 864), (864, 1280))


PART_AXES = ((0, 1, 2), (1, 2, 0), (2, 0, 1))


def scatter_grads(keep, send):
    keep, send = list(keep), list(send)
    for leg in range(3):
        for number in (1, 0):
            for part, axes in enumerate(PART_AXES):
                axis = axes[leg]
                got = swapped(send[part], along((axis, axis), number))
                mine = keep[part]

                def total(at, mine=mine, got=got):
                    return mine[at].astype(f32) + got[at].astype(f32)

                if number:
                    keep[part] = total(0).astype(bf16)
                    send[part] = total(1).astype(bf16)
                elif leg < 2:
                    keep[part] = total(slice(0, 2)).astype(bf16)
                    send[part] = total(slice(2, 4)).astype(bf16)
                else:
                    keep[part] = total(slice(None))
    return jnp.concatenate(keep)


def lane_of(shape):
    return lax.broadcasted_iota(jnp.int32, shape, len(shape) - 1)


def half_swapped(block):
    lane = lane_of(block.shape)
    return jnp.where(lane % HD < HD // 2, pltpu.roll(block, 96, 1), pltpu.roll(block, 32, 1))


def normed_of(u, gain):
    scale = lax.rsqrt(jnp.mean(u * u, axis=-1, keepdims=True) + eps)
    return scale, (u * scale * gain).astype(bf16)


def front_weight(idx_ref, wa_ref, wb_ref, c):
    pieces = []
    for d in range(10):
        low, high = 96 * c, 96 * c + 96
        if low < HALF:
            pieces.append(wa_ref[idx_ref[d], low : min(high, HALF), :])
        if high > HALF:
            pieces.append(wb_ref[idx_ref[16 + d], max(low, HALF) - HALF : high - HALF, :])
    return jnp.concatenate(pieces, axis=0)


def project_kernel(idx_ref, u_ref, g_ref, cos_ref, sin_ref, wa_ref, wb_ref, qt_ref, kv_ref):
    u = u_ref[...].astype(f32)
    _, a = normed_of(u, g_ref[...])
    cos, sin = cos_ref[...], sin_ref[...]
    blocks = []
    for c in range(0, 13, 2):
        w = front_weight(idx_ref, wa_ref, wb_ref, c)
        if c + 1 < 13:
            w = jnp.concatenate([w, front_weight(idx_ref, wa_ref, wb_ref, c + 1)], axis=1)
        y = mm(a, w)
        for k in range(w.shape[1] // 128):
            b = y[:, 128 * k : 128 * k + 128]
            if c + k < 10:
                b = b * cos + half_swapped(b) * sin
            blocks.append(b)
    for c in range(8):
        t = (blocks[c].astype(bf16).astype(f32) * 0.125).T.astype(bf16)
        count = 128 if c < 7 else 64
        qt_ref[128 * c : 128 * c + count, :] = t[:count]
    qt_ref[D:, :] = jnp.zeros((QPAD - D, R), bf16)
    kv_ref[:, 640:] = jnp.zeros((R, 128), bf16)
    lane = lane_of((R, 128))
    for g in range(KVH):
        k, v = blocks[(15 + g) // 2], blocks[(20 + g) // 2]
        if (15 + g) % 2:
            k = pltpu.roll(k, 64, 1)
        if (20 + g) % 2 == 0:
            v = pltpu.roll(v, 64, 1)
        kv_ref[:, 128 * g : 128 * g + 128] = jnp.where(lane < 64, k, v).astype(bf16)


def project(u, gain, cos, sin, idx, front):
    whole = lambda *shape: pl.BlockSpec(shape, lambda i, idx: (0,) * len(shape))
    return pl.pallas_call(
        project_kernel,
        name="project",
        grid_spec=pltpu.PrefetchScalarGridSpec(
            num_scalar_prefetch=1,
            grid=(1,),
            in_specs=[
                whole(R, D),
                whole(1, D),
                whole(R, 128),
                whole(R, 128),
                whole(16, HALF, 128),
                whole(16, HALF + 16, 128),
            ],
            out_specs=[whole(QPAD, R), whole(R, 768)],
        ),
        out_shape=[
            jax.ShapeDtypeStruct((QPAD, R), bf16),
            jax.ShapeDtypeStruct((R, 768), bf16),
        ],
        compiler_params=pltpu.CompilerParams(vmem_limit_bytes=22 << 20),
        cost_estimate=pl.CostEstimate(flops=400_000_000, bytes_accessed=6_000_000, transcendentals=0),
    )(idx, u, gain, cos, sin, *front)


def heads_wide(ref, low):
    top = jnp.concatenate([ref[64 * h : 64 * h + 64, :] for h in range(GRP)], axis=1)
    zero = jnp.zeros_like(top)
    return jnp.concatenate([top, zero] if low else [zero, top], axis=0)


SMALL = 64
LANES = GRP * R


def chunk_of(kv_ref, need_ref, i):
    rows = [
        kv_ref[pl.ds(pl.multiple_of(need_ref[CHUNK // SMALL * i + k] * SMALL, SMALL), SMALL), :]
        for k in range(CHUNK // SMALL)
    ]
    return jnp.concatenate(rows, axis=0)


def chunk_rows(i):
    return pl.ds(pl.multiple_of(i * CHUNK, CHUNK), CHUNK)


def attend_kernel(need_ref, qt_ref, kv_ref, bias_ref, mixed_ref, lse_ref, s_ref, c_ref):
    q = heads_wide(qt_ref, True)
    count = need_ref[KEYS // SMALL]

    def score(pair, peak):
        for i in (2 * pair, 2 * pair + 1):
            kv = chunk_of(kv_ref, need_ref, i)
            c_ref[chunk_rows(i), :] = kv
            b = bias_ref[chunk_rows(i), :]
            s = mm(kv, q) + jnp.concatenate([b, b, b], axis=1)
            s_ref[chunk_rows(i), :] = s
            peak = jnp.maximum(peak, jnp.max(s, axis=0, keepdims=True))
        return peak

    peak = lax.fori_loop(0, count, score, jnp.full((1, LANES), masked_fill, f32))

    def mix(pair, state):
        total, acc = state
        for i in (2 * pair, 2 * pair + 1):
            p = jnp.exp(s_ref[chunk_rows(i), :] - peak)
            total = total + jnp.sum(p, axis=0, keepdims=True)
            acc = acc + mm(c_ref[chunk_rows(i), :].T, p.astype(bf16))
        return total, acc

    total, acc = lax.fori_loop(
        0, count, mix, (jnp.zeros((1, LANES), f32), jnp.zeros((128, LANES), f32))
    )
    lse_ref[0] = peak + jnp.log(total)
    o = (acc[64:] / total).astype(bf16)
    for h in range(GRP):
        mixed_ref[64 * h : 64 * h + 64, :] = o[:, 128 * h : 128 * h + 128]


def attend(need, qt, kv_all, bias):
    return pl.pallas_call(
        attend_kernel,
        name="attend",
        grid_spec=pltpu.PrefetchScalarGridSpec(
            num_scalar_prefetch=1,
            grid=(SIDE,),
            in_specs=[
                pl.BlockSpec((GRP * HD, R), lambda g, n: (g, 0)),
                pl.BlockSpec((KEYS, 128), lambda g, n: (0, g)),
                pl.BlockSpec((KEYS, R), lambda g, n: (0, 0)),
            ],
            out_specs=[
                pl.BlockSpec((GRP * HD, R), lambda g, n: (g, 0)),
                pl.BlockSpec((1, 1, LANES), lambda g, n: (g, 0, 0)),
            ],
            scratch_shapes=[pltpu.VMEM((KEYS, LANES), f32), pltpu.VMEM((KEYS, 128), bf16)],
        ),
        out_shape=[
            jax.ShapeDtypeStruct((QSIDE, R), bf16),
            jax.ShapeDtypeStruct((SIDE, 1, LANES), f32),
        ],
        compiler_params=pltpu.CompilerParams(vmem_limit_bytes=24 << 20),
        cost_estimate=pl.CostEstimate(
            flops=2_400_000_000, bytes_accessed=6_000_000, transcendentals=4_700_000
        ),
    )(need, qt, kv_all, bias)


def out_weight(refs, c):
    return jnp.concatenate(
        [ref[:, 160 * c : 160 * c + 160, :].reshape(320, 128) for ref in refs], axis=0
    )


def gu_weight(refs, c):
    gl, gh, ul, uh = refs
    gate = jnp.concatenate([gl[:, c].reshape(512, 128), gh[:, c].reshape(512, 128)], axis=0)
    up = jnp.concatenate([ul[:, c].reshape(512, 128), uh[:, c].reshape(512, 128)], axis=0)
    return jnp.concatenate([gate, up], axis=1)


def down_weight(ref, c):
    return ref[:, 160 * c : 160 * c + 160, :].reshape(640, 128)


WEIGHT_SPECS = (
    [pl.BlockSpec((2, ROWS, 128), lambda j, k=k: (5 + k, 0, 0)) for k in range(3)]
    + [
        pl.BlockSpec((16, 5, 32, 128), lambda j, d=d, o=o: (1 + d, o + j, 0, 0))
        for o in (0, 4)
        for d in (0, 1)
    ]
    + [pl.BlockSpec((4, ROWS, 128), lambda j: (12 + j, 0, 0))]
)


def weight_args(gathered):
    fine = gathered.reshape(SHARDS, 40, 32, 128)
    return [gathered] * 3 + [fine] * 4 + [gathered]


def feed_kernel(
    mixed_ref, u_ref, g_ref, pad_ref, o0, o1, o2, gl, gh, ul, uh, wd,
    y_ref, h_ref, nt_ref, gate_ref, up_ref, mt_ref, n_scr, y_scr,
):
    step = pl.program_id(0)

    @pl.when(step == 0)
    def _():
        mixed = mixed_ref[...].T
        for c in range(0, 8, 2):
            w = jnp.concatenate(
                [out_weight((o0, o1, o2), c), out_weight((o0, o1, o2), c + 1)], axis=1
            )
            y = mm(mixed, w)
            end = min(128 * c + 256, D)
            h_ref[:, 128 * c : end] = u_ref[:, 128 * c : end].astype(f32) + y[:, : end - 128 * c]
        _, n = normed_of(h_ref[...], g_ref[...])
        padded = mm(n, pad_ref[...])
        n_scr[...] = padded.astype(bf16)
        nt_ref[...] = padded.T.astype(bf16)
        y_scr[...] = jnp.zeros_like(y_scr)

    n = n_scr[...]
    inner = []
    for c in range(5):
        gu = mm(n, gu_weight((gl, gh, ul, uh), c))
        gate, up = gu[:, :128], gu[:, 128:]
        cols = slice(128 * c, 128 * c + 128)
        gate_ref[:, cols] = gate
        up_ref[:, cols] = up
        m = gate * jax.nn.sigmoid(gate) * up
        mt_ref[cols, :] = m.T.astype(bf16)
        inner.append(m.astype(bf16))
    inner = jnp.concatenate(inner, axis=1)
    for c in range(0, 8, 2):
        w = jnp.concatenate([down_weight(wd, c), down_weight(wd, c + 1)], axis=1)
        y_scr[:, 128 * c : 128 * c + 256] += mm(inner, w)

    @pl.when(step == 3)
    def _():
        y_ref[...] = (h_ref[...] + y_scr[:, :D]).astype(bf16)


def feed(mixed, u, gain, pad, gathered):
    whole = lambda *shape: pl.BlockSpec(shape, lambda j: (0,) * len(shape))
    return pl.pallas_call(
        feed_kernel,
        name="feed",
        grid=(4,),
        in_specs=[whole(D, R), whole(R, D), whole(1, D), whole(D, PADD)] + WEIGHT_SPECS,
        out_specs=[
            whole(R, D),
            whole(R, D),
            whole(PADD, R),
            pl.BlockSpec((R, 640), lambda j: (0, j)),
            pl.BlockSpec((R, 640), lambda j: (0, j)),
            pl.BlockSpec((640, R), lambda j: (j, 0)),
        ],
        out_shape=[
            jax.ShapeDtypeStruct((R, D), bf16),
            jax.ShapeDtypeStruct((R, D), f32),
            jax.ShapeDtypeStruct((PADD, R), bf16),
            jax.ShapeDtypeStruct((R, FF), f32),
            jax.ShapeDtypeStruct((R, FF), f32),
            jax.ShapeDtypeStruct((FF, R), bf16),
        ],
        scratch_shapes=[pltpu.VMEM((R, PADD), bf16), pltpu.VMEM((R, PADD), f32)],
        compiler_params=pltpu.CompilerParams(vmem_limit_bytes=30 << 20),
        cost_estimate=pl.CostEstimate(
            flops=2_200_000_000, bytes_accessed=22_000_000, transcendentals=400_000
        ),
    )(mixed, u, gain, pad, *weight_args(gathered))


def norm_back(d_out, values, gain):
    scales = lax.rsqrt(jnp.mean(values * values, axis=-1, keepdims=True) + eps)
    scaled = d_out * gain
    d_gain = jnp.sum(d_out * values * scales, axis=0, keepdims=True)
    d_values = scales * scaled - values * (scales * scales * scales) * jnp.mean(
        scaled * values, axis=-1, keepdims=True
    )
    return d_values, d_gain


def feed_back_kernel(
    c_ref, gate_ref, up_ref, h_ref, g_ref, pad_ref, o0, o1, o2, gl, gh, ul, uh, wd,
    dgate_ref, dup_ref, dh_ref, dhb_ref, dg_ref, dot_ref, cb_ref, dn_scr,
):
    step = pl.program_id(0)

    @pl.when(step == 0)
    def _():
        cb_ref[...] = jnp.zeros_like(cb_ref)
        cb_ref[:, :D] = c_ref[...].astype(bf16)
        dn_scr[...] = jnp.zeros_like(dn_scr)

    d_inner = jnp.zeros((R, 640), f32)
    for c in range(0, 8, 2):
        w = jnp.concatenate([down_weight(wd, c), down_weight(wd, c + 1)], axis=1)
        d_inner = d_inner + mm_nt(cb_ref[:, 128 * c : 128 * c + 256], w)
    for c in range(5):
        cols = slice(128 * c, 128 * c + 128)
        gate, up, dm = gate_ref[:, cols], up_ref[:, cols], d_inner[:, cols]
        sigma = jax.nn.sigmoid(gate)
        d_gate = (dm * up * sigma * (1.0 + gate * (1.0 - sigma))).astype(bf16)
        d_up = (dm * gate * sigma).astype(bf16)
        dgate_ref[:, cols] = d_gate
        dup_ref[:, cols] = d_up
        both = jnp.concatenate([d_gate, d_up], axis=1)
        dn_scr[...] += mm_nt(both, gu_weight((gl, gh, ul, uh), c))

    @pl.when(step == 3)
    def _():
        padded = dn_scr[...]
        high = padded.astype(bf16)
        low = (padded - high.astype(f32)).astype(bf16)
        dn = mm_nt(high, pad_ref[...]) + mm_nt(low, pad_ref[...])
        d_h, d_gain = norm_back(dn, h_ref[...], g_ref[...])
        d_h = c_ref[...] + d_h
        dg_ref[...] = d_gain
        dh_ref[...] = d_h
        dhb_ref[...] = jnp.zeros_like(dhb_ref)
        dhb_ref[:, :D] = d_h.astype(bf16)
        d_mixed = jnp.zeros((R, D), f32)
        for c in range(0, 8, 2):
            w = jnp.concatenate(
                [out_weight((o0, o1, o2), c), out_weight((o0, o1, o2), c + 1)], axis=1
            )
            d_mixed = d_mixed + mm_nt(dhb_ref[:, 128 * c : 128 * c + 256], w)
        dot_ref[:D, :] = d_mixed.T
        dot_ref[D:, :] = jnp.zeros((QPAD - D, R), f32)


def feed_back(cot, gate, up, hidden, gain, pad, gathered):
    whole = lambda *shape: pl.BlockSpec(shape, lambda j: (0,) * len(shape))
    block = pl.BlockSpec((R, 640), lambda j: (0, j))
    return pl.pallas_call(
        feed_back_kernel,
        name="feed_back",
        grid=(4,),
        in_specs=[whole(R, D), block, block, whole(R, D), whole(1, D), whole(D, PADD)]
        + WEIGHT_SPECS,
        out_specs=[
            block,
            block,
            whole(R, D),
            whole(R, PADD),
            whole(1, D),
            whole(QPAD, R),
            whole(R, PADD),
        ],
        out_shape=[
            jax.ShapeDtypeStruct((R, FF), bf16),
            jax.ShapeDtypeStruct((R, FF), bf16),
            jax.ShapeDtypeStruct((R, D), f32),
            jax.ShapeDtypeStruct((R, PADD), bf16),
            jax.ShapeDtypeStruct((1, D), f32),
            jax.ShapeDtypeStruct((QPAD, R), f32),
            jax.ShapeDtypeStruct((R, PADD), bf16),
        ],
        scratch_shapes=[pltpu.VMEM((R, PADD), f32)],
        compiler_params=pltpu.CompilerParams(vmem_limit_bytes=30 << 20),
        cost_estimate=pl.CostEstimate(
            flops=2_200_000_000, bytes_accessed=22_000_000, transcendentals=400_000
        ),
    )(cot, gate, up, hidden, gain, pad, *weight_args(gathered))


def attend_back_kernel(
    need_ref, qt_ref, kv_ref, bias_ref, dot_ref, mixed_ref, lse_ref, dkv_ref, dqt_ref
):
    q = heads_wide(qt_ref, True)
    d_o = heads_wide(dot_ref, False)
    o = heads_wide(mixed_ref, False)
    delta = jnp.sum(d_o * o.astype(f32), axis=0, keepdims=True)
    d_o = d_o.astype(bf16)
    lse = lse_ref[0]
    both = jnp.concatenate([q, d_o], axis=1)
    dkv_ref[...] = jnp.zeros_like(dkv_ref)

    def fold(i, acc):
        kv = chunk_of(kv_ref, need_ref, i)
        b = bias_ref[chunk_rows(i), :]
        p = jnp.exp(mm(kv, q) + jnp.concatenate([b, b, b], axis=1) - lse)
        ds = (p * (mm(kv, d_o) - delta)).astype(bf16)
        part = mm_nt(jnp.concatenate([ds, p.astype(bf16)], axis=1), both).astype(bf16)
        for k in range(CHUNK // SMALL):
            at = pl.multiple_of(need_ref[CHUNK // SMALL * i + k] * SMALL, SMALL)
            dkv_ref[pl.ds(at, SMALL), :] = part[SMALL * k : SMALL * k + SMALL]
        return acc + mm(kv.T, ds)

    acc = lax.fori_loop(0, need_ref[KEYS // SMALL + 1], fold, jnp.zeros((128, LANES), f32))
    acc = acc[:64] * 0.125
    for h in range(GRP):
        dqt_ref[64 * h : 64 * h + 64, :] = acc[:, 128 * h : 128 * h + 128]


def attend_back(need, qt, kv_all, bias, d_mixed, mixed, lse):
    heads = pl.BlockSpec((GRP * HD, R), lambda g, n: (g, 0))
    return pl.pallas_call(
        attend_back_kernel,
        name="attend_back",
        grid_spec=pltpu.PrefetchScalarGridSpec(
            num_scalar_prefetch=1,
            grid=(SIDE,),
            in_specs=[
                heads,
                pl.BlockSpec((KEYS, 128), lambda g, n: (0, g)),
                pl.BlockSpec((KEYS, R), lambda g, n: (0, 0)),
                heads,
                heads,
                pl.BlockSpec((1, 1, LANES), lambda g, n: (g, 0, 0)),
            ],
            out_specs=[pl.BlockSpec((KEYS, 128), lambda g, n: (0, g)), heads],
        ),
        out_shape=[
            jax.ShapeDtypeStruct((KEYS, SIDE * 128), bf16),
            jax.ShapeDtypeStruct((QSIDE, R), f32),
        ],
        compiler_params=pltpu.CompilerParams(vmem_limit_bytes=24 << 20),
        cost_estimate=pl.CostEstimate(
            flops=6_000_000_000, bytes_accessed=10_000_000, transcendentals=4_700_000
        ),
    )(need, qt, kv_all, bias, d_mixed, mixed, lse)


def project_back_kernel(
    idx_ref, dqt_ref, dkv_ref, cos_ref, sin_ref, u_ref, g_ref, dh_ref, wa_ref, wb_ref,
    du_ref, dqkv_ref, at_ref, dg_ref,
):
    cos, sin = cos_ref[...], sin_ref[...]
    lane = lane_of((R, 128))
    dkv = [dkv_ref[:, 128 * g : 128 * g + 128] for g in range(KVH)]
    rolled = [pltpu.roll(b, 64, 1) for b in dkv]
    zero = jnp.zeros((R, 128), f32)
    blocks = [dqt_ref[128 * c : 128 * c + 128, :].T for c in range(7)]
    last = jnp.concatenate([dqt_ref[896:960, :], jnp.zeros((64, R), f32)], axis=0).T
    low = lane < 64
    blocks.append(jnp.where(low, last, rolled[0]))
    blocks.append(jnp.where(low, dkv[1], rolled[2]))
    blocks.append(jnp.where(low, dkv[3], rolled[4]))
    blocks = [b * cos - half_swapped(b) * sin for b in blocks]
    blocks.append(jnp.where(low, rolled[0], dkv[1]))
    blocks.append(jnp.where(low, rolled[2], dkv[3]))
    blocks.append(jnp.where(low, rolled[4], zero))
    da = jnp.zeros((R, D), f32)
    for c in range(0, 13, 2):
        d, w = blocks[c].astype(bf16), front_weight(idx_ref, wa_ref, wb_ref, c)
        if c + 1 < 13:
            d = jnp.concatenate([d, blocks[c + 1].astype(bf16)], axis=1)
            w = jnp.concatenate([w, front_weight(idx_ref, wa_ref, wb_ref, c + 1)], axis=1)
        dqkv_ref[:, 128 * c : 128 * c + d.shape[1]] = d
        da = da + mm_nt(d, w)
    u = u_ref[...].astype(f32)
    gain = g_ref[...]
    _, a = normed_of(u, gain)
    at_ref[...] = a.T
    d_u, d_gain = norm_back(da, u, gain)
    dg_ref[...] = d_gain
    du_ref[...] = dh_ref[...] + d_u


def project_back(d_query, d_kv, cos, sin, u, gain, d_hidden, idx, front):
    whole = lambda *shape: pl.BlockSpec(shape, lambda j, idx: (0,) * len(shape))
    return pl.pallas_call(
        project_back_kernel,
        name="project_back",
        grid_spec=pltpu.PrefetchScalarGridSpec(
            num_scalar_prefetch=1,
            grid=(1,),
            in_specs=[
                whole(D, R),
                whole(R, 640),
                whole(R, 128),
                whole(R, 128),
                whole(R, D),
                whole(1, D),
                whole(R, D),
                whole(16, HALF, 128),
                whole(16, HALF + 16, 128),
            ],
            out_specs=[whole(R, D), whole(R, 13 * 128), whole(D, R), whole(1, D)],
        ),
        out_shape=[
            jax.ShapeDtypeStruct((R, D), f32),
            jax.ShapeDtypeStruct((R, 13 * 128), bf16),
            jax.ShapeDtypeStruct((D, R), bf16),
            jax.ShapeDtypeStruct((1, D), f32),
        ],
        compiler_params=pltpu.CompilerParams(vmem_limit_bytes=24 << 20),
        cost_estimate=pl.CostEstimate(flops=400_000_000, bytes_accessed=7_000_000, transcendentals=0),
    )(idx, d_query, d_kv, cos, sin, u, gain, d_hidden, *front)


def outer_kernel(
    slot_ref, at_ref, dqkv_ref, mixed_ref, dhb_ref, nt_ref, dgate_ref, dup_ref, mt_ref, cb_ref,
    gain_ref, k0, k1, k2, s0, s1, s2, stage, sems,
):
    step = pl.program_id(0)
    buf = step % 2
    slot_y, slot_x = slot_ref[step // 4], slot_ref[4 + step % 4]
    zslot = [slot_ref[8 + k] for k in range(4)]
    out_ref = stage.at[buf]
    (a0, b0), (a1, b1), (a2, b2) = PART_ROWS

    def copy(i, buf, half=0):
        src = stage.at[buf]
        if i == 0:
            src, dst = src.at[:, a0:b0], (k0, s0)[half].at[slot_y % 2, slot_x]
        elif i == 1:
            src, dst = src.at[:, a1:b1], (k1, s1)[half].at[slot_x % 2, :, slot_y]
        elif i == 2:
            src, dst = src.at[0:2, a2:b2], k2.at[:, slot_y, slot_x]
        else:
            src, dst = src.at[2:4, a2:b2], s2.at[:, slot_y, slot_x]
        return pltpu.make_async_copy(src, dst, sems.at[buf, i])

    @pl.when(step >= 2)
    def _():
        for i in range(4):
            copy(i, buf).wait()

    def row_of(k, count, at):
        row = lax.broadcasted_iota(jnp.int32, (count, 128), 0)
        return jnp.where(row == at, gain_ref[pl.ds(4 * step + k, 1), :], 0.0)

    def narrow(start, ks):
        count = len(ks)
        rows = at_ref[pl.ds(pl.multiple_of(start, 32), 96 * count), :]
        for c in range(0, 13, 2):
            width = min(256, 1664 - 128 * c)
            res = mm(rows, dqkv_ref[:, 128 * c : 128 * c + width])
            for i, k in enumerate(ks):
                for h in range(width // 128):
                    out_ref[zslot[k], 96 * (c + h) : 96 * (c + h) + 96, :] = res[
                        96 * i : 96 * i + 96, 128 * h : 128 * h + 128
                    ].astype(bf16)
        for k in ks:
            out_ref[zslot[k], 1248:1280, :] = row_of(k, 32, 0).astype(bf16)

    def wide(ref, start, cot_ref, ks):
        rows = ref[pl.ds(pl.multiple_of(start, 32), 160 * len(ks)), :]
        for c in range(0, 8, 2):
            res = mm(rows, cot_ref[:, 128 * c : 128 * c + 256])
            for i, k in enumerate(ks):
                for h in range(2):
                    b = res[160 * i : 160 * i + 160, 128 * h : 128 * h + 128]
                    if c + h == 7:
                        b = b + row_of(k, 160, 0)
                    at = 160 * (c + h)
                    out_ref[zslot[k], at : at + 160, :] = b.astype(bf16)

    @pl.when(step < 2)
    def _():
        narrow(384 * step, (0, 1, 2, 3))

    @pl.when(step == 2)
    def _():
        narrow(768, (0, 1))
        wide(mixed_ref, 0, dhb_ref, (2, 3))

    @pl.when(step == 3)
    def _():
        wide(mixed_ref, 320, dhb_ref, (0, 1, 2, 3))

    @pl.when((step >= 4) & (step < 12))
    def _():
        rows = nt_ref[pl.ds(pl.multiple_of(128 * (step - 4), 128), 128), :]
        for part, ref in enumerate((dgate_ref, dup_ref)):
            for c in range(0, 20, 2):
                res = mm(rows, ref[:, 128 * c : 128 * c + 256])
                for k in range(4):
                    for h in range(2):
                        b = res[32 * k : 32 * k + 32, 128 * h : 128 * h + 128]
                        at = 32 * (20 * part + c + h)
                        if at == 0:
                            b = b + row_of(k, 32, 30)
                        out_ref[zslot[k], at : at + 32, :] = b.astype(bf16)

    @pl.when(step >= 12)
    def _():
        wide(mt_ref, 640 * (step - 12), cb_ref, (0, 1, 2, 3))

    for half in range(2):

        @pl.when(slot_y // 2 == half)
        def _(half=half):
            copy(0, buf, half).start()

        @pl.when(slot_x // 2 == half)
        def _(half=half):
            copy(1, buf, half).start()

    copy(2, buf).start()
    copy(3, buf).start()

    @pl.when(step == 15)
    def _():
        for last in (0, 1):
            for i in range(4):
                copy(i, last).wait()


def outer(slots, at, dqkv, mixed, dhb, nt, dgate, dup, mt, cb, gains):
    whole = lambda v: pl.BlockSpec(v.shape, lambda s, slot: (0,) * v.ndim)
    args = (at, dqkv, mixed, dhb, nt, dgate, dup, mt, cb, gains)
    shapes = [
        jax.ShapeDtypeStruct((2, 4, 4, end - begin, 128), bf16) for begin, end in PART_ROWS
    ]
    out = pl.pallas_call(
        outer_kernel,
        name="outer",
        grid_spec=pltpu.PrefetchScalarGridSpec(
            num_scalar_prefetch=1,
            grid=(16,),
            in_specs=[whole(v) for v in args],
            out_specs=[pl.BlockSpec(memory_space=pl.ANY)] * 6,
            scratch_shapes=[
                pltpu.VMEM((2, 4, ROWS, 128), bf16),
                pltpu.SemaphoreType.DMA((2, 4)),
            ],
        ),
        out_shape=shapes * 2,
        compiler_params=pltpu.CompilerParams(vmem_limit_bytes=20 << 20),
        cost_estimate=pl.CostEstimate(
            flops=2_600_000_000, bytes_accessed=24_000_000, transcendentals=0
        ),
    )(slots, *args)
    return out[:3], out[3:]


def shard_kind(rank):
    return jnp.where(rank < 10, 0, jnp.where((rank >= 16) & (rank < 48), 2, 1))


def shard_blocks(flat, rank):
    def narrow(_):
        w = jnp.pad(flat.reshape(96, 1600), ((0, 0), (0, 64)))
        w = w.reshape(96, 13, 128).transpose(1, 0, 2).reshape(1248, 128)
        return jnp.pad(w, ((0, 32), (0, 0)))

    def square(_):
        w = jnp.pad(flat.reshape(160, 960), ((0, 0), (0, 64)))
        return w.reshape(160, 8, 128).transpose(1, 0, 2).reshape(ROWS, 128)

    def broad(_):
        w = jnp.pad(flat.reshape(30, 40, 128), ((0, 2), (0, 0), (0, 0)))
        return w.transpose(1, 0, 2).reshape(ROWS, 128)

    return lax.switch(shard_kind(rank), [narrow, square, broad], 0)


def blocks_shard(blocks, rank):
    def narrow(_):
        w = blocks[:1248].reshape(13, 96, 128).transpose(1, 0, 2).reshape(96, 1664)[:, :1600]
        return w.reshape(SHARD), blocks[1248, :30]

    def square(_):
        w = blocks.reshape(8, 160, 128).transpose(1, 0, 2).reshape(160, 1024)[:, :960]
        return w.reshape(SHARD), blocks[1120, 64:94]

    def broad(_):
        w = blocks.reshape(40, 32, 128).transpose(1, 0, 2)[:30]
        return w.reshape(SHARD), blocks[30, :30]

    return lax.switch(shard_kind(rank), [narrow, square, broad], 0)


def gain_rows(one, two):
    gains = jnp.concatenate([one, two], axis=1).reshape(SHARDS, 30)
    shards = jnp.arange(SHARDS, dtype=jnp.int32)
    square = (((shards >= 10) & (shards < 16)) | (shards >= 48))[:, None]
    return jnp.where(
        square, jnp.pad(gains, ((0, 0), (64, 34))), jnp.pad(gains, ((0, 0), (0, 98)))
    )


def per_device(layer_in, out_grad, segment_ids, block_pair, params, norm_gains):
    phase = lax.axis_index("phase")
    ctx = lax.axis_index("ctx")
    rank = ctx * 2 + lax.axis_index("fsdp")
    y, x, z = rank // 16, (rank // 4) % 4, rank % 4
    zh = z // 2

    own = shard_blocks(params[0], rank)
    front, own = gather_front(own, norm_gains[0], y, phase)
    gathered = lax.all_gather(own, ("ctx", "fsdp"), axis=0)

    seg_row = segment_ids[0]
    pair = lax.dynamic_index_in_dim(block_pair, ctx, 0, keepdims=False)
    within = jnp.arange(HD, dtype=jnp.int32)
    place_q = jnp.concatenate([pair * 64 + within, (63 - pair) * 64 + within])
    seg_q = jnp.concatenate(
        [
            lax.dynamic_slice_in_dim(seg_row, pair * 64, 64),
            lax.dynamic_slice_in_dim(seg_row, (63 - pair) * 64, 64),
        ]
    )
    start_q = jnp.sum((seg_row[:, None] < seg_q[None, :]).astype(jnp.int32), axis=0)
    pairs_k = block_pair[key_order(y, x, zh, phase)]
    spot_k = jnp.stack([pairs_k, 63 - pairs_k], axis=1).reshape(64)
    seen_by = lambda at, spot: (spot_k <= spot) & (spot_k * 64 + 63 >= start_q[at])
    seen = seen_by(0, pair) | seen_by(64, 63 - pair)
    seen_count = jnp.sum(seen.astype(jnp.int32))
    before = jnp.arange(64)[:, None] > jnp.arange(64)[None, :]
    rank_seen = jnp.sum((before & seen[None, :]).astype(jnp.int32), axis=1)
    rank_k = jnp.where(seen, rank_seen, seen_count + jnp.arange(64) - rank_seen)
    chosen = rank_k[None, :] == jnp.arange(64)[:, None]
    order_k = jnp.sum(jnp.where(chosen, jnp.arange(64)[None, :], 0), axis=1)
    spot_k = jnp.sum(jnp.where(chosen & seen[None, :], spot_k[None, :], 0), axis=1)
    spot_k = jnp.where(jnp.arange(64) < seen_count, spot_k, 1 << 16)
    turns = jnp.stack([(seen_count + 15) // 16, (seen_count + 7) // 8])
    need = jnp.concatenate([order_k, turns]).astype(jnp.int32)
    place_k = (spot_k[:, None] * 64 + within[None, :]).reshape(KEYS)
    bias = jnp.where(
        (place_k[:, None] <= place_q[None, :]) & (place_k[:, None] >= start_q[None, :]),
        0.0,
        masked_fill,
    ).astype(f32)
    frequency = rope_theta ** (-2.0 * jnp.arange(HD // 2, dtype=f32) / HD)
    angles = (place_q - start_q).astype(f32)[:, None] * frequency[None, :]
    cosine, sine = jnp.cos(angles), jnp.sin(angles)
    cos = jnp.concatenate([cosine] * 4, axis=1)
    sin = jnp.concatenate([-sine, sine, -sine, sine], axis=1)
    spread = jnp.arange(PADD, dtype=jnp.int32)
    target = jnp.where(spread % 32 < 30, (spread // 32) * 30 + spread % 32, -1)
    pad = (jnp.arange(D, dtype=jnp.int32)[:, None] == target[None, :]).astype(bf16)

    four = jnp.arange(4, dtype=jnp.int32)
    slots_y, slots_x, slots_z = (slot_of(four ^ at_axis, phase) for at_axis in (y, x, z))
    idx = jnp.concatenate(
        [
            (slots_x[:, None] + 4 * slots_z[None, :]).reshape(16),
            (4 * slots_x[:, None] + slots_z[None, :]).reshape(16),
        ]
    )
    slots = jnp.concatenate([slots_y, slots_x, slots_z])
    gains = front[1][:, HALF : HALF + 4, :30][idx[16:]].astype(f32)
    gains = gains.transpose(1, 0, 2).reshape(1, 2 * D)
    gain_one, gain_two = gains[:, :D], gains[:, D:]
    first = phase == 0

    u = layer_in[0]
    mixed = None
    kept = []
    for tick in range(2):
        active = phase == tick
        qt, kv = project(u, gain_one, cos, sin, idx, front)
        kv_side = jnp.where(active, kv[:, :384], over(kv[:, 384:], tick))
        qt_side = jnp.where(active, qt[:QSIDE], over(qt[QSIDE:], tick))
        kv_all = gather_keys(kv_side)
        mixed_side, lse = attend(need, qt_side, kv_all, bias)
        kept.append((qt_side, kv_all, mixed_side, lse))
        far = over(mixed_side[: D - QSIDE], 1 - tick)
        whole = jnp.concatenate([mixed_side, far])
        mixed = whole if tick == 0 else jnp.where(active, whole, mixed)
        result, hidden, nt, gate, up, mt = feed(mixed, u, gain_two, pad, gathered)
        if tick == 0:
            u = jnp.where(first, u, over(result, 0))

    cot = out_grad[0]
    d_query = d_kv = None
    for tick in range(2):
        layer = 1 - tick
        active = phase == layer
        qt_side, kv_all, mixed_side, lse = kept[layer]
        dgate, dup, dh, dhb, dg_two, d_mixed, cb = feed_back(
            cot, gate, up, hidden, gain_two, pad, gathered
        )
        d_side = jnp.where(active, d_mixed[:QSIDE], over(d_mixed[QSIDE:], layer))
        d_kv_all, dq_side = attend_back(need, qt_side, kv_all, bias, d_side, mixed_side, lse)
        dq_new = jnp.concatenate([dq_side, over(dq_side[: D - QSIDE], tick)])
        dkv_side = scatter_keys(d_kv_all)
        dkv_new = jnp.concatenate([dkv_side, over(dkv_side[:, :256], tick)], axis=1)
        d_query = dq_new if tick == 0 else jnp.where(active, dq_new, d_query)
        d_kv = dkv_new if tick == 0 else jnp.where(active, dkv_new, d_kv)
        d_u, dqkv, at, dg_one = project_back(
            d_query, d_kv, cos, sin, u, gain_one, dh, idx, front
        )
        if tick == 0:
            cot = jnp.where(first, over(d_u.astype(bf16), 1).astype(f32), cot)

    keep, send = outer(
        slots, at, dqkv, mixed, dhb, nt, dgate, dup, mt, cb, gain_rows(dg_one, dg_two)
    )
    total = scatter_grads(keep, send)
    param_part, gain_part = blocks_shard(total, rank)
    return (result[None, None], d_u[None, None], param_part[None], gain_part[None])


def solution(mesh):
    return jax.shard_map(
        per_device,
        mesh=mesh,
        in_specs=(
            P("fsdp", "ctx", None),
            P("fsdp", "ctx", None),
            P("fsdp", None),
            P(),
            P("phase", ("ctx", "fsdp")),
            P("phase", ("ctx", "fsdp")),
        ),
        out_specs=(
            P("phase", "fsdp", "ctx", None),
            P("phase", "fsdp", "ctx", None),
            P("phase", ("ctx", "fsdp")),
            P("phase", ("ctx", "fsdp")),
        ),
        check_vma=False,
    )
```
